128 devices in a mesh: gx: 16 (over y, z_lo, core), gy: 8 (over x, z_hi).
Axes of the slice: x: 4, y: 4, z: 4 (z_hi: 2, z_lo: 2; z = z_hi * 2 + z_lo), core: 2. Of those that a mesh axis runs over, the one named last changes fastest.
Arguments:
- fields: float32 [5, 24, 1024, 1024], P(None, None, 'gx', 'gy'), may hold values from -60 to 60
- embed_weight: bfloat16 [2560, 768], replicated, may hold values from -0.125 to 0.125
- qkv_weight: bfloat16 [768, 2304], replicated, may hold values from -0.21875 to 0.21875
- out_weight: bfloat16 [768, 768], replicated, may hold values from -0.21875 to 0.21875
- up_weight: bfloat16 [768, 3072], replicated, may hold values from -0.21875 to 0.21875
- down_weight: bfloat16 [3072, 768], replicated, may hold values from -0.109375 to 0.109375
Outputs:
- tokens_out: bfloat16 [2, 128, 128, 768], P(None, 'gy', 'gx')
The draws below stay inside these ranges and needn't reach their ends.
All inputs are finite; a program needn't handle non-finite values.
Results may differ from the reference program's by a relative error of at most 0.029.
Values may be sent and summed in bfloat16 or wider, within the bound.
No kernel may reach another device: no remote copies, remote signals or barrier semaphores. Data moves between devices by JAX's collectives and lax.ppermute only.
A program may use at most 128 MiB of HBM per device.

```python
import math
import jax
import jax.numpy as jnp
from jax import lax

NF = 5
R = 4
P_SIZE = 8
ZP = 2
D = 768
HEADS = 12
FF = 3072
ZS = 16
ZT = 24
KIN = 2560
NX = 1024
NY = 1024


def wave_table(key, count, length, period, fast_lo, fast_hi, slow_lo, slow_hi, slow_mask):
    key_fast, key_slow, key_phase = jax.random.split(key, 3)
    fast = jax.random.randint(key_fast, (count, NF), fast_lo, fast_hi)
    slow = jax.random.randint(key_slow, (count, NF), slow_lo, slow_hi)
    number = jnp.where(slow_mask, slow, fast).astype(jnp.int32)
    phase = jax.random.uniform(key_phase, (count, NF), jnp.float32, 0.0, 2.0 * math.pi)
    cells = jnp.arange(length).astype(jnp.int32)
    turns = number[:, :, None] * cells[None, None, :] % period
    angle = turns.astype(jnp.float32) * (2.0 * math.pi / period) + phase[:, :, None]
    return jnp.cos(angle)


def draw_fields(key, part):
    key = jax.random.fold_in(key, 11)
    count = 3
    amp_lo = 9.0
    amp_hi = 18.0
    keys = jax.random.split(key, 6)
    slow_axis = jax.random.randint(keys[0], (count, NF), 0, 3)
    waves_x = wave_table(keys[1], count, NX, NX, (235 * NX + 999) // 1000, 265 * NX // 1000 + 1, (120 * NX + 999) // 1000, 150 * NX // 1000 + 1, slow_axis == 0)
    waves_y = wave_table(keys[2], count, NY, NY, (235 * NY + 999) // 1000, 265 * NY // 1000 + 1, (120 * NY + 999) // 1000, 150 * NY // 1000 + 1, slow_axis == 1)
    waves_z = wave_table(keys[3], count, ZT, 64, 15, 18, 8, 10, slow_axis == 2)
    amplitude = jax.random.uniform(keys[4], (count, NF), jnp.float32, amp_lo, amp_hi)
    total = jnp.clip(0.02 * jax.random.normal(keys[5], (NF, ZT, NX, NY), jnp.float32), -0.1, 0.1)
    for term in range(count):
        plane = waves_x[term][:, :, None] * waves_y[term][:, None, :]
        column = amplitude[term][:, None] * waves_z[term]
        total = total + column[:, :, None, None] * plane[:, None, :, :]
    return total.astype(jnp.float32)


def bell_draw(key, extent, scale, most, kind=jnp.bfloat16):
    drawn = jax.random.normal(key, extent, jnp.float32) * scale
    return jnp.minimum(jnp.maximum(drawn, -most), most).astype(kind)


def setup_inputs(seed: int = 0) -> dict:
    seeds = jax.random.split(jax.random.key(seed), 7)
    return {
        "fields": draw_fields(jax.random.fold_in(seeds[6], 71), 0),
        "embed_weight": bell_draw(seeds[1], (KIN, D), KIN ** -0.5, 0.125),
        "qkv_weight": bell_draw(seeds[2], (D, 3 * D), D ** -0.5, 0.21875),
        "out_weight": bell_draw(seeds[3], (D, D), D ** -0.5, 0.21875),
        "up_weight": bell_draw(seeds[4], (D, FF), D ** -0.5, 0.21875),
        "down_weight": bell_draw(seeds[5], (FF, D), FF ** -0.5, 0.109375),
    }


def filter_taps():
    offsets = jnp.arange(-R, R + 1).astype(jnp.float32)
    values = jnp.exp(-offsets * offsets / 4.5)
    return values / jnp.sum(values)

def layer_norm(hidden):
    center = hidden - lax.optimization_barrier(jnp.mean(hidden, axis=-1, keepdims=True))
    spread = lax.optimization_barrier(jnp.mean(center * center, axis=-1, keepdims=True))
    return (center * lax.rsqrt(spread + 1e-05)).astype(jnp.bfloat16)

def line_attention(normed, qkv_weight, out_weight):
    zdim, lines, length, width = normed.shape
    both = jnp.dot(normed.reshape(-1, width), qkv_weight, preferred_element_type=jnp.float32)
    both = both.astype(jnp.bfloat16).reshape(zdim, lines, length, 3, HEADS, width // HEADS)
    query = both[:, :, :, 0].astype(jnp.float32)
    keys = both[:, :, :, 1].astype(jnp.float32)
    values = both[:, :, :, 2].astype(jnp.float32)
    scores = jnp.einsum('zlshe,zlthe->zlhst', query, keys) * (1.0 / (width // HEADS) ** 0.5)
    weights = jnp.exp(scores)
    weights = (weights / lax.optimization_barrier(jnp.sum(weights, axis=-1, keepdims=True))).astype(jnp.bfloat16)
    mixed = jnp.einsum('zlhst,zlthe->zlshe', weights.astype(jnp.float32), values).astype(jnp.bfloat16)
    mixed = mixed.reshape(-1, width)
    branch = jnp.dot(mixed, out_weight, preferred_element_type=jnp.float32).astype(jnp.bfloat16)
    return branch.reshape(zdim, lines, length, width)

def reference(fields, embed_weight, qkv_weight, out_weight, up_weight, down_weight):
    taps = filter_taps()
    along_x = jnp.zeros_like(fields)
    for index in range(2 * R + 1):
        along_x = along_x + taps[index] * jnp.roll(fields, -(index - R), axis=2)
    along_y = jnp.zeros_like(fields)
    for index in range(2 * R + 1):
        along_y = along_y + taps[index] * jnp.roll(along_x, -(index - R), axis=3)
    span = ZS
    smooth = jnp.zeros((NF, span, NX, NY), jnp.float32)
    for index in range(2 * R + 1):
        smooth = smooth + taps[index] * along_y[:, index:index + span]
    filtered = smooth.astype(jnp.bfloat16)
    split = filtered.reshape(NF, ZP, P_SIZE, NX // P_SIZE, P_SIZE, NY // P_SIZE, P_SIZE)
    patches = jnp.transpose(split, (1, 5, 3, 0, 2, 4, 6)).reshape(-1, KIN)
    hidden = jnp.dot(patches, embed_weight, preferred_element_type=jnp.float32)
    hidden = hidden.reshape(ZP, NY // P_SIZE, NX // P_SIZE, D)
    hidden = hidden + line_attention(layer_norm(hidden), qkv_weight, out_weight).astype(jnp.float32)
    turned = jnp.swapaxes(hidden, 1, 2)
    turned = turned + line_attention(layer_norm(turned), qkv_weight, out_weight).astype(jnp.float32)
    hidden = jnp.swapaxes(turned, 1, 2)
    normed = layer_norm(hidden).reshape(-1, D)
    upper = jnp.dot(normed, up_weight, preferred_element_type=jnp.float32)
    upper = jax.nn.gelu(upper, approximate=True).astype(jnp.bfloat16)
    lower = jnp.dot(upper, down_weight, preferred_element_type=jnp.float32).reshape(hidden.shape)
    return (hidden + lower).astype(jnp.bfloat16)
```

```python
import functools

import jax
import jax.numpy as jnp
import ml_dtypes
import numpy as np
from jax import lax
from jax.experimental import pallas as pl
from jax.experimental.pallas import tpu as pltpu
from jax.sharding import PartitionSpec as P

R = 4
NF = 5
ZS = 16
CX = 64
CY = 128
D = 768
FF = 3072
KIN = 2560
PAIRS = 6
NXL = 16
TOK = 256
EXT = 10
SLOTS = 32
BOUND = (0, 1, 8, 9)
HI_ROWS = EXT * 32
ALL_ROWS = HI_ROWS + 128
PADX = 16
bf16 = jnp.bfloat16
f32 = jnp.float32


def np_taps():
    offsets = np.arange(-R, R + 1).astype(np.float32)
    values = np.exp(-offsets * offsets / np.float32(4.5)).astype(np.float32)
    return (values / values.sum(dtype=np.float32)).astype(np.float32)


TAPS = np_taps()


def as_bf16(values):
    return np.asarray(values, np.float32).astype(ml_dtypes.bfloat16)


def split_np(values):
    high = as_bf16(values)
    low = as_bf16(values - high.astype(np.float32))
    return high, low


def band_tables():
    wide = np.zeros((CY + 2 * R, CY), np.float32)
    for out in range(CY):
        column = (out % 8) * 16 + out // 8
        for k in range(2 * R + 1):
            wide[out + k, column] = TAPS[k]
    main_hi, main_lo = split_np(wide[R : R + CY])
    zero = np.zeros_like(main_hi)
    main = np.concatenate(
        [np.concatenate([main_hi, main_lo], 1), np.concatenate([main_hi, zero], 1)], 0
    )
    side_hi, side_lo = split_np(np.concatenate([wide[:R], wide[R + CY :]], 0))
    side = np.concatenate([side_hi, side_hi, side_lo, np.zeros_like(side_hi)], 0)
    return main, side


def permutation(rows, columns, source):
    table = np.zeros((rows, columns), np.float32)
    for row in range(rows):
        for column in source(row):
            table[row, column] = 1.0
    return as_bf16(table)


def weight_order():
    return permutation(256, 256, lambda r: [(r % 32) * 8 + r // 32])


def message_order():
    return permutation(
        16 * SLOTS,
        ALL_ROWS,
        lambda r: [(r % SLOTS) * 16 + r // SLOTS] if r % SLOTS < ALL_ROWS // 16 else [],
    )


def gather_sum():
    low = {ext: 2 * EXT + 2 * n for n, ext in enumerate(BOUND)}

    def source(row):
        a, i, c = row // 128, row // 8 % 16, row % 8
        found = [i * SLOTS + (c + 1) * 2 + a]
        if c == 0:
            left = (i - 1) % NXL * SLOTS
            found += [i * SLOTS + low[1] + a, left + 18 + a, left + low[9] + a]
        if c == 7:
            right = (i + 1) % NXL * SLOTS
            found += [i * SLOTS + low[8] + a, right + a, right + low[0] + a]
        return found

    return permutation(TOK, NXL * SLOTS, source)


def interleave():
    return permutation(TOK, TOK, lambda r: [(r % 2) * 128 + r // 2])


def separate():
    return permutation(TOK, TOK, lambda r: [(r % 128) * 2 + r // 128])


def to_owners():
    return permutation(TOK, TOK, lambda r: [(r // 16 % 2) * 128 + (r % 16) * 8 + r // 32])


def to_home():
    return permutation(TOK, TOK, lambda r: [(r % 8) * 32 + r // 8])


def dot(left, right):
    return lax.dot_general(left, right, (((1,), (0,)), ((), ())), preferred_element_type=f32)


def dot_t(left, right):
    return lax.dot_general(left, right, (((1,), (1,)), ((), ())), preferred_element_type=f32)


def halves(values):
    high = values.astype(bf16)
    return high, (values - high.astype(f32)).astype(bf16)


def prep_kernel(fields_ref, smooth_ref, upper_ref, lower_ref):
    for tile in range(CX // 8):
        rows = slice(tile * 8, tile * 8 + 8)
        plane = [fields_ref[0, z, rows, :] for z in range(ZS + 2 * R)]
        for z in range(ZS):
            total = float(TAPS[R]) * plane[z + R]
            for k in range(1, R + 1):
                total = total + float(TAPS[R + k]) * (plane[z + R - k] + plane[z + R + k])
            smooth_ref[0, z, rows, :] = total
    for pair in range(ZS // 2):
        turned = smooth_ref[0, 2 * pair : 2 * pair + 2].reshape(128, 128).T
        lower_ref[0, :, pair * 128 : pair * 128 + 128] = turned[:R]
        upper_ref[0, :, pair * 128 : pair * 128 + 128] = turned[CY - R :]


def band_kernel(smooth_ref, band_ref, along_ref):
    band = band_ref[...]

    def step(index, carry):
        f, part = index // 4, index % 4
        values = smooth_ref[f, pl.ds(part * 4, 4)].reshape(256, CY)
        high, low = halves(values)
        both = dot(jnp.concatenate([high, low], 1), band)
        along_ref[f, pl.ds(part * 4, 4)] = (both[:, :CY] + both[:, CY:]).reshape(4, CX, CY)
        return carry

    lax.fori_loop(0, NF * 4, step, 0)


def weight_kernel(weight_ref, order_ref, out_ref):
    order = order_ref[...]
    for tile in range(KIN // 256):
        turned = dot(order, weight_ref[tile * 256 : tile * 256 + 256, :]).astype(bf16)
        for y in range(8):
            if tile < 8:
                pair, inner = tile // 4, tile % 4
                start = pair * 1024 + y * 128 + inner * 32
            else:
                start = 2048 + y * 64 + (tile - 8) * 32
            out_ref[start : start + 32, :] = turned[y * 32 : y * 32 + 32]


def embed_kernel(
    along_ref, upper_ref, lower_ref, side_ref, weight_ref, order_ref, out_ref, wide, smooth, lhs, mid
):
    side = side_ref[...]
    zero = jnp.zeros((ZS, PADX, CY), f32)
    for f in range(NF):
        wide[f, :, 0:PADX] = zero
        wide[f, :, PADX + CX :] = zero
        cells = jnp.concatenate([upper_ref[f], lower_ref[f]], 0)
        high = cells.astype(bf16).astype(f32)
        stacked = jnp.concatenate([high, cells - high, high, jnp.zeros_like(high)], 0)
        added = dot(stacked.T.astype(bf16), side)
        wide[f, :, PADX : PADX + CX] = along_ref[f] + added.reshape(ZS, CX, CY)

    def step(index, carry):
        f, z = index // ZS, index % ZS
        total = float(TAPS[R]) * wide[f, z, pl.ds(PADX - 8, 80), :]
        for k in range(1, R + 1):
            total = total + float(TAPS[R + k]) * (
                wide[f, z, pl.ds(PADX - 8 - k, 80), :] + wide[f, z, pl.ds(PADX - 8 + k, 80), :]
            )
        smooth[f, z] = total
        return carry

    lax.fori_loop(0, NF * ZS, step, 0)

    lane = lax.broadcasted_iota(jnp.int32, (16, 128), 1)
    first = lane < 64

    def put(ext, a, start, values):
        high, low = halves(values)
        row = (ext * 2 + a) * 16
        lhs[row : row + 16, start : start + 128] = high
        if ext in BOUND:
            row = HI_ROWS + (BOUND.index(ext) * 2 + a) * 16
            lhs[row : row + 16, start : start + 128] = low

    for ext in range(EXT):
        rows = slice(ext * 8, ext * 8 + 8)
        for a in range(2):
            for pair in range(2):
                block = smooth[2 * pair : 2 * pair + 2, a * 8 : a * 8 + 8, rows, :]
                turned = block.reshape(128, 128).T
                for y in range(8):
                    put(ext, a, pair * 1024 + y * 128, turned[y * 16 : y * 16 + 16])
        turned = smooth[4, :, rows, :].reshape(128, 128).T
        for m in range(4):
            even = turned[m * 32 : m * 32 + 16]
            odd = turned[m * 32 + 16 : m * 32 + 32]
            start = 2048 + m * 128
            put(ext, 0, start, jnp.where(first, even, pltpu.roll(odd, 64, 1)))
            put(ext, 1, start, jnp.where(first, pltpu.roll(even, 64, 1), odd))

    for tile in range(3):
        columns = slice(tile * 256, tile * 256 + 256)
        both = dot(lhs[...], weight_ref[:, columns])
        lead = both[:64] + both[HI_ROWS : HI_ROWS + 64]
        tail = both[256:HI_ROWS] + both[HI_ROWS + 64 :]
        lead_hi, lead_lo = halves(lead)
        tail_hi, tail_lo = halves(tail)
        mid[0:64] = lead_hi
        mid[64:256] = both[64:256].astype(bf16)
        mid[256:HI_ROWS] = tail_hi
        mid[HI_ROWS : HI_ROWS + 64] = lead_lo
        mid[HI_ROWS + 64 :] = tail_lo
        out_ref[:, columns] = dot(order_ref[...], mid[...]).astype(bf16)


def layer_norm(hidden):
    center = hidden - jnp.mean(hidden, axis=-1, keepdims=True)
    spread = jnp.mean(center * center, axis=-1, keepdims=True)
    return (center * lax.rsqrt(spread + 1e-05)).astype(bf16)


def attend(hidden, qkv_ref, out_ref, three, mixed):
    normed = layer_norm(hidden[...])
    for tile in range(9):
        columns = slice(tile * 256, tile * 256 + 256)
        three[:, columns] = dot(normed, qkv_ref[:, columns]).astype(bf16)
    first = lax.broadcasted_iota(jnp.int32, (128, 128), 1) < 64
    none = jnp.zeros((128, 128), bf16)
    for a in range(2):
        rows = slice(a * 128, a * 128 + 128)
        for pair in range(PAIRS):
            start = pair * 128
            query = three[rows, start : start + 128]
            keys = three[rows, D + start : D + start + 128]
            values = three[rows, 2 * D + start : 2 * D + start + 128]
            keys = jnp.concatenate([jnp.where(first, keys, none), jnp.where(first, none, keys)], 0)
            values = jnp.concatenate(
                [jnp.where(first, values, none), jnp.where(first, none, values)], 0
            )
            weights = jnp.exp(dot_t(query, keys) * 0.125)
            left, right = weights[:, :128], weights[:, 128:]
            left = left * (1.0 / jnp.sum(left, axis=-1, keepdims=True))
            right = right * (1.0 / jnp.sum(right, axis=-1, keepdims=True))
            weights = jnp.concatenate([left.astype(bf16), right.astype(bf16)], 1)
            mixed[rows, start : start + 128] = dot(weights, values).astype(bf16)
    for tile in range(3):
        columns = slice(tile * 256, tile * 256 + 256)
        branch = dot(mixed[...], out_ref[:, columns]).astype(bf16)
        hidden[:, columns] = hidden[:, columns] + branch.astype(f32)


def x_kernel(slots_ref, sum_ref, qkv_ref, outw_ref, order_ref, out_ref, hidden, three, mixed):
    hidden[...] = dot(sum_ref[...], slots_ref[...])
    attend(hidden, qkv_ref, outw_ref, three, mixed)
    out_ref[...] = dot(order_ref[...], hidden[...].astype(bf16)).astype(bf16)


def y_kernel(
    tokens_ref,
    split_ref,
    qkv_ref,
    outw_ref,
    up_ref,
    down_ref,
    order_ref,
    out_ref,
    hidden,
    three,
    mixed,
    upper,
):
    hidden[...] = dot(split_ref[...], tokens_ref[...])
    attend(hidden, qkv_ref, outw_ref, three, mixed)
    normed = layer_norm(hidden[...])
    for tile in range(FF // 256):
        columns = slice(tile * 256, tile * 256 + 256)
        upper[:, columns] = jax.nn.gelu(dot(normed, up_ref[:, columns]), approximate=True).astype(bf16)
    for tile in range(3):
        columns = slice(tile * 256, tile * 256 + 256)
        total = hidden[:, columns] + dot(upper[...], down_ref[:, columns])
        out_ref[:, columns] = dot(order_ref[...], total.astype(bf16)).astype(bf16)


def home_kernel(tokens_ref, order_ref, out_ref):
    out_ref[...] = dot(order_ref[...], tokens_ref[...]).astype(bf16)


def whole(kernel, out_shape, scratch, flops, limit):
    space = pl.BlockSpec(memory_space=pltpu.VMEM)

    def call(*operands):
        size = sum(x.size * x.dtype.itemsize for x in operands)
        return pl.pallas_call(
            kernel,
            out_shape=out_shape,
            in_specs=[space] * len(operands),
            out_specs=space,
            scratch_shapes=scratch,
            compiler_params=pltpu.CompilerParams(vmem_limit_bytes=limit << 20),
            cost_estimate=pl.CostEstimate(flops=flops, bytes_accessed=size, transcendentals=0),
        )(*operands)

    return call


def like(shape, kind=bf16):
    return jax.ShapeDtypeStruct(shape, kind)


def prepare(fields):
    plane = (1, ZS + 2 * R, CX, CY)
    strip = pl.BlockSpec((1, R, ZS * CX), lambda f: (f, 0, 0))
    return pl.pallas_call(
        prep_kernel,
        grid=(NF,),
        in_specs=[pl.BlockSpec(plane, lambda f: (f, 0, 0, 0))],
        out_specs=[pl.BlockSpec((1, ZS, CX, CY), lambda f: (f, 0, 0, 0)), strip, strip],
        out_shape=[
            like((NF, ZS, CX, CY), f32),
            like((NF, R, ZS * CX), f32),
            like((NF, R, ZS * CX), f32),
        ],
        compiler_params=pltpu.CompilerParams(vmem_limit_bytes=16 << 20),
    )(fields)


def shards(fields, embed_weight, qkv_weight, out_weight, up_weight, down_weight):
    band, side = band_tables()
    count = lax.axis_size("gy")
    smooth, upper, lower = prepare(fields)
    upper = lax.ppermute(upper, "gy", [(i, (i + 1) % count) for i in range(count)])
    lower = lax.ppermute(lower, "gy", [((i + 1) % count, i) for i in range(count)])
    along = whole(band_kernel, like((NF, ZS, CX, CY), f32), [], 2 * 5120 * 256 * 256, 16)(
        smooth, band
    )
    weight = whole(weight_kernel, like((KIN, D)), [], 2 * KIN * 256 * D, 24)(
        embed_weight, weight_order()
    )
    slots = whole(
        embed_kernel,
        like((16 * SLOTS, D)),
        [
            pltpu.VMEM((NF, ZS, CX + 2 * PADX, CY), f32),
            pltpu.VMEM((NF, ZS, 80, CY), f32),
            pltpu.VMEM((ALL_ROWS, KIN), bf16),
            pltpu.VMEM((ALL_ROWS, 256), bf16),
        ],
        2 * ALL_ROWS * KIN * D,
        40,
    )(along, upper, lower, side, weight, message_order())
    slots = lax.all_to_all(
        slots.reshape(NXL, SLOTS, D), "gx", split_axis=0, concat_axis=0, tiled=True
    ).reshape(NXL * SLOTS, D)
    attention = [
        pltpu.VMEM((TOK, D), f32),
        pltpu.VMEM((TOK, 3 * D), bf16),
        pltpu.VMEM((TOK, D), bf16),
    ]
    tokens = whole(x_kernel, like((TOK, D)), attention, 2 * TOK * D * 4 * D, 24)(
        slots, gather_sum(), qkv_weight, out_weight, interleave()
    )
    tokens = lax.all_to_all(
        tokens.reshape(128, 2, D), ("gx", "gy"), split_axis=0, concat_axis=0, tiled=True
    ).reshape(TOK, D)
    tokens = whole(
        y_kernel,
        like((TOK, D)),
        attention + [pltpu.VMEM((TOK, FF), bf16)],
        2 * TOK * D * (4 * D + 2 * FF),
        40,
    )(tokens, separate(), qkv_weight, out_weight, up_weight, down_weight, to_owners())
    tokens = lax.all_to_all(
        tokens.reshape(8, 32, D), "gy", split_axis=0, concat_axis=0, tiled=True
    ).reshape(TOK, D)
    tokens = whole(home_kernel, like((TOK, D)), [], 2 * TOK * TOK * D, 8)(tokens, to_home())
    return tokens.reshape(2, 16, 8, D)


def solution(mesh):
    return jax.shard_map(
        shards,
        mesh=mesh,
        in_specs=(P(None, None, "gx", "gy"), P(), P(), P(), P(), P()),
        out_specs=P(None, "gy", "gx", None),
        check_vma=False,
    )
```

```python
import functools

import jax
import jax.numpy as jnp
import ml_dtypes
import numpy as np
from jax import lax
from jax.experimental import pallas as pl
from jax.experimental.pallas import tpu as pltpu
from jax.sharding import PartitionSpec as P

R = 4
NF = 5
ZS = 16
CX = 64
CY = 128
D = 768
FF = 3072
KIN = 2560
PAIRS = 6
NXL = 16
TOK = 256
EXT = 10
SLOTS = 32
BOUND = (0, 1, 8, 9)
HI_ROWS = EXT * 32
ALL_ROWS = HI_ROWS + 128
PADX = 16
bf16 = jnp.bfloat16
f32 = jnp.float32


def np_taps():
    offsets = np.arange(-R, R + 1).astype(np.float32)
    values = np.exp(-offsets * offsets / np.float32(4.5)).astype(np.float32)
    return (values / values.sum(dtype=np.float32)).astype(np.float32)


TAPS = np_taps()


def as_bf16(values):
    return np.asarray(values, np.float32).astype(ml_dtypes.bfloat16)


def split_np(values):
    high = as_bf16(values)
    low = as_bf16(values - high.astype(np.float32))
    return high, low


def band_tables():
    wide = np.zeros((CY + 2 * R, CY), np.float32)
    for out in range(CY):
        column = (out % 8) * 16 + out // 8
        for k in range(2 * R + 1):
            wide[out + k, column] = TAPS[k]
    main_hi, main_lo = split_np(wide[R : R + CY])
    zero = np.zeros_like(main_hi)
    main = np.concatenate(
        [np.concatenate([main_hi, main_lo], 1), np.concatenate([main_hi, zero], 1)], 0
    )
    side_hi, side_lo = split_np(np.concatenate([wide[:R], wide[R + CY :]], 0))
    side = np.concatenate([side_hi, side_hi, side_lo, np.zeros_like(side_hi)], 0)
    return main, side


def permutation(rows, columns, source):
    table = np.zeros((rows, columns), np.float32)
    for row in range(rows):
        for column in source(row):
            table[row, column] = 1.0
    return as_bf16(table)


def weight_order():
    return permutation(256, 256, lambda r: [(r % 32) * 8 + r // 32])


def message_order():
    return permutation(
        16 * SLOTS,
        ALL_ROWS,
        lambda r: [(r % SLOTS) * 16 + r // SLOTS] if r % SLOTS < ALL_ROWS // 16 else [],
    )


def gather_sum():
    low = {ext: 2 * EXT + 2 * n for n, ext in enumerate(BOUND)}

    def source(row):
        a, i, c = row // 128, row // 8 % 16, row % 8
        found = [i * SLOTS + (c + 1) * 2 + a]
        if c == 0:
            left = (i - 1) % NXL * SLOTS
            found += [i * SLOTS + low[1] + a, left + 18 + a, left + low[9] + a]
        if c == 7:
            right = (i + 1) % NXL * SLOTS
            found += [i * SLOTS + low[8] + a, right + a, right + low[0] + a]
        return found

    return permutation(TOK, NXL * SLOTS, source)


def interleave():
    return permutation(TOK, TOK, lambda r: [(r % 2) * 128 + r // 2])


def separate():
    return permutation(TOK, TOK, lambda r: [(r % 128) * 2 + r // 128])


def to_owners():
    return permutation(TOK, TOK, lambda r: [(r // 16 % 2) * 128 + (r % 16) * 8 + r // 32])


def to_home():
    return permutation(TOK, TOK, lambda r: [(r % 8) * 32 + r // 8])


def dot(left, right):
    return lax.dot_general(left, right, (((1,), (0,)), ((), ())), preferred_element_type=f32)


def dot_t(left, right):
    return lax.dot_general(left, right, (((1,), (1,)), ((), ())), preferred_element_type=f32)


def halves(values):
    high = values.astype(bf16)
    return high, (values - high.astype(f32)).astype(bf16)


def prep_kernel(fields_ref, smooth_ref, upper_ref, lower_ref):
    for tile in range(CX // 8):
        rows = slice(tile * 8, tile * 8 + 8)
        plane = [fields_ref[0, z, rows, :] for z in range(ZS + 2 * R)]
        for z in range(ZS):
            total = float(TAPS[R]) * plane[z + R]
            for k in range(1, R + 1):
                total = total + float(TAPS[R + k]) * (plane[z + R - k] + plane[z + R + k])
            smooth_ref[0, z, rows, :] = total
    for pair in range(ZS // 2):
        turned = smooth_ref[0, 2 * pair : 2 * pair + 2].reshape(128, 128).T
        lower_ref[0, :, pair * 128 : pair * 128 + 128] = turned[:R]
        upper_ref[0, :, pair * 128 : pair * 128 + 128] = turned[CY - R :]


def band_kernel(smooth_ref, band_ref, along_ref):
    band = band_ref[...]

    def step(index, carry):
        f, part = index // 4, index % 4
        values = smooth_ref[f, pl.ds(part * 4, 4)].reshape(256, CY)
        high, low = halves(values)
        both = dot(jnp.concatenate([high, low], 1), band)
        along_ref[f, pl.ds(part * 4, 4)] = (both[:, :CY] + both[:, CY:]).reshape(4, CX, CY)
        return carry

    lax.fori_loop(0, NF * 4, step, 0)


def weight_kernel(weight_ref, order_ref, out_ref):
    order = order_ref[...]
    for tile in range(KIN // 256):
        turned = dot(order, weight_ref[tile * 256 : tile * 256 + 256, :]).astype(bf16)
        for y in range(8):
            if tile < 8:
                pair, inner = tile // 4, tile % 4
                start = pair * 1024 + y * 128 + inner * 32
            else:
                start = 2048 + y * 64 + (tile - 8) * 32
            out_ref[start : start + 32, :] = turned[y * 32 : y * 32 + 32]


def embed_kernel(
    along_ref, upper_ref, lower_ref, side_ref, weight_ref, order_ref, out_ref, wide, smooth, lhs, mid
):
    side = side_ref[...]
    zero = jnp.zeros((ZS, PADX, CY), f32)
    for f in range(NF):
        wide[f, :, 0:PADX] = zero
        wide[f, :, PADX + CX :] = zero
        cells = jnp.concatenate([upper_ref[f], lower_ref[f]], 0)
        high = cells.astype(bf16).astype(f32)
        stacked = jnp.concatenate([high, cells - high, high, jnp.zeros_like(high)], 0)
        added = dot(stacked.T.astype(bf16), side)
        wide[f, :, PADX : PADX + CX] = along_ref[f] + added.reshape(ZS, CX, CY)

    def step(index, carry):
        f, z = index // ZS, index % ZS
        total = float(TAPS[R]) * wide[f, z, pl.ds(PADX - 8, 80), :]
        for k in range(1, R + 1):
            total = total + float(TAPS[R + k]) * (
                wide[f, z, pl.ds(PADX - 8 - k, 80), :] + wide[f, z, pl.ds(PADX - 8 + k, 80), :]
            )
        smooth[f, z] = total
        return carry

    lax.fori_loop(0, NF * ZS, step, 0)

    lane = lax.broadcasted_iota(jnp.int32, (16, 128), 1)
    first = lane < 64

    def put(ext, a, start, values):
        high, low = halves(values)
        row = (ext * 2 + a) * 16
        lhs[row : row + 16, start : start + 128] = high
        if ext in BOUND:
            row = HI_ROWS + (BOUND.index(ext) * 2 + a) * 16
            lhs[row : row + 16, start : start + 128] = low

    for ext in range(EXT):
        rows = slice(ext * 8, ext * 8 + 8)
        for a in range(2):
            for pair in range(2):
                block = smooth[2 * pair : 2 * pair + 2, a * 8 : a * 8 + 8, rows, :]
                turned = block.reshape(128, 128).T
                for y in range(8):
                    put(ext, a, pair * 1024 + y * 128, turned[y * 16 : y * 16 + 16])
        turned = smooth[4, :, rows, :].reshape(128, 128).T
        for m in range(4):
            even = turned[m * 32 : m * 32 + 16]
            odd = turned[m * 32 + 16 : m * 32 + 32]
            start = 2048 + m * 128
            put(ext, 0, start, jnp.where(first, even, pltpu.roll(odd, 64, 1)))
            put(ext, 1, start, jnp.where(first, pltpu.roll(even, 64, 1), odd))

    for tile in range(3):
        columns = slice(tile * 256, tile * 256 + 256)
        both = dot(lhs[...], weight_ref[:, columns])
        lead = both[:64] + both[HI_ROWS : HI_ROWS + 64]
        tail = both[256:HI_ROWS] + both[HI_ROWS + 64 :]
        lead_hi, lead_lo = halves(lead)
        tail_hi, tail_lo = halves(tail)
        mid[0:64] = lead_hi
        mid[64:256] = both[64:256].astype(bf16)
        mid[256:HI_ROWS] = tail_hi
        mid[HI_ROWS : HI_ROWS + 64] = lead_lo
        mid[HI_ROWS + 64 :] = tail_lo
        out_ref[:, columns] = dot(order_ref[...], mid[...]).astype(bf16)


def layer_norm(hidden):
    center = hidden - jnp.mean(hidden, axis=-1, keepdims=True)
    spread = jnp.mean(center * center, axis=-1, keepdims=True)
    return (center * lax.rsqrt(spread + 1e-05)).astype(bf16)


def attend(hidden, qkv_ref, out_ref, three, mixed):
    normed = layer_norm(hidden[...])
    for tile in range(9):
        columns = slice(tile * 256, tile * 256 + 256)
        three[:, columns] = dot(normed, qkv_ref[:, columns]).astype(bf16)
    first = lax.broadcasted_iota(jnp.int32, (128, 128), 1) < 64
    none = jnp.zeros((128, 128), bf16)
    for a in range(2):
        rows = slice(a * 128, a * 128 + 128)
        for pair in range(PAIRS):
            start = pair * 128
            query = three[rows, start : start + 128]
            keys = three[rows, D + start : D + start + 128]
            values = three[rows, 2 * D + start : 2 * D + start + 128]
            keys = jnp.concatenate([jnp.where(first, keys, none), jnp.where(first, none, keys)], 0)
            values = jnp.concatenate(
                [jnp.where(first, values, none), jnp.where(first, none, values)], 0
            )
            weights = jnp.exp(dot_t(query, keys) * 0.125)
            left, right = weights[:, :128], weights[:, 128:]
            left = left * (1.0 / jnp.sum(left, axis=-1, keepdims=True))
            right = right * (1.0 / jnp.sum(right, axis=-1, keepdims=True))
            weights = jnp.concatenate([left.astype(bf16), right.astype(bf16)], 1)
            mixed[rows, start : start + 128] = dot(weights, values).astype(bf16)
    for tile in range(3):
        columns = slice(tile * 256, tile * 256 + 256)
        branch = dot(mixed[...], out_ref[:, columns]).astype(bf16)
        hidden[:, columns] = hidden[:, columns] + branch.astype(f32)


def x_kernel(slots_ref, sum_ref, qkv_ref, outw_ref, order_ref, out_ref, hidden, three, mixed):
    hidden[...] = dot(sum_ref[...], slots_ref[...])
    attend(hidden, qkv_ref, outw_ref, three, mixed)
    tokens = dot(order_ref[...], hidden[...].astype(bf16)).astype(bf16)
    out_ref[...] = tokens.reshape(128, 2, D)


def y_kernel(
    tokens_ref,
    split_ref,
    qkv_ref,
    outw_ref,
    up_ref,
    down_ref,
    order_ref,
    out_ref,
    hidden,
    three,
    mixed,
    upper,
):
    hidden[...] = dot(split_ref[...], tokens_ref[...].reshape(TOK, D))
    attend(hidden, qkv_ref, outw_ref, three, mixed)
    normed = layer_norm(hidden[...])
    for tile in range(FF // 256):
        columns = slice(tile * 256, tile * 256 + 256)
        upper[:, columns] = jax.nn.gelu(dot(normed, up_ref[:, columns]), approximate=True).astype(bf16)
    for tile in range(3):
        columns = slice(tile * 256, tile * 256 + 256)
        total = hidden[:, columns] + dot(upper[...], down_ref[:, columns])
        out_ref[:, columns] = dot(order_ref[...], total.astype(bf16)).astype(bf16)


def home_kernel(tokens_ref, order_ref, out_ref):
    out_ref[...] = dot(order_ref[...], tokens_ref[...]).astype(bf16)


def whole(kernel, out_shape, scratch, flops, limit):
    space = pl.BlockSpec(memory_space=pltpu.VMEM)

    def call(*operands):
        size = sum(x.size * x.dtype.itemsize for x in operands)
        return pl.pallas_call(
            kernel,
            out_shape=out_shape,
            in_specs=[space] * len(operands),
            out_specs=space,
            scratch_shapes=scratch,
            compiler_params=pltpu.CompilerParams(vmem_limit_bytes=limit << 20),
            cost_estimate=pl.CostEstimate(flops=flops, bytes_accessed=size, transcendentals=0),
        )(*operands)

    return call


def like(shape, kind=bf16):
    return jax.ShapeDtypeStruct(shape, kind)


def prepare(fields):
    plane = (1, ZS + 2 * R, CX, CY)
    strip = pl.BlockSpec((1, R, ZS * CX), lambda f: (f, 0, 0))
    return pl.pallas_call(
        prep_kernel,
        grid=(NF,),
        in_specs=[pl.BlockSpec(plane, lambda f: (f, 0, 0, 0))],
        out_specs=[pl.BlockSpec((1, ZS, CX, CY), lambda f: (f, 0, 0, 0)), strip, strip],
        out_shape=[
            like((NF, ZS, CX, CY), f32),
            like((NF, R, ZS * CX), f32),
            like((NF, R, ZS * CX), f32),
        ],
        compiler_params=pltpu.CompilerParams(vmem_limit_bytes=8 << 20),
    )(fields)


def shards(fields, embed_weight, qkv_weight, out_weight, up_weight, down_weight):
    band, side = band_tables()
    count = lax.axis_size("gy")
    smooth, upper, lower = prepare(fields)
    upper = lax.ppermute(upper, "gy", [(i, (i + 1) % count) for i in range(count)])
    lower = lax.ppermute(lower, "gy", [((i + 1) % count, i) for i in range(count)])
    along = whole(band_kernel, like((NF, ZS, CX, CY), f32), [], 2 * 5120 * 256 * 256, 8)(
        smooth, band
    )
    weight = whole(weight_kernel, like((KIN, D)), [], 2 * KIN * 256 * D, 8)(
        embed_weight, weight_order()
    )
    slots = whole(
        embed_kernel,
        like((16 * SLOTS, D)),
        [
            pltpu.VMEM((NF, ZS, CX + 2 * PADX, CY), f32),
            pltpu.VMEM((NF, ZS, 80, CY), f32),
            pltpu.VMEM((ALL_ROWS, KIN), bf16),
            pltpu.VMEM((ALL_ROWS, 256), bf16),
        ],
        2 * ALL_ROWS * KIN * D,
        14,
    )(along, upper, lower, side, weight, message_order())
    slots = lax.all_to_all(
        slots.reshape(NXL, SLOTS, D), "gx", split_axis=0, concat_axis=0, tiled=True
    ).reshape(NXL * SLOTS, D)
    attention = [
        pltpu.VMEM((TOK, D), f32),
        pltpu.VMEM((TOK, 3 * D), bf16),
        pltpu.VMEM((TOK, D), bf16),
    ]
    tokens = whole(x_kernel, like((128, 2, D)), attention, 2 * TOK * D * 4 * D, 10)(
        slots, gather_sum(), qkv_weight, out_weight, interleave()
    )
    tokens = lax.all_to_all(
        tokens, ("gx", "gy"), split_axis=0, concat_axis=0, tiled=True
    )
    tokens = whole(
        y_kernel,
        like((TOK, D)),
        attention + [pltpu.VMEM((TOK, FF), bf16)],
        2 * TOK * D * (4 * D + 2 * FF),
        14,
    )(tokens, separate(), qkv_weight, out_weight, up_weight, down_weight, to_owners())
    tokens = lax.all_to_all(
        tokens.reshape(8, 32, D), "gy", split_axis=0, concat_axis=0, tiled=True
    ).reshape(TOK, D)
    tokens = whole(home_kernel, like((TOK, D)), [], 2 * TOK * TOK * D, 8)(tokens, to_home())
    return tokens.reshape(2, 16, 8, D)


def solution(mesh):
    return jax.shard_map(
        shards,
        mesh=mesh,
        in_specs=(P(None, None, "gx", "gy"), P(), P(), P(), P(), P()),
        out_specs=P(None, "gy", "gx", None),
        check_vma=False,
    )
```

```python
import functools

import jax
import jax.numpy as jnp
import ml_dtypes
import numpy as np
from jax import lax
from jax.experimental import pallas as pl
from jax.experimental.pallas import tpu as pltpu
from jax.sharding import PartitionSpec as P

R = 4
NF = 5
ZS = 16
CX = 64
CY = 128
D = 768
FF = 3072
KIN = 2560
PAIRS = 6
NXL = 16
TOK = 256
EXT = 10
SLOTS = 28
BOUND = (0, 1, 8, 9)
HI_ROWS = EXT * 32
ALL_ROWS = HI_ROWS + 128
PADX = 16
bf16 = jnp.bfloat16
f32 = jnp.float32


def np_taps():
    offsets = np.arange(-R, R + 1).astype(np.float32)
    values = np.exp(-offsets * offsets / np.float32(4.5)).astype(np.float32)
    return (values / values.sum(dtype=np.float32)).astype(np.float32)


TAPS = np_taps()


def as_bf16(values):
    return np.asarray(values, np.float32).astype(ml_dtypes.bfloat16)


def split_np(values):
    high = as_bf16(values)
    low = as_bf16(values - high.astype(np.float32))
    return high, low


def side_table():
    wide = np.zeros((CY + 2 * R, CY), np.float32)
    for out in range(CY):
        column = (out % 8) * 16 + out // 8
        for k in range(2 * R + 1):
            wide[out + k, column] = TAPS[k]
    high, low = split_np(np.concatenate([wide[:R], wide[R + CY :]], 0))
    return np.concatenate([high, high, low, np.zeros_like(high)], 0)


def band_table():
    row = lax.broadcasted_iota(jnp.int32, (CY, CY), 0)
    column = lax.broadcasted_iota(jnp.int32, (CY, CY), 1)
    apart = jnp.abs(row - ((column & 15) * 8 + (column >> 4)))
    high = jnp.zeros((CY, CY), f32)
    low = jnp.zeros((CY, CY), f32)
    for k in range(R + 1):
        tap_hi, tap_lo = split_np(TAPS[R + k])
        high = jnp.where(apart == k, float(tap_hi), high)
        low = jnp.where(apart == k, float(tap_lo), low)
    left = jnp.concatenate([high, high], 0)
    right = jnp.concatenate([low, jnp.zeros_like(low)], 0)
    return jnp.concatenate([left, right], 1).astype(bf16)


def weight_order():
    row = lax.broadcasted_iota(jnp.int32, (256, 256), 0)
    column = lax.broadcasted_iota(jnp.int32, (256, 256), 1)
    return jnp.where(column == (row & 31) * 8 + (row >> 5), 1.0, 0.0).astype(bf16)


def permutation(rows, columns, source):
    table = np.zeros((rows, columns), np.float32)
    for row in range(rows):
        for column in source(row):
            table[row, column] = 1.0
    return as_bf16(table)


def message_order():
    return permutation(16 * SLOTS, ALL_ROWS, lambda r: [(r % SLOTS) * 16 + r // SLOTS])


def gather_sum():
    low = {ext: 2 * EXT + 2 * n for n, ext in enumerate(BOUND)}

    def source(row):
        a, i, c = row // 128, row // 8 % 16, row % 8
        found = [i * SLOTS + (c + 1) * 2 + a]
        if c == 0:
            left = (i - 1) % NXL * SLOTS
            found += [i * SLOTS + low[1] + a, left + 18 + a, left + low[9] + a]
        if c == 7:
            right = (i + 1) % NXL * SLOTS
            found += [i * SLOTS + low[8] + a, right + a, right + low[0] + a]
        return found

    return permutation(TOK, NXL * SLOTS, source)


def interleave():
    return permutation(TOK, TOK, lambda r: [(r % 2) * 128 + r // 2])


def separate():
    return permutation(TOK, TOK, lambda r: [(r % 128) * 2 + r // 128])


def to_owners():
    return permutation(TOK, TOK, lambda r: [(r // 16 % 2) * 128 + (r % 16) * 8 + r // 32])


def to_home():
    return permutation(TOK, TOK, lambda r: [(r % 8) * 32 + r // 8])


def dot(left, right):
    return lax.dot_general(left, right, (((1,), (0,)), ((), ())), preferred_element_type=f32)


def dot_t(left, right):
    return lax.dot_general(left, right, (((1,), (1,)), ((), ())), preferred_element_type=f32)


def halves(values):
    high = values.astype(bf16)
    return high, (values - high.astype(f32)).astype(bf16)


def prep_kernel(fields_ref, smooth_ref, upper_ref, lower_ref, cells, arrived):
    copies = [
        pltpu.make_async_copy(fields_ref.at[f], cells.at[f], arrived.at[f]) for f in range(NF)
    ]
    for copy in copies:
        copy.start()
    for f in range(NF):
        copies[f].wait()
        for tile in range(CX // 8):
            rows = slice(tile * 8, tile * 8 + 8)
            plane = [cells[f, z, rows, :] for z in range(ZS + 2 * R)]
            for z in range(ZS):
                total = float(TAPS[R]) * plane[z + R]
                for k in range(1, R + 1):
                    total = total + float(TAPS[R + k]) * (plane[z + R - k] + plane[z + R + k])
                smooth_ref[f, z, rows, :] = total
        for pair in range(ZS // 2):
            turned = smooth_ref[f, 2 * pair : 2 * pair + 2].reshape(128, 128).T
            lower_ref[f, :, pair * 128 : pair * 128 + 128] = turned[:R]
            upper_ref[f, :, pair * 128 : pair * 128 + 128] = turned[CY - R :]


def band_kernel(smooth_ref, weight_ref, along_ref, out_ref):
    band = band_table()
    order = weight_order()
    for f in range(NF):
        for part in range(4):
            planes = slice(part * 4, part * 4 + 4)
            high, low = halves(smooth_ref[f, planes].reshape(256, CY))
            both = dot(jnp.concatenate([high, low], 1), band)
            along_ref[f, planes] = (both[:, :CY] + both[:, CY:]).reshape(4, CX, CY)
        for tile in (2 * f, 2 * f + 1):
            turned = dot(order, weight_ref[tile * 256 : tile * 256 + 256, :]).astype(bf16)
            for y in range(8):
                if tile < 8:
                    start = tile // 4 * 1024 + y * 128 + tile % 4 * 32
                else:
                    start = 2048 + y * 64 + (tile - 8) * 32
                out_ref[start : start + 32, :] = turned[y * 32 : y * 32 + 32]


def embed_kernel(
    along_ref, upper_ref, lower_ref, side_ref, weight_ref, order_ref, out_ref, wide, smooth, lhs, both, mid
):
    side = side_ref[...]
    zero = jnp.zeros((ZS, PADX, CY), f32)
    lane = lax.broadcasted_iota(jnp.int32, (16, 128), 1)
    first = lane < 64

    def put(ext, a, start, values):
        high, low = halves(values)
        row = (ext * 2 + a) * 16
        lhs[row : row + 16, start : start + 128] = high
        if ext in BOUND:
            row = HI_ROWS + (BOUND.index(ext) * 2 + a) * 16
            lhs[row : row + 16, start : start + 128] = low

    for chunk, members in enumerate(((0, 1), (2, 3), (4,))):
        for f in members:
            wide[f, :, 0:PADX] = zero
            wide[f, :, PADX + CX :] = zero
            cells = jnp.concatenate([upper_ref[f], lower_ref[f]], 0)
            high = cells.astype(bf16).astype(f32)
            stacked = jnp.concatenate([high, cells - high, high, jnp.zeros_like(high)], 0)
            added = dot(stacked.T.astype(bf16), side)
            wide[f, :, PADX : PADX + CX] = along_ref[f] + added.reshape(ZS, CX, CY)
            for z in range(ZS):
                total = float(TAPS[R]) * wide[f, z, PADX - 8 : PADX + 72, :]
                for k in range(1, R + 1):
                    total = total + float(TAPS[R + k]) * (
                        wide[f, z, PADX - 8 - k : PADX + 72 - k, :]
                        + wide[f, z, PADX - 8 + k : PADX + 72 + k, :]
                    )
                smooth[f, z] = total
        for ext in range(EXT):
            rows = slice(ext * 8, ext * 8 + 8)
            if len(members) == 2:
                for a in range(2):
                    block = smooth[members[0] : members[0] + 2, a * 8 : a * 8 + 8, rows, :]
                    turned = block.reshape(128, 128).T
                    for y in range(8):
                        put(ext, a, chunk * 1024 + y * 128, turned[y * 16 : y * 16 + 16])
            else:
                turned = smooth[4, :, rows, :].reshape(128, 128).T
                for m in range(4):
                    even = turned[m * 32 : m * 32 + 16]
                    odd = turned[m * 32 + 16 : m * 32 + 32]
                    start = 2048 + m * 128
                    put(ext, 0, start, jnp.where(first, even, pltpu.roll(odd, 64, 1)))
                    put(ext, 1, start, jnp.where(first, pltpu.roll(even, 64, 1), odd))
        deep = slice(chunk * 1024, min(chunk * 1024 + 1024, KIN))
        for tile in range(3):
            columns = slice(tile * 256, tile * 256 + 256)
            part = dot(lhs[:, deep], weight_ref[deep, columns])
            both[:, columns] = part if chunk == 0 else both[:, columns] + part

    for tile in range(3):
        columns = slice(tile * 256, tile * 256 + 256)
        lead = both[:64, columns] + both[HI_ROWS : HI_ROWS + 64, columns]
        tail = both[256:HI_ROWS, columns] + both[HI_ROWS + 64 :, columns]
        lead_hi, lead_lo = halves(lead)
        tail_hi, tail_lo = halves(tail)
        mid[0:64, columns] = lead_hi
        mid[64:256, columns] = both[64:256, columns].astype(bf16)
        mid[256:HI_ROWS, columns] = tail_hi
        mid[HI_ROWS : HI_ROWS + 64, columns] = lead_lo
        mid[HI_ROWS + 64 :, columns] = tail_lo
    slots = dot(order_ref[...], mid[...]).astype(bf16)
    out_ref[...] = slots.reshape(16 * SLOTS // 4, 4, D)


def layer_norm(hidden):
    center = hidden - jnp.mean(hidden, axis=-1, keepdims=True)
    spread = jnp.mean(center * center, axis=-1, keepdims=True)
    return (center * lax.rsqrt(spread + 1e-05)).astype(bf16)


def attend(hidden, qkv_ref, out_ref, three, mixed):
    normed = layer_norm(hidden[...])
    for tile in range(9):
        columns = slice(tile * 256, tile * 256 + 256)
        three[:, columns] = dot(normed, qkv_ref[:, columns]).astype(bf16)
    first = lax.broadcasted_iota(jnp.int32, (128, 128), 1) < 64
    none = jnp.zeros((128, 128), bf16)
    for a in range(2):
        rows = slice(a * 128, a * 128 + 128)
        for pair in range(PAIRS):
            start = pair * 128
            query = three[rows, start : start + 128]
            keys = three[rows, D + start : D + start + 128]
            values = three[rows, 2 * D + start : 2 * D + start + 128]
            keys = jnp.concatenate([jnp.where(first, keys, none), jnp.where(first, none, keys)], 0)
            values = jnp.concatenate(
                [jnp.where(first, values, none), jnp.where(first, none, values)], 0
            )
            weights = jnp.exp(dot_t(query, keys) * 0.125)
            left, right = weights[:, :128], weights[:, 128:]
            left = left * (1.0 / jnp.sum(left, axis=-1, keepdims=True))
            right = right * (1.0 / jnp.sum(right, axis=-1, keepdims=True))
            weights = jnp.concatenate([left.astype(bf16), right.astype(bf16)], 1)
            mixed[rows, start : start + 128] = dot(weights, values).astype(bf16)
    for tile in range(3):
        columns = slice(tile * 256, tile * 256 + 256)
        branch = dot(mixed[...], out_ref[:, columns]).astype(bf16)
        hidden[:, columns] = hidden[:, columns] + branch.astype(f32)


def x_kernel(slots_ref, sum_ref, qkv_ref, outw_ref, order_ref, out_ref, hidden, three, mixed):
    hidden[...] = dot(sum_ref[...], slots_ref[...].reshape(NXL * SLOTS, D))
    attend(hidden, qkv_ref, outw_ref, three, mixed)
    tokens = dot(order_ref[...], hidden[...].astype(bf16)).astype(bf16)
    out_ref[...] = tokens.reshape(128, 2, D)


def y_kernel(
    tokens_ref,
    split_ref,
    qkv_ref,
    outw_ref,
    up_ref,
    down_ref,
    order_ref,
    out_ref,
    hidden,
    three,
    mixed,
    upper,
):
    hidden[...] = dot(split_ref[...], tokens_ref[...].reshape(TOK, D))
    attend(hidden, qkv_ref, outw_ref, three, mixed)
    normed = layer_norm(hidden[...])
    for tile in range(FF // 256):
        columns = slice(tile * 256, tile * 256 + 256)
        upper[:, columns] = jax.nn.gelu(dot(normed, up_ref[:, columns]), approximate=True).astype(bf16)
    for tile in range(3):
        columns = slice(tile * 256, tile * 256 + 256)
        total = hidden[:, columns] + dot(upper[...], down_ref[:, columns])
        out_ref[:, columns] = dot(order_ref[...], total.astype(bf16)).astype(bf16)


def home_kernel(tokens_ref, order_ref, out_ref):
    out_ref[...] = dot(order_ref[...], tokens_ref[...]).astype(bf16)


def whole(kernel, out_shape, scratch, flops, limit):
    space = pl.BlockSpec(memory_space=pltpu.VMEM)

    def call(*operands):
        size = sum(x.size * x.dtype.itemsize for x in operands)
        return pl.pallas_call(
            kernel,
            out_shape=out_shape,
            in_specs=[space] * len(operands),
            out_specs=[space] * len(out_shape) if isinstance(out_shape, list) else space,
            scratch_shapes=scratch,
            compiler_params=pltpu.CompilerParams(vmem_limit_bytes=limit << 20),
            cost_estimate=pl.CostEstimate(flops=flops, bytes_accessed=size, transcendentals=0),
        )(*operands)

    return call


def like(shape, kind=bf16):
    return jax.ShapeDtypeStruct(shape, kind)


def prepare(fields):
    space = pl.BlockSpec(memory_space=pltpu.VMEM)
    return pl.pallas_call(
        prep_kernel,
        in_specs=[pl.BlockSpec(memory_space=pltpu.HBM)],
        out_specs=[space] * 3,
        out_shape=[
            like((NF, ZS, CX, CY), f32),
            like((NF, R, ZS * CX), f32),
            like((NF, R, ZS * CX), f32),
        ],
        scratch_shapes=[
            pltpu.VMEM((NF, ZS + 2 * R, CX, CY), f32),
            pltpu.SemaphoreType.DMA((NF,)),
        ],
        compiler_params=pltpu.CompilerParams(vmem_limit_bytes=49 << 20),
    )(fields)


def shards(fields, embed_weight, qkv_weight, out_weight, up_weight, down_weight):
    count = lax.axis_size("gy")
    smooth, upper, lower = prepare(fields)
    upper = lax.ppermute(upper, "gy", [(i, (i + 1) % count) for i in range(count)])
    lower = lax.ppermute(lower, "gy", [((i + 1) % count, i) for i in range(count)])
    along, weight = whole(
        band_kernel,
        [like((NF, ZS, CX, CY), f32), like((KIN, D))],
        [],
        2 * 5120 * 256 * 256 + 2 * KIN * 256 * D,
        8,
    )(smooth, embed_weight)
    slots = whole(
        embed_kernel,
        like((16 * SLOTS // 4, 4, D)),
        [
            pltpu.VMEM((NF, ZS, CX + 2 * PADX, CY), f32),
            pltpu.VMEM((NF, ZS, 80, CY), f32),
            pltpu.VMEM((ALL_ROWS, KIN), bf16),
            pltpu.VMEM((ALL_ROWS, D), f32),
            pltpu.VMEM((ALL_ROWS, D), bf16),
        ],
        2 * ALL_ROWS * KIN * D,
        18,
    )(along, upper, lower, side_table(), weight, message_order())
    slots = lax.all_to_all(
        slots.reshape(NXL, SLOTS // 4, 4, D), "gx", split_axis=0, concat_axis=0, tiled=True
    ).reshape(NXL * SLOTS // 4, 4, D)
    attention = [
        pltpu.VMEM((TOK, D), f32),
        pltpu.VMEM((TOK, 3 * D), bf16),
        pltpu.VMEM((TOK, D), bf16),
    ]
    tokens = whole(x_kernel, like((128, 2, D)), attention, 2 * TOK * D * 4 * D, 10)(
        slots, gather_sum(), qkv_weight, out_weight, interleave()
    )
    tokens = lax.all_to_all(
        tokens, ("gx", "gy"), split_axis=0, concat_axis=0, tiled=True
    )
    tokens = whole(
        y_kernel,
        like((TOK, D)),
        attention + [pltpu.VMEM((TOK, FF), bf16)],
        2 * TOK * D * (4 * D + 2 * FF),
        14,
    )(tokens, separate(), qkv_weight, out_weight, up_weight, down_weight, to_owners())
    tokens = lax.all_to_all(
        tokens.reshape(8, 32, D), "gy", split_axis=0, concat_axis=0, tiled=True
    ).reshape(TOK, D)
    tokens = whole(home_kernel, like((TOK, D)), [], 2 * TOK * TOK * D, 8)(tokens, to_home())
    return tokens.reshape(2, 16, 8, D)


def solution(mesh):
    return jax.shard_map(
        shards,
        mesh=mesh,
        in_specs=(P(None, None, "gx", "gy"), P(), P(), P(), P(), P()),
        out_specs=P(None, "gy", "gx", None),
        check_vma=False,
    )
```

```python
import functools

import jax
import jax.numpy as jnp
import ml_dtypes
import numpy as np
from jax import lax
from jax.experimental import pallas as pl
from jax.experimental.pallas import tpu as pltpu
from jax.sharding import PartitionSpec as P

R = 4
NF = 5
ZS = 16
CX = 64
CY = 128
D = 768
FF = 3072
KIN = 2560
PAIRS = 6
NXL = 16
TOK = 256
EXT = 10
SLOTS = 28
BOUND = (0, 1, 8, 9)
HI_ROWS = EXT * 32
ALL_ROWS = HI_ROWS + 128
PADX = 16
bf16 = jnp.bfloat16
f32 = jnp.float32


def np_taps():
    offsets = np.arange(-R, R + 1).astype(np.float32)
    values = np.exp(-offsets * offsets / np.float32(4.5)).astype(np.float32)
    return (values / values.sum(dtype=np.float32)).astype(np.float32)


TAPS = np_taps()


def as_bf16(values):
    return np.asarray(values, np.float32).astype(ml_dtypes.bfloat16)


def split_np(values):
    high = as_bf16(values)
    low = as_bf16(values - high.astype(np.float32))
    return high, low


def side_table():
    wide = np.zeros((CY + 2 * R, CY), np.float32)
    for out in range(CY):
        column = (out % 8) * 16 + out // 8
        for k in range(2 * R + 1):
            wide[out + k, column] = TAPS[k]
    high, low = split_np(np.concatenate([wide[:R], wide[R + CY :]], 0))
    return np.concatenate([high, high, low, np.zeros_like(high)], 0)


def band_table():
    row = lax.broadcasted_iota(jnp.int32, (CY, CY), 0)
    column = lax.broadcasted_iota(jnp.int32, (CY, CY), 1)
    apart = jnp.abs(row - ((column & 15) * 8 + (column >> 4)))
    high = jnp.zeros((CY, CY), f32)
    low = jnp.zeros((CY, CY), f32)
    for k in range(R + 1):
        tap_hi, tap_lo = split_np(TAPS[R + k])
        high = jnp.where(apart == k, float(tap_hi), high)
        low = jnp.where(apart == k, float(tap_lo), low)
    left = jnp.concatenate([high, high], 0)
    right = jnp.concatenate([low, jnp.zeros_like(low)], 0)
    return jnp.concatenate([left, right], 1).astype(bf16)


def strip_tables():
    inside = np.zeros((128, 128), np.float32)
    beyond = np.zeros((512, 128), np.float32)
    for x in range(CX):
        for k in range(-R, R + 1):
            if 0 <= x + k < CX:
                for z in range(2):
                    inside[z * 64 + x, z * 64 + x + k] = TAPS[R + k]
            else:
                place = x + k + 8 if x + k < 0 else x + k - 56
                for z in range(8):
                    beyond[z * 64 + x, z * 16 + place] = TAPS[R + k]
    tables = []
    for table in (inside, beyond):
        high, low = split_np(table)
        tables.append(np.concatenate([high, high, low], 0))
    return tables


def weight_order():
    row = lax.broadcasted_iota(jnp.int32, (256, 256), 0)
    column = lax.broadcasted_iota(jnp.int32, (256, 256), 1)
    return jnp.where(column == (row & 31) * 8 + (row >> 5), 1.0, 0.0).astype(bf16)


def permutation(rows, columns, source):
    table = np.zeros((rows, columns), np.float32)
    for row in range(rows):
        for column in source(row):
            table[row, column] = 1.0
    return as_bf16(table)


def message_order():
    return permutation(16 * SLOTS, ALL_ROWS, lambda r: [(r % SLOTS) * 16 + r // SLOTS])


def gather_sum():
    low = {ext: 2 * EXT + 2 * n for n, ext in enumerate(BOUND)}

    def source(row):
        a, i, c = row // 128, row // 8 % 16, row % 8
        found = [i * SLOTS + (c + 1) * 2 + a]
        if c == 0:
            left = (i - 1) % NXL * SLOTS
            found += [i * SLOTS + low[1] + a, left + 18 + a, left + low[9] + a]
        if c == 7:
            right = (i + 1) % NXL * SLOTS
            found += [i * SLOTS + low[8] + a, right + a, right + low[0] + a]
        return found

    return permutation(TOK, NXL * SLOTS, source)


def interleave():
    return permutation(TOK, TOK, lambda r: [(r % 2) * 128 + r // 2])


def separate():
    return permutation(TOK, TOK, lambda r: [(r % 128) * 2 + r // 128])


def to_owners():
    return permutation(TOK, TOK, lambda r: [(r // 16 % 2) * 128 + (r % 16) * 8 + r // 32])


def to_home():
    return permutation(TOK, TOK, lambda r: [(r % 8) * 32 + r // 8])


def dot(left, right):
    return lax.dot_general(left, right, (((1,), (0,)), ((), ())), preferred_element_type=f32)


def dot_split(left, table):
    high, low = halves(left)
    return dot(jnp.concatenate([high, low, high], 1), table)


def dot_t(left, right):
    return lax.dot_general(left, right, (((1,), (1,)), ((), ())), preferred_element_type=f32)


def halves(values):
    high = values.astype(bf16)
    return high, (values - high.astype(f32)).astype(bf16)


def prep_kernel(fields_ref, smooth_ref, upper_ref, lower_ref, cells, arrived):
    copies = [
        pltpu.make_async_copy(fields_ref.at[f], cells.at[f], arrived.at[f]) for f in range(NF)
    ]
    for copy in copies:
        copy.start()
    zero = jnp.zeros((NF, ZS, PADX, CY), f32)
    smooth_ref[:, :, 0:PADX] = zero
    smooth_ref[:, :, PADX + CX :] = zero
    for f in range(NF):
        copies[f].wait()
        for tile in range(CX // 8):
            rows = slice(tile * 8, tile * 8 + 8)
            plane = [cells[f, z, rows, :] for z in range(ZS + 2 * R)]
            for z in range(ZS):
                total = float(TAPS[R]) * plane[z + R]
                for k in range(1, R + 1):
                    total = total + float(TAPS[R + k]) * (plane[z + R - k] + plane[z + R + k])
                smooth_ref[f, z, PADX + tile * 8 : PADX + tile * 8 + 8, :] = total
        for pair in range(ZS // 2):
            block = smooth_ref[f, 2 * pair : 2 * pair + 2, PADX : PADX + CX]
            turned = block.reshape(128, 128).T
            lower_ref[f, :, pair * 128 : pair * 128 + 128] = turned[:R]
            upper_ref[f, :, pair * 128 : pair * 128 + 128] = turned[CY - R :]


def band_kernel(smooth_ref, weight_ref, along_ref, out_ref, across):
    band = band_table()
    order = weight_order()
    for f in range(NF):
        for z in range(ZS):
            total = float(TAPS[R]) * smooth_ref[f, z, PADX - 8 : PADX + 72, :]
            for k in range(1, R + 1):
                total = total + float(TAPS[R + k]) * (
                    smooth_ref[f, z, PADX - 8 - k : PADX + 72 - k, :]
                    + smooth_ref[f, z, PADX - 8 + k : PADX + 72 + k, :]
                )
            across[f, z] = total
        for part in range(4):
            planes = slice(part * 4, part * 4 + 4)
            high, low = halves(across[f, planes].reshape(320, CY))
            both = dot(jnp.concatenate([high, low], 1), band)
            along_ref[f, planes] = (both[:, :CY] + both[:, CY:]).reshape(4, 80, CY)
        for tile in (2 * f, 2 * f + 1):
            turned = dot(order, weight_ref[tile * 256 : tile * 256 + 256, :]).astype(bf16)
            for y in range(8):
                if tile < 8:
                    start = tile // 4 * 1024 + y * 128 + tile % 4 * 32
                else:
                    start = 2048 + y * 64 + (tile - 8) * 32
                out_ref[start : start + 32, :] = turned[y * 32 : y * 32 + 32]


def embed_kernel(
    along_ref,
    upper_ref,
    lower_ref,
    inside_ref,
    beyond_ref,
    side_ref,
    weight_ref,
    order_ref,
    out_ref,
    smooth,
    lhs,
    both,
    mid,
):
    side = side_ref[...]
    strips = [jnp.concatenate([upper_ref[f], lower_ref[f]], 0) for f in range(NF)]
    within = [strips[f][:, p * 128 : p * 128 + 128] for f in range(NF) for p in range(ZS // 2)]
    within = dot_split(jnp.concatenate(within, 0), inside_ref[...])
    ends = [strips[f][:, h * 512 : h * 512 + 512] for f in range(NF) for h in range(2)]
    ends = dot_split(jnp.concatenate(ends, 0), beyond_ref[...])
    lane = lax.broadcasted_iota(jnp.int32, (16, 128), 1)
    first = lane < 64

    def put(ext, a, start, values):
        high, low = halves(values)
        row = (ext * 2 + a) * 16
        lhs[row : row + 16, start : start + 128] = high
        if ext in BOUND:
            row = HI_ROWS + (BOUND.index(ext) * 2 + a) * 16
            lhs[row : row + 16, start : start + 128] = low

    for chunk, members in enumerate(((0, 1), (2, 3), (4,))):
        for f in members:
            parts = [within[(f * 8 + p) * 8 : (f * 8 + p) * 8 + 8] for p in range(ZS // 2)]
            parts += [ends[(f * 2 + h) * 8 : (f * 2 + h) * 8 + 8] for h in range(2)]
            cells = jnp.concatenate(parts, 1)
            high = cells.astype(bf16).astype(f32)
            stacked = jnp.concatenate([high, cells - high, high, jnp.zeros_like(high)], 0)
            added = dot(stacked.T.astype(bf16), side)
            middle = added[: ZS * CX].reshape(ZS, CX, CY)
            outer = added[ZS * CX :].reshape(ZS, 16, CY)
            smooth[f, :, 0:8] = along_ref[f, :, 0:8] + outer[:, :8]
            smooth[f, :, 8:72] = along_ref[f, :, 8:72] + middle
            smooth[f, :, 72:80] = along_ref[f, :, 72:80] + outer[:, 8:]
        for ext in range(EXT):
            rows = slice(ext * 8, ext * 8 + 8)
            if len(members) == 2:
                for a in range(2):
                    block = smooth[members[0] : members[0] + 2, a * 8 : a * 8 + 8, rows, :]
                    turned = block.reshape(128, 128).T
                    for y in range(8):
                        put(ext, a, chunk * 1024 + y * 128, turned[y * 16 : y * 16 + 16])
            else:
                turned = smooth[4, :, rows, :].reshape(128, 128).T
                for m in range(4):
                    even = turned[m * 32 : m * 32 + 16]
                    odd = turned[m * 32 + 16 : m * 32 + 32]
                    start = 2048 + m * 128
                    put(ext, 0, start, jnp.where(first, even, pltpu.roll(odd, 64, 1)))
                    put(ext, 1, start, jnp.where(first, pltpu.roll(even, 64, 1), odd))
        deep = slice(chunk * 1024, min(chunk * 1024 + 1024, KIN))
        for tile in range(3):
            columns = slice(tile * 256, tile * 256 + 256)
            part = dot(lhs[:, deep], weight_ref[deep, columns])
            both[:, columns] = part if chunk == 0 else both[:, columns] + part

    for tile in range(3):
        columns = slice(tile * 256, tile * 256 + 256)
        lead = both[:64, columns] + both[HI_ROWS : HI_ROWS + 64, columns]
        tail = both[256:HI_ROWS, columns] + both[HI_ROWS + 64 :, columns]
        lead_hi, lead_lo = halves(lead)
        tail_hi, tail_lo = halves(tail)
        mid[0:64, columns] = lead_hi
        mid[64:256, columns] = both[64:256, columns].astype(bf16)
        mid[256:HI_ROWS, columns] = tail_hi
        mid[HI_ROWS : HI_ROWS + 64, columns] = lead_lo
        mid[HI_ROWS + 64 :, columns] = tail_lo
    slots = dot(order_ref[...], mid[...]).astype(bf16)
    out_ref[...] = slots.reshape(16 * SLOTS // 4, 4, D)


def layer_norm(hidden):
    center = hidden - jnp.mean(hidden, axis=-1, keepdims=True)
    spread = jnp.mean(center * center, axis=-1, keepdims=True)
    return (center * lax.rsqrt(spread + 1e-05)).astype(bf16)


def attend(hidden, qkv_ref, out_ref, three, mixed):
    normed = layer_norm(hidden[...])
    for tile in range(9):
        columns = slice(tile * 256, tile * 256 + 256)
        three[:, columns] = dot(normed, qkv_ref[:, columns]).astype(bf16)
    first = lax.broadcasted_iota(jnp.int32, (128, 128), 1) < 64
    none = jnp.zeros((128, 128), bf16)
    for a in range(2):
        rows = slice(a * 128, a * 128 + 128)
        for pair in range(PAIRS):
            start = pair * 128
            query = three[rows, start : start + 128]
            keys = three[rows, D + start : D + start + 128]
            values = three[rows, 2 * D + start : 2 * D + start + 128]
            keys = jnp.concatenate([jnp.where(first, keys, none), jnp.where(first, none, keys)], 0)
            values = jnp.concatenate(
                [jnp.where(first, values, none), jnp.where(first, none, values)], 0
            )
            weights = jnp.exp(dot_t(query, keys) * 0.125)
            left, right = weights[:, :128], weights[:, 128:]
            left = left * (1.0 / jnp.sum(left, axis=-1, keepdims=True))
            right = right * (1.0 / jnp.sum(right, axis=-1, keepdims=True))
            weights = jnp.concatenate([left.astype(bf16), right.astype(bf16)], 1)
            mixed[rows, start : start + 128] = dot(weights, values).astype(bf16)
    for tile in range(3):
        columns = slice(tile * 256, tile * 256 + 256)
        branch = dot(mixed[...], out_ref[:, columns]).astype(bf16)
        hidden[:, columns] = hidden[:, columns] + branch.astype(f32)


def x_kernel(slots_ref, sum_ref, qkv_ref, outw_ref, order_ref, out_ref, hidden, three, mixed):
    hidden[...] = dot(sum_ref[...], slots_ref[...].reshape(NXL * SLOTS, D))
    attend(hidden, qkv_ref, outw_ref, three, mixed)
    tokens = dot(order_ref[...], hidden[...].astype(bf16)).astype(bf16)
    out_ref[...] = tokens.reshape(128, 2, D)


def y_kernel(
    tokens_ref,
    split_ref,
    qkv_ref,
    outw_ref,
    up_ref,
    down_ref,
    order_ref,
    out_ref,
    hidden,
    three,
    mixed,
    upper,
):
    hidden[...] = dot(split_ref[...], tokens_ref[...].reshape(TOK, D))
    attend(hidden, qkv_ref, outw_ref, three, mixed)
    normed = layer_norm(hidden[...])
    for tile in range(FF // 256):
        columns = slice(tile * 256, tile * 256 + 256)
        upper[:, columns] = jax.nn.gelu(dot(normed, up_ref[:, columns]), approximate=True).astype(bf16)
    for tile in range(3):
        columns = slice(tile * 256, tile * 256 + 256)
        total = hidden[:, columns] + dot(upper[...], down_ref[:, columns])
        out_ref[:, columns] = dot(order_ref[...], total.astype(bf16)).astype(bf16)


def home_kernel(tokens_ref, order_ref, out_ref):
    out_ref[...] = dot(order_ref[...], tokens_ref[...]).astype(bf16)


def whole(kernel, out_shape, scratch, flops, limit):
    space = pl.BlockSpec(memory_space=pltpu.VMEM)

    def call(*operands):
        size = sum(x.size * x.dtype.itemsize for x in operands)
        return pl.pallas_call(
            kernel,
            out_shape=out_shape,
            in_specs=[space] * len(operands),
            out_specs=[space] * len(out_shape) if isinstance(out_shape, list) else space,
            scratch_shapes=scratch,
            compiler_params=pltpu.CompilerParams(vmem_limit_bytes=limit << 20),
            cost_estimate=pl.CostEstimate(flops=flops, bytes_accessed=size, transcendentals=0),
        )(*operands)

    return call


def like(shape, kind=bf16):
    return jax.ShapeDtypeStruct(shape, kind)


def prepare(fields):
    space = pl.BlockSpec(memory_space=pltpu.VMEM)
    return pl.pallas_call(
        prep_kernel,
        in_specs=[pl.BlockSpec(memory_space=pltpu.HBM)],
        out_specs=[space] * 3,
        out_shape=[
            like((NF, ZS, CX + 2 * PADX, CY), f32),
            like((NF, R, ZS * CX), f32),
            like((NF, R, ZS * CX), f32),
        ],
        scratch_shapes=[
            pltpu.VMEM((NF, ZS + 2 * R, CX, CY), f32),
            pltpu.SemaphoreType.DMA((NF,)),
        ],
        compiler_params=pltpu.CompilerParams(vmem_limit_bytes=49 << 20),
    )(fields)


def shards(fields, embed_weight, qkv_weight, out_weight, up_weight, down_weight):
    count = lax.axis_size("gy")
    smooth, upper, lower = prepare(fields)
    upper = lax.ppermute(upper, "gy", [(i, (i + 1) % count) for i in range(count)])
    lower = lax.ppermute(lower, "gy", [((i + 1) % count, i) for i in range(count)])
    along, weight = whole(
        band_kernel,
        [like((NF, ZS, 80, CY), f32), like((KIN, D))],
        [pltpu.VMEM((NF, ZS, 80, CY), f32)],
        2 * 6400 * 256 * 256 + 2 * KIN * 256 * D,
        8,
    )(smooth, embed_weight)
    slots = whole(
        embed_kernel,
        like((16 * SLOTS // 4, 4, D)),
        [
            pltpu.VMEM((NF, ZS, 80, CY), f32),
            pltpu.VMEM((ALL_ROWS, KIN), bf16),
            pltpu.VMEM((ALL_ROWS, D), f32),
            pltpu.VMEM((ALL_ROWS, D), bf16),
        ],
        2 * ALL_ROWS * KIN * D,
        14,
    )(along, upper, lower, *strip_tables(), side_table(), weight, message_order())
    slots = lax.all_to_all(
        slots.reshape(NXL, SLOTS // 4, 4, D), "gx", split_axis=0, concat_axis=0, tiled=True
    ).reshape(NXL * SLOTS // 4, 4, D)
    attention = [
        pltpu.VMEM((TOK, D), f32),
        pltpu.VMEM((TOK, 3 * D), bf16),
        pltpu.VMEM((TOK, D), bf16),
    ]
    tokens = whole(x_kernel, like((128, 2, D)), attention, 2 * TOK * D * 4 * D, 10)(
        slots, gather_sum(), qkv_weight, out_weight, interleave()
    )
    tokens = lax.all_to_all(
        tokens, ("gx", "gy"), split_axis=0, concat_axis=0, tiled=True
    )
    tokens = whole(
        y_kernel,
        like((TOK, D)),
        attention + [pltpu.VMEM((TOK, FF), bf16)],
        2 * TOK * D * (4 * D + 2 * FF),
        14,
    )(tokens, separate(), qkv_weight, out_weight, up_weight, down_weight, to_owners())
    tokens = lax.all_to_all(
        tokens.reshape(8, 32, D), "gy", split_axis=0, concat_axis=0, tiled=True
    ).reshape(TOK, D)
    tokens = whole(home_kernel, like((TOK, D)), [], 2 * TOK * TOK * D, 8)(tokens, to_home())
    return tokens.reshape(2, 16, 8, D)


def solution(mesh):
    return jax.shard_map(
        shards,
        mesh=mesh,
        in_specs=(P(None, None, "gx", "gy"), P(), P(), P(), P(), P()),
        out_specs=P(None, "gy", "gx", None),
        check_vma=False,
    )
```

```python
import functools

import jax
import jax.numpy as jnp
import ml_dtypes
import numpy as np
from jax import lax
from jax.experimental import pallas as pl
from jax.experimental.pallas import tpu as pltpu
from jax.sharding import PartitionSpec as P

R = 4
NF = 5
ZS = 16
CX = 64
CY = 128
D = 768
FF = 3072
KIN = 2560
PAIRS = 6
NXL = 16
TOK = 256
EXT = 10
SLOTS = 28
BOUND = (0, 1, 8, 9)
HI_ROWS = EXT * 32
ALL_ROWS = HI_ROWS + 128
PADX = 16
bf16 = jnp.bfloat16
f32 = jnp.float32


def np_taps():
    offsets = np.arange(-R, R + 1).astype(np.float32)
    values = np.exp(-offsets * offsets / np.float32(4.5)).astype(np.float32)
    return (values / values.sum(dtype=np.float32)).astype(np.float32)


TAPS = np_taps()


def as_bf16(values):
    return np.asarray(values, np.float32).astype(ml_dtypes.bfloat16)


def split_np(values):
    high = as_bf16(values)
    low = as_bf16(values - high.astype(np.float32))
    return high, low


def band_table():
    row = lax.broadcasted_iota(jnp.int32, (CY, CY), 0)
    column = lax.broadcasted_iota(jnp.int32, (CY, CY), 1)
    apart = jnp.abs(row - ((column & 15) * 8 + (column >> 4)))
    high = jnp.zeros((CY, CY), f32)
    low = jnp.zeros((CY, CY), f32)
    for k in range(R + 1):
        tap_hi, tap_lo = split_np(TAPS[R + k])
        high = jnp.where(apart == k, float(tap_hi), high)
        low = jnp.where(apart == k, float(tap_lo), low)
    left = jnp.concatenate([high, high], 0)
    right = jnp.concatenate([low, jnp.zeros_like(low)], 0)
    return jnp.concatenate([left, right], 1).astype(bf16)


def strip_table():
    table = np.zeros((384, 128), np.float32)
    for group in range(16):
        for x in range(8):
            for k in range(-R, R + 1):
                source = x + k + 8
                table[source // 8 * 128 + group * 8 + source % 8, group * 8 + x] = TAPS[R + k]
    high, low = split_np(table)
    return np.concatenate([high, high, low], 0)


def weight_order():
    row = lax.broadcasted_iota(jnp.int32, (256, 256), 0)
    column = lax.broadcasted_iota(jnp.int32, (256, 256), 1)
    return jnp.where(column == (row & 31) * 8 + (row >> 5), 1.0, 0.0).astype(bf16)


def permutation(rows, columns, source):
    table = np.zeros((rows, columns), np.float32)
    for row in range(rows):
        for column in source(row):
            table[row, column] = 1.0
    return as_bf16(table)


def message_order():
    return permutation(16 * SLOTS, ALL_ROWS, lambda r: [(r % SLOTS) * 16 + r // SLOTS])


def gather_sum():
    low = {ext: 2 * EXT + 2 * n for n, ext in enumerate(BOUND)}

    def source(row):
        a, i, c = row // 16 % 2, row // 32 * 2 + row // 8 % 2, row % 8
        found = [i * SLOTS + (c + 1) * 2 + a]
        if c == 0:
            left = (i - 1) % NXL * SLOTS
            found += [i * SLOTS + low[1] + a, left + 18 + a, left + low[9] + a]
        if c == 7:
            right = (i + 1) % NXL * SLOTS
            found += [i * SLOTS + low[8] + a, right + a, right + low[0] + a]
        return found

    return permutation(TOK, NXL * SLOTS, source)


def interleave():
    return permutation(TOK, TOK, lambda r: [r // 32 * 32 + r % 2 * 16 + r // 2 % 16])


def separate():
    return permutation(TOK, TOK, lambda r: [((r % 16) * 8 + r // 32) * 2 + r // 16 % 2])


def to_home():
    return permutation(TOK, TOK, lambda r: [(r % 8) * 32 + r // 8])


def dot(left, right):
    return lax.dot_general(left, right, (((1,), (0,)), ((), ())), preferred_element_type=f32)


def dot_split(left, table):
    high, low = halves(left)
    return dot(jnp.concatenate([high, low, high], 1), table)


def dot_t(left, right):
    return lax.dot_general(left, right, (((1,), (1,)), ((), ())), preferred_element_type=f32)


def halves(values):
    high = values.astype(bf16)
    return high, (values - high.astype(f32)).astype(bf16)


def prep_kernel(fields_ref, smooth_ref, upper_ref, lower_ref, cells, arrived):
    copies = [
        pltpu.make_async_copy(fields_ref.at[f], cells.at[f], arrived.at[f]) for f in range(NF)
    ]
    for copy in copies:
        copy.start()
    zero = jnp.zeros((NF, ZS, PADX, CY), f32)
    smooth_ref[:, :, 0:PADX] = zero
    smooth_ref[:, :, PADX + CX :] = zero

    def strip(index, block):
        turned = block.reshape(128, 128).T
        lower_ref[index] = turned[:R]
        upper_ref[index] = turned[CY - R :]

    for f in range(NF):
        copies[f].wait()
        for tile in range(CX // 8):
            rows = slice(tile * 8, tile * 8 + 8)
            plane = [cells[f, z, rows, :] for z in range(ZS + 2 * R)]
            for z in range(ZS):
                total = float(TAPS[R]) * plane[z + R]
                for k in range(1, R + 1):
                    total = total + float(TAPS[R + k]) * (plane[z + R - k] + plane[z + R + k])
                smooth_ref[f, z, PADX + tile * 8 : PADX + tile * 8 + 8, :] = total
        if f % 2 == 1:
            for a in range(2):
                for c in range(8):
                    rows = slice(PADX + c * 8, PADX + c * 8 + 8)
                    block = smooth_ref[f - 1 : f + 1, a * 8 : a * 8 + 8, rows, :]
                    strip((f // 2 * 2 + a) * 8 + c, block)
    for c in range(8):
        strip(32 + c, smooth_ref[NF - 1, :, PADX + c * 8 : PADX + c * 8 + 8, :])


def main_kernel(smooth_ref, weight_ref, total_ref, edge_ref, order_ref, across, along, lhs, both):
    band = band_table()
    order = weight_order()
    first = lax.broadcasted_iota(jnp.int32, (16, 128), 1) < 64
    edge_ref[...] = jnp.zeros_like(edge_ref)

    def filtered(f):
        for z in range(ZS):
            total = float(TAPS[R]) * smooth_ref[f, z, PADX - 8 : PADX + 72, :]
            for k in range(1, R + 1):
                total = total + float(TAPS[R + k]) * (
                    smooth_ref[f, z, PADX - 8 - k : PADX + 72 - k, :]
                    + smooth_ref[f, z, PADX - 8 + k : PADX + 72 + k, :]
                )
            across[f, z] = total
        for part in range(4):
            planes = slice(part * 4, part * 4 + 4)
            high, low = halves(across[f, planes].reshape(320, CY))
            pair = dot(jnp.concatenate([high, low], 1), band)
            along[f, planes] = (pair[:, :CY] + pair[:, CY:]).reshape(4, 80, CY)

    def reordered(f):
        for tile in (2 * f, 2 * f + 1):
            turned = dot(order, weight_ref[tile * 256 : tile * 256 + 256, :]).astype(bf16)
            for y in range(8):
                if tile < 8:
                    start = tile // 4 * 1024 + y * 128 + tile % 4 * 32
                else:
                    start = 2048 + y * 64 + (tile - 8) * 32
                order_ref[start : start + 32, :] = turned[y * 32 : y * 32 + 32]

    def put(ext, a, start, side, place, values):
        high = values.astype(bf16)
        rest = values - high.astype(f32)
        row = (ext * 2 + a) * 16
        lhs[row : row + 16, start : start + 128] = high
        if ext in BOUND:
            row = HI_ROWS + (BOUND.index(ext) * 2 + a) * 16
            lhs[row : row + 16, start : start + 128] = rest.astype(bf16)
        else:
            row = a * 16 + ext
            edge_ref[side, row : row + 1, place : place + 128] = rest[side * 15 : side * 15 + 1]

    for chunk, members in enumerate(((0, 1), (2, 3), (4,))):
        for f in members:
            filtered(f)
            reordered(f)
        for ext in range(EXT):
            rows = slice(ext * 8, ext * 8 + 8)
            if len(members) == 2:
                for a in range(2):
                    block = along[members[0] : members[0] + 2, a * 8 : a * 8 + 8, rows, :]
                    turned = block.reshape(128, 128).T
                    for y in range(8):
                        values = turned[y * 16 : y * 16 + 16]
                        start = chunk * 1024 + y * 128
                        put(ext, a, start, y // 4, chunk * 512 + y % 4 * 128, values)
            else:
                turned = along[4, :, rows, :].reshape(128, 128).T
                for m in range(4):
                    even = turned[m * 32 : m * 32 + 16]
                    odd = turned[m * 32 + 16 : m * 32 + 32]
                    start, place = 2048 + m * 128, 1024 + m % 2 * 128
                    put(ext, 0, start, m // 2, place, jnp.where(first, even, pltpu.roll(odd, 64, 1)))
                    put(ext, 1, start, m // 2, place, jnp.where(first, pltpu.roll(even, 64, 1), odd))
        deep = slice(chunk * 1024, min(chunk * 1024 + 1024, KIN))
        for tile in range(3):
            columns = slice(tile * 256, tile * 256 + 256)
            part = dot(lhs[:, deep], order_ref[deep, columns])
            if chunk < 2:
                both[:, columns] = part if chunk == 0 else both[:, columns] + part
            else:
                part = both[:, columns] + part
                total_ref[0:64, columns] = part[:64] + part[HI_ROWS : HI_ROWS + 64]
                total_ref[64:256, columns] = part[64:256]
                total_ref[256:HI_ROWS, columns] = part[256:HI_ROWS] + part[HI_ROWS + 64 :]


def edge_kernel(
    upper_ref,
    lower_ref,
    table_ref,
    edge_ref,
    total_ref,
    weight_ref,
    order_ref,
    out_ref,
    parts,
    mixed,
    lhs,
    mid,
):
    cells = jnp.concatenate([upper_ref[...], lower_ref[...]], 1).reshape(320, 128)
    place = lax.broadcasted_iota(jnp.int32, (320, 128), 0) & 7
    sums = jnp.zeros((320, 128), f32)
    for m in range(R):
        ahead = cells if m == 0 else pltpu.roll(cells, 320 - m, 0)
        behind = cells if m == 0 else pltpu.roll(cells, m, 0)
        used = jnp.where(place < R - m, ahead, jnp.where(place >= R + m, behind, 0.0))
        sums = sums + float(TAPS[2 * R - m]) * used
    none = jnp.zeros((16, 128), f32)
    blocks = []
    for group in range(5):
        tiles = sums[group * 64 : group * 64 + 64]
        blocks.append(
            jnp.concatenate(
                [
                    jnp.concatenate([none, tiles], 0),
                    jnp.concatenate([none[:8], tiles, none[:8]], 0),
                    jnp.concatenate([tiles, none], 0),
                ],
                1,
            )
        )
    high, low = halves(jnp.concatenate(blocks, 0))
    parts[...] = dot(jnp.concatenate([high, low, high], 1), table_ref[...])
    last = parts[320:]
    first = lax.broadcasted_iota(jnp.int32, (80, 128), 1) < 64
    rolled = pltpu.roll(last, 64, 1)
    mixed[0:80] = jnp.where(first, last, pltpu.roll(rolled, 79, 0))
    mixed[80:160] = jnp.where(first, rolled, pltpu.roll(last, 79, 0))
    lhs[...] = edge_ref[...]
    for side in range(2):
        for a in range(2):
            rows = slice(a * 16, a * 16 + EXT)
            for pair in range(2):
                for q in range(4):
                    columns = slice(pair * 512 + q * 128, pair * 512 + q * 128 + 128)
                    found = parts[pl.ds((pair * 2 + a) * 80 + side * 4 + q, EXT, stride=8), :]
                    lhs[side, rows, columns] += found
            for q in range(2):
                columns = slice(1024 + q * 128, 1024 + q * 128 + 128)
                found = mixed[pl.ds(a * 80 + side * 4 + q * 2, EXT, stride=8), :]
                lhs[side, rows, columns] += found
    added = []
    for side in range(2):
        high, low = halves(lhs[side])
        values = jnp.concatenate([high, low], 0)
        result = dot(values[:, :512], weight_ref[side * 512 : side * 512 + 512, :])
        result = result + dot(values[:, 512:1024], weight_ref[1024 + side * 512 : 1536 + side * 512, :])
        result = result + dot(values[:, 1024:], weight_ref[2048 + side * 256 : 2304 + side * 256, :])
        added.append(result[:32] + result[32:])
    patch = lax.broadcasted_iota(jnp.int32, (16, D), 0)
    for ext in range(EXT):
        for a in range(2):
            row = (ext * 2 + a) * 16
            near = a * 16 + ext
            values = total_ref[row : row + 16]
            values = values + jnp.where(patch == 0, added[0][near : near + 1], 0.0)
            values = values + jnp.where(patch == 15, added[1][near : near + 1], 0.0)
            high, low = halves(values)
            mid[row : row + 16] = high
            if ext in BOUND:
                row = HI_ROWS + (BOUND.index(ext) * 2 + a) * 16
                mid[row : row + 16] = low
    slots = dot(order_ref[...], mid[...]).astype(bf16)
    out_ref[...] = slots.reshape(16 * SLOTS // 4, 4, D)


def layer_norm(hidden):
    center = hidden - jnp.mean(hidden, axis=-1, keepdims=True)
    spread = jnp.mean(center * center, axis=-1, keepdims=True)
    return (center * lax.rsqrt(spread + 1e-05)).astype(bf16)


def attend(hidden, qkv_ref, out_ref, three, mixed):
    normed = layer_norm(hidden[...])
    for tile in range(9):
        columns = slice(tile * 256, tile * 256 + 256)
        three[:, columns] = dot(normed, qkv_ref[:, columns]).astype(bf16)
    first = lax.broadcasted_iota(jnp.int32, (128, 128), 1) < 64
    none = jnp.zeros((128, 128), bf16)
    for a in range(2):
        groups = [slice(g * 32 + a * 16, g * 32 + a * 16 + 16) for g in range(8)]
        for pair in range(PAIRS):
            start = pair * 128
            query, keys, values = [
                jnp.concatenate([three[rows, D * n + start : D * n + start + 128] for rows in groups], 0)
                for n in range(3)
            ]
            keys = jnp.concatenate([jnp.where(first, keys, none), jnp.where(first, none, keys)], 0)
            values = jnp.concatenate(
                [jnp.where(first, values, none), jnp.where(first, none, values)], 0
            )
            weights = jnp.exp(dot_t(query, keys) * 0.125)
            left, right = weights[:, :128], weights[:, 128:]
            left = left * (1.0 / jnp.sum(left, axis=-1, keepdims=True))
            right = right * (1.0 / jnp.sum(right, axis=-1, keepdims=True))
            weights = jnp.concatenate([left.astype(bf16), right.astype(bf16)], 1)
            result = dot(weights, values).astype(bf16)
            for g, rows in enumerate(groups):
                mixed[rows, start : start + 128] = result[g * 16 : g * 16 + 16]
    for tile in range(3):
        columns = slice(tile * 256, tile * 256 + 256)
        branch = dot(mixed[...], out_ref[:, columns]).astype(bf16)
        hidden[:, columns] = hidden[:, columns] + branch.astype(f32)


def x_kernel(slots_ref, sum_ref, qkv_ref, outw_ref, order_ref, out_ref, hidden, three, mixed):
    hidden[...] = dot(sum_ref[...], slots_ref[...].reshape(NXL * SLOTS, D))
    attend(hidden, qkv_ref, outw_ref, three, mixed)
    tokens = dot(order_ref[...], hidden[...].astype(bf16)).astype(bf16)
    out_ref[...] = tokens.reshape(128, 2, D)


def y_kernel(
    tokens_ref,
    split_ref,
    qkv_ref,
    outw_ref,
    up_ref,
    down_ref,
    out_ref,
    hidden,
    three,
    mixed,
    upper,
):
    hidden[...] = dot(split_ref[...], tokens_ref[...].reshape(TOK, D))
    attend(hidden, qkv_ref, outw_ref, three, mixed)
    normed = layer_norm(hidden[...])
    for tile in range(FF // 256):
        columns = slice(tile * 256, tile * 256 + 256)
        upper[:, columns] = jax.nn.gelu(dot(normed, up_ref[:, columns]), approximate=True).astype(bf16)
    for tile in range(3):
        columns = slice(tile * 256, tile * 256 + 256)
        total = hidden[:, columns] + dot(upper[...], down_ref[:, columns])
        out_ref[:, columns] = total.astype(bf16)


def home_kernel(tokens_ref, order_ref, out_ref):
    out_ref[...] = dot(order_ref[...], tokens_ref[...]).astype(bf16)


def whole(kernel, out_shape, scratch, flops, limit):
    space = pl.BlockSpec(memory_space=pltpu.VMEM)

    def call(*operands):
        size = sum(x.size * x.dtype.itemsize for x in operands)
        return pl.pallas_call(
            kernel,
            out_shape=out_shape,
            in_specs=[space] * len(operands),
            out_specs=[space] * len(out_shape) if isinstance(out_shape, list) else space,
            scratch_shapes=scratch,
            compiler_params=pltpu.CompilerParams(vmem_limit_bytes=limit << 20),
            cost_estimate=pl.CostEstimate(flops=flops, bytes_accessed=size, transcendentals=0),
        )(*operands)

    return call


def like(shape, kind=bf16):
    return jax.ShapeDtypeStruct(shape, kind)


def prepare(fields):
    space = pl.BlockSpec(memory_space=pltpu.VMEM)
    return pl.pallas_call(
        prep_kernel,
        in_specs=[pl.BlockSpec(memory_space=pltpu.HBM)],
        out_specs=[space] * 3,
        out_shape=[
            like((NF, ZS, CX + 2 * PADX, CY), f32),
            like((40, R, 128), f32),
            like((40, R, 128), f32),
        ],
        scratch_shapes=[
            pltpu.VMEM((NF, ZS + 2 * R, CX, CY), f32),
            pltpu.SemaphoreType.DMA((NF,)),
        ],
        compiler_params=pltpu.CompilerParams(vmem_limit_bytes=49 << 20),
    )(fields)


def shards(fields, embed_weight, qkv_weight, out_weight, up_weight, down_weight):
    count = lax.axis_size("gy")
    smooth, upper, lower = prepare(fields)
    upper = lax.ppermute(upper, "gy", [(i, (i + 1) % count) for i in range(count)])
    lower = lax.ppermute(lower, "gy", [((i + 1) % count, i) for i in range(count)])
    total, edge, weight = whole(
        main_kernel,
        [like((HI_ROWS, D), f32), like((2, 32, KIN // 2), f32), like((KIN, D))],
        [
            pltpu.VMEM((NF, ZS, 80, CY), f32),
            pltpu.VMEM((NF, ZS, 80, CY), f32),
            pltpu.VMEM((ALL_ROWS, KIN), bf16),
            pltpu.VMEM((ALL_ROWS, D), f32),
        ],
        2 * 6400 * 256 * 256 + 2 * KIN * 256 * D + 2 * ALL_ROWS * KIN * D,
        16,
    )(smooth, embed_weight)
    slots = whole(
        edge_kernel,
        like((16 * SLOTS // 4, 4, D)),
        [
            pltpu.VMEM((400, 128), f32),
            pltpu.VMEM((160, 128), f32),
            pltpu.VMEM((2, 32, KIN // 2), f32),
            pltpu.VMEM((ALL_ROWS, D), bf16),
        ],
        2 * 64 * KIN * D,
        8,
    )(upper, lower, strip_table(), edge, total, weight, message_order())
    slots = lax.all_to_all(
        slots.reshape(NXL, SLOTS // 4, 4, D), "gx", split_axis=0, concat_axis=0, tiled=True
    ).reshape(NXL * SLOTS // 4, 4, D)
    attention = [
        pltpu.VMEM((TOK, D), f32),
        pltpu.VMEM((TOK, 3 * D), bf16),
        pltpu.VMEM((TOK, D), bf16),
    ]
    tokens = whole(x_kernel, like((128, 2, D)), attention, 2 * TOK * D * 4 * D, 10)(
        slots, gather_sum(), qkv_weight, out_weight, interleave()
    )
    tokens = lax.all_to_all(
        tokens, ("gx", "gy"), split_axis=0, concat_axis=0, tiled=True
    )
    tokens = whole(
        y_kernel,
        like((TOK, D)),
        attention + [pltpu.VMEM((TOK, FF), bf16)],
        2 * TOK * D * (4 * D + 2 * FF),
        14,
    )(tokens, separate(), qkv_weight, out_weight, up_weight, down_weight)
    tokens = lax.all_to_all(
        tokens.reshape(8, 32, D), "gy", split_axis=0, concat_axis=0, tiled=True
    ).reshape(TOK, D)
    tokens = whole(home_kernel, like((TOK, D)), [], 2 * TOK * TOK * D, 8)(tokens, to_home())
    return tokens.reshape(2, 16, 8, D)


def solution(mesh):
    return jax.shard_map(
        shards,
        mesh=mesh,
        in_specs=(P(None, None, "gx", "gy"), P(), P(), P(), P(), P()),
        out_specs=P(None, "gy", "gx", None),
        check_vma=False,
    )
```

```python
import functools

import jax
import jax.numpy as jnp
import ml_dtypes
import numpy as np
from jax import lax
from jax.experimental import pallas as pl
from jax.experimental.pallas import tpu as pltpu
from jax.sharding import PartitionSpec as P

R = 4
NF = 5
ZS = 16
CX = 64
CY = 128
D = 768
FF = 3072
KIN = 2560
PAIRS = 6
NXL = 16
TOK = 256
EXT = 10
SLOTS = 28
BOUND = (0, 1, 8, 9)
HI_ROWS = EXT * 32
ALL_ROWS = HI_ROWS + 128
PADX = 16
SHRINK = 2.0**15
bf16 = jnp.bfloat16
f32 = jnp.float32


def np_taps():
    offsets = np.arange(-R, R + 1).astype(np.float32)
    values = np.exp(-offsets * offsets / np.float32(4.5)).astype(np.float32)
    return (values / values.sum(dtype=np.float32)).astype(np.float32)


TAPS = np_taps()


def as_bf16(values):
    return np.asarray(values, np.float32).astype(ml_dtypes.bfloat16)


def split_np(values):
    high = as_bf16(values)
    low = as_bf16(values - high.astype(np.float32))
    return high, low


def band_table():
    row = lax.broadcasted_iota(jnp.int32, (CY, CY), 0)
    column = lax.broadcasted_iota(jnp.int32, (CY, CY), 1)
    apart = jnp.abs(row - ((column & 15) * 8 + (column >> 4)))
    high = jnp.zeros((CY, CY), f32)
    low = jnp.zeros((CY, CY), f32)
    for k in range(R + 1):
        tap_hi, tap_lo = split_np(TAPS[R + k])
        high = jnp.where(apart == k, float(tap_hi), high)
        low = jnp.where(apart == k, float(tap_lo), low)
    left = jnp.concatenate([high, high], 0)
    right = jnp.concatenate([low, jnp.zeros_like(low)], 0)
    return jnp.concatenate([left, right], 1).astype(bf16)


def strip_table():
    table = np.zeros((384, 128), np.float32)
    for group in range(16):
        for x in range(8):
            for k in range(-R, R + 1):
                source = x + k + 8
                table[source // 8 * 128 + group * 8 + source % 8, group * 8 + x] = TAPS[R + k]
    high, low = split_np(table)
    return np.concatenate([high, high, low], 0)


def weight_order():
    row = lax.broadcasted_iota(jnp.int32, (256, 256), 0)
    column = lax.broadcasted_iota(jnp.int32, (256, 256), 1)
    return jnp.where(column == (row & 31) * 8 + (row >> 5), 1.0, 0.0).astype(bf16)


def permutation(rows, columns, source):
    table = np.zeros((rows, columns), np.float32)
    for row in range(rows):
        for column in source(row):
            table[row, column] = 1.0
    return as_bf16(table)


def message_order():
    row = lax.broadcasted_iota(jnp.int32, (ALL_ROWS, ALL_ROWS), 0)
    column = lax.broadcasted_iota(jnp.int32, (ALL_ROWS, ALL_ROWS), 1)
    slot, line = column >> 4, column & 15
    return jnp.where(row == line * SLOTS + slot, 1.0, 0.0).astype(bf16)


def gather_sum():
    low = {ext: 2 * EXT + 2 * n for n, ext in enumerate(BOUND)}

    def source(row):
        a, i, c = row // 16 % 2, row // 32 * 2 + row // 8 % 2, row % 8
        found = [i * SLOTS + (c + 1) * 2 + a]
        if c == 0:
            left = (i - 1) % NXL * SLOTS
            found += [i * SLOTS + low[1] + a, left + 18 + a, left + low[9] + a]
        if c == 7:
            right = (i + 1) % NXL * SLOTS
            found += [i * SLOTS + low[8] + a, right + a, right + low[0] + a]
        return found

    return permutation(TOK, NXL * SLOTS, source)


def interleave():
    return permutation(TOK, TOK, lambda r: [r // 32 * 32 + r % 2 * 16 + r // 2 % 16])


def separate():
    return permutation(TOK, TOK, lambda r: [((r % 16) * 8 + r // 32) * 2 + r // 16 % 2])


def to_home():
    return permutation(TOK, TOK, lambda r: [(r % 8) * 32 + r // 8])


def dot(left, right):
    return lax.dot_general(left, right, (((1,), (0,)), ((), ())), preferred_element_type=f32)


def dot_split(left, table):
    high, low = halves(left)
    return dot(jnp.concatenate([high, low, high], 1), table)


def dot_t(left, right):
    return lax.dot_general(left, right, (((1,), (1,)), ((), ())), preferred_element_type=f32)


def halves(values):
    high = values.astype(bf16)
    return high, (values - high.astype(f32)).astype(bf16)


def prep_kernel(fields_ref, smooth_ref, upper_ref, lower_ref, cells, arrived):
    copies = [
        pltpu.make_async_copy(fields_ref.at[f], cells.at[f], arrived.at[f]) for f in range(NF)
    ]
    for copy in copies:
        copy.start()
    zero = jnp.zeros((NF, ZS, PADX, CY), f32)
    smooth_ref[:, :, 0:PADX] = zero
    smooth_ref[:, :, PADX + CX :] = zero

    def strip(index, block):
        turned = block.reshape(128, 128).T
        lower_ref[index] = turned[:R]
        upper_ref[index] = turned[CY - R :]

    for f in range(NF):
        copies[f].wait()
        for tile in range(CX // 8):
            rows = slice(tile * 8, tile * 8 + 8)
            plane = [cells[f, z, rows, :] for z in range(ZS + 2 * R)]
            for z in range(ZS):
                total = float(TAPS[R]) * plane[z + R]
                for k in range(1, R + 1):
                    total = total + float(TAPS[R + k]) * (plane[z + R - k] + plane[z + R + k])
                smooth_ref[f, z, PADX + tile * 8 : PADX + tile * 8 + 8, :] = total
        if f % 2 == 1:
            for a in range(2):
                for c in range(8):
                    rows = slice(PADX + c * 8, PADX + c * 8 + 8)
                    block = smooth_ref[f - 1 : f + 1, a * 8 : a * 8 + 8, rows, :]
                    strip((f // 2 * 2 + a) * 8 + c, block)
    for c in range(8):
        strip(32 + c, smooth_ref[NF - 1, :, PADX + c * 8 : PADX + c * 8 + 8, :])


def main_kernel(
    smooth_ref,
    weight_ref,
    out_ref,
    base_ref,
    edge_ref,
    order_ref,
    across,
    along,
    lhs,
    both,
    sums,
    mid,
):
    band = band_table()
    order = weight_order()
    first = lax.broadcasted_iota(jnp.int32, (16, 128), 1) < 64
    edge_ref[...] = jnp.zeros_like(edge_ref)

    def filtered(f):
        for z in range(ZS):
            total = float(TAPS[R]) * smooth_ref[f, z, PADX - 8 : PADX + 72, :]
            for k in range(1, R + 1):
                total = total + float(TAPS[R + k]) * (
                    smooth_ref[f, z, PADX - 8 - k : PADX + 72 - k, :]
                    + smooth_ref[f, z, PADX - 8 + k : PADX + 72 + k, :]
                )
            across[f, z] = total
        for part in range(4):
            planes = slice(part * 4, part * 4 + 4)
            high, low = halves(across[f, planes].reshape(320, CY))
            pair = dot(jnp.concatenate([high, low], 1), band)
            along[f, planes] = (pair[:, :CY] + pair[:, CY:]).reshape(4, 80, CY)

    def reordered(f):
        for tile in (2 * f, 2 * f + 1):
            turned = dot(order, weight_ref[tile * 256 : tile * 256 + 256, :]).astype(bf16)
            for y in range(8):
                if tile < 8:
                    start = tile // 4 * 1024 + y * 128 + tile % 4 * 32
                else:
                    start = 2048 + y * 64 + (tile - 8) * 32
                order_ref[start : start + 32, :] = turned[y * 32 : y * 32 + 32]

    def put(ext, a, start, side, place, values):
        high = values.astype(bf16)
        rest = values - high.astype(f32)
        row = (ext * 2 + a) * 16
        lhs[row : row + 16, start : start + 128] = high
        if ext in BOUND:
            row = HI_ROWS + (BOUND.index(ext) * 2 + a) * 16
            lhs[row : row + 16, start : start + 128] = rest.astype(bf16)
        else:
            row = ext * 2 + a
            edge_ref[side * 10 + place, row : row + 1, :] = rest[side * 15 : side * 15 + 1]

    for chunk, members in enumerate(((0, 1), (2, 3), (4,))):
        for f in members:
            filtered(f)
            reordered(f)
        for ext in range(EXT):
            rows = slice(ext * 8, ext * 8 + 8)
            if len(members) == 2:
                for a in range(2):
                    block = along[members[0] : members[0] + 2, a * 8 : a * 8 + 8, rows, :]
                    turned = block.reshape(128, 128).T
                    for y in range(8):
                        values = turned[y * 16 : y * 16 + 16]
                        start = chunk * 1024 + y * 128
                        put(ext, a, start, y // 4, chunk * 4 + y % 4, values)
            else:
                turned = along[4, :, rows, :].reshape(128, 128).T
                for m in range(4):
                    even = turned[m * 32 : m * 32 + 16]
                    odd = turned[m * 32 + 16 : m * 32 + 32]
                    start, place = 2048 + m * 128, 8 + m % 2
                    put(ext, 0, start, m // 2, place, jnp.where(first, even, pltpu.roll(odd, 64, 1)))
                    put(ext, 1, start, m // 2, place, jnp.where(first, pltpu.roll(even, 64, 1), odd))
        deep = slice(chunk * 1024, min(chunk * 1024 + 1024, KIN))
        for tile in range(3):
            columns = slice(tile * 256, tile * 256 + 256)
            part = dot(lhs[:, deep], order_ref[deep, columns])
            both[:, columns] = part if chunk == 0 else both[:, columns] + part
    for tile in range(6):
        columns = slice(tile * 128, tile * 128 + 128)
        for start, low in ((0, HI_ROWS), (256, HI_ROWS + 64)):
            rows, rest = slice(start, start + 64), slice(low, low + 64)
            total = both[rows, columns] + both[rest, columns]
            sums[tile, rows] = total
            mid[rows, columns], mid[rest, columns] = halves(total)
        total = both[64:256, columns]
        sums[tile, 64:256] = total
        mid[64:256, columns] = total.astype(bf16)
        for side in range(2):
            base_ref[side, 0 : 2 * EXT, columns] = sums[tile, pl.ds(side * 15, 2 * EXT, stride=16), :]
            base_ref[side, 2 * EXT :, columns] = jnp.zeros((4, 128), f32)
    slots = dot(message_order(), mid[...]).astype(bf16)
    out_ref[...] = slots.reshape(16 * SLOTS // 4, 4, D)


def edge_kernel(
    upper_ref,
    lower_ref,
    table_ref,
    edge_ref,
    base_ref,
    weight_ref,
    slots_ref,
    out_ref,
    parts,
    mixed,
    lhs,
    copied,
):
    inner = pl.ds(SLOTS // 4, 14 * SLOTS // 4)
    copy = pltpu.make_async_copy(slots_ref.at[inner], out_ref.at[inner], copied)
    copy.start()
    cells = jnp.concatenate([upper_ref[...], lower_ref[...]], 1).reshape(320, 128)
    place = lax.broadcasted_iota(jnp.int32, (320, 128), 0) & 7
    sums = jnp.zeros((320, 128), f32)
    for m in range(R):
        ahead = cells if m == 0 else pltpu.roll(cells, 320 - m, 0)
        behind = cells if m == 0 else pltpu.roll(cells, m, 0)
        used = jnp.where(place < R - m, ahead, jnp.where(place >= R + m, behind, 0.0))
        sums = sums + float(TAPS[2 * R - m]) * used
    none = jnp.zeros((16, 128), f32)
    blocks = []
    for group in range(5):
        tiles = sums[group * 64 : group * 64 + 64]
        blocks.append(
            jnp.concatenate(
                [
                    jnp.concatenate([none, tiles], 0),
                    jnp.concatenate([none[:8], tiles, none[:8]], 0),
                    jnp.concatenate([tiles, none], 0),
                ],
                1,
            )
        )
    high, low = halves(jnp.concatenate(blocks, 0))
    parts[...] = dot(jnp.concatenate([high, low, high], 1), table_ref[...])
    last = parts[320:]
    first = lax.broadcasted_iota(jnp.int32, (80, 128), 1) < 64
    rolled = pltpu.roll(last, 64, 1)
    mixed[0:80] = jnp.where(first, last, pltpu.roll(rolled, 79, 0))
    mixed[80:160] = jnp.where(first, rolled, pltpu.roll(last, 79, 0))
    lhs[...] = edge_ref[...]
    for side in range(2):
        for a in range(2):
            rows = pl.ds(a, EXT, stride=2)
            for pair in range(2):
                for q in range(4):
                    columns = slice(pair * 512 + q * 128, pair * 512 + q * 128 + 128)
                    found = parts[pl.ds((pair * 2 + a) * 80 + side * 4 + q, EXT, stride=8), :]
                    lhs[side * 10 + pair * 4 + q, rows] += found
            for q in range(2):
                found = mixed[pl.ds(a * 80 + side * 4 + q * 2, EXT, stride=8), :]
                lhs[side * 10 + 8 + q, rows] += found
    for side in range(2):
        result = base_ref[side]
        values = jnp.concatenate([lhs[side * 10 + n] for n in range(10)], 1)
        high, low = halves(values)
        values = jnp.concatenate([high.astype(f32), low.astype(f32)], 0).astype(bf16)
        for first_lane, start, count in (
            (0, side * 512, 512),
            (512, 1024 + side * 512, 512),
            (1024, 2048 + side * 256, 256),
        ):
            part = dot(values[:, first_lane : first_lane + count], weight_ref[start : start + count, :])
            result = result + (part[:24] + part[24:])
        high = result.astype(bf16).astype(f32)
        low = result - high
        slots = jnp.concatenate([high[: 2 * EXT], low[:4], low[16 : 2 * EXT]], 0).astype(bf16)
        row = side * 15 * SLOTS // 4
        out_ref[row : row + SLOTS // 4] = slots.reshape(SLOTS // 4, 4, D)
    copy.wait()


def layer_norm(hidden):
    center = hidden - jnp.mean(hidden, axis=-1, keepdims=True)
    spread = jnp.mean(center * center, axis=-1, keepdims=True)
    return (center * lax.rsqrt(spread + 1e-05)).astype(bf16)


def attend(hidden, qkv_ref, out_ref, three, mixed):
    normed = layer_norm(hidden[...])
    for tile in range(9):
        columns = slice(tile * 256, tile * 256 + 256)
        three[:, columns] = dot(normed, qkv_ref[:, columns]).astype(bf16)
    first = lax.broadcasted_iota(jnp.int32, (128, 128), 1) < 64
    none = jnp.zeros((128, 128), bf16)
    ones = jnp.concatenate([jnp.where(first, 1.0, 0.0), jnp.where(first, 0.0, 1.0)], 0).astype(bf16)
    for a in range(2):
        groups = [slice(g * 32 + a * 16, g * 32 + a * 16 + 16) for g in range(8)]
        for pair in range(PAIRS):
            start = pair * 128
            query, keys, values = [
                jnp.concatenate([three[rows, D * n + start : D * n + start + 128] for rows in groups], 0)
                for n in range(3)
            ]
            keys = jnp.concatenate([jnp.where(first, keys, none), jnp.where(first, none, keys)], 0)
            values = values * (1.0 / SHRINK)
            values = jnp.concatenate(
                [jnp.where(first, values, none), jnp.where(first, none, values)], 0
            )
            weights = jnp.exp(dot_t(query, keys) * 0.125).astype(bf16)
            result = dot(weights, jnp.concatenate([values, ones], 1))
            result = (result[:, :128] * (1.0 / result[:, 128:]) * SHRINK).astype(bf16)
            for g, rows in enumerate(groups):
                mixed[rows, start : start + 128] = result[g * 16 : g * 16 + 16]
    for tile in range(3):
        columns = slice(tile * 256, tile * 256 + 256)
        branch = dot(mixed[...], out_ref[:, columns]).astype(bf16)
        hidden[:, columns] = hidden[:, columns] + branch.astype(f32)


def x_kernel(slots_ref, sum_ref, qkv_ref, outw_ref, order_ref, out_ref, hidden, three, mixed):
    hidden[...] = dot(sum_ref[...], slots_ref[...].reshape(NXL * SLOTS, D))
    attend(hidden, qkv_ref, outw_ref, three, mixed)
    tokens = dot(order_ref[...], hidden[...].astype(bf16)).astype(bf16)
    out_ref[...] = tokens.reshape(128, 2, D)


def y_kernel(
    tokens_ref,
    split_ref,
    qkv_ref,
    outw_ref,
    up_ref,
    down_ref,
    out_ref,
    hidden,
    three,
    mixed,
    upper,
):
    hidden[...] = dot(split_ref[...], tokens_ref[...].reshape(TOK, D))
    attend(hidden, qkv_ref, outw_ref, three, mixed)
    normed = layer_norm(hidden[...])
    for tile in range(FF // 256):
        columns = slice(tile * 256, tile * 256 + 256)
        upper[:, columns] = jax.nn.gelu(dot(normed, up_ref[:, columns]), approximate=True).astype(bf16)
    for tile in range(3):
        columns = slice(tile * 256, tile * 256 + 256)
        total = hidden[:, columns] + dot(upper[...], down_ref[:, columns])
        out_ref[:, columns] = total.astype(bf16)


def home_kernel(tokens_ref, order_ref, out_ref):
    out_ref[...] = dot(order_ref[...], tokens_ref[...]).astype(bf16)


def whole(kernel, out_shape, scratch, flops, limit):
    space = pl.BlockSpec(memory_space=pltpu.VMEM)

    def call(*operands):
        size = sum(x.size * x.dtype.itemsize for x in operands)
        return pl.pallas_call(
            kernel,
            out_shape=out_shape,
            in_specs=[space] * len(operands),
            out_specs=[space] * len(out_shape) if isinstance(out_shape, list) else space,
            scratch_shapes=scratch,
            compiler_params=pltpu.CompilerParams(vmem_limit_bytes=limit << 20),
            cost_estimate=pl.CostEstimate(flops=flops, bytes_accessed=size, transcendentals=0),
        )(*operands)

    return call


def like(shape, kind=bf16):
    return jax.ShapeDtypeStruct(shape, kind)


def prepare(fields):
    space = pl.BlockSpec(memory_space=pltpu.VMEM)
    return pl.pallas_call(
        prep_kernel,
        in_specs=[pl.BlockSpec(memory_space=pltpu.HBM)],
        out_specs=[space] * 3,
        out_shape=[
            like((NF, ZS, CX + 2 * PADX, CY), f32),
            like((40, R, 128), f32),
            like((40, R, 128), f32),
        ],
        scratch_shapes=[
            pltpu.VMEM((NF, ZS + 2 * R, CX, CY), f32),
            pltpu.SemaphoreType.DMA((NF,)),
        ],
        compiler_params=pltpu.CompilerParams(vmem_limit_bytes=49 << 20),
    )(fields)


def shards(fields, embed_weight, qkv_weight, out_weight, up_weight, down_weight):
    count = lax.axis_size("gy")
    smooth, upper, lower = prepare(fields)
    upper = lax.ppermute(upper, "gy", [(i, (i + 1) % count) for i in range(count)])
    lower = lax.ppermute(lower, "gy", [((i + 1) % count, i) for i in range(count)])
    slots = like((16 * SLOTS // 4, 4, D))
    inner, base, edge, weight = whole(
        main_kernel,
        [slots, like((2, 24, D), f32), like((20, 24, 128), f32), like((KIN, D))],
        [
            pltpu.VMEM((NF, ZS, 80, CY), f32),
            pltpu.VMEM((NF, ZS, 80, CY), f32),
            pltpu.VMEM((ALL_ROWS, KIN), bf16),
            pltpu.VMEM((ALL_ROWS, D), f32),
            pltpu.VMEM((6, HI_ROWS, 128), f32),
            pltpu.VMEM((ALL_ROWS, D), bf16),
        ],
        2 * 6400 * 256 * 256 + 2 * KIN * 256 * D + 2 * ALL_ROWS * KIN * D,
        18,
    )(smooth, embed_weight)
    slots = whole(
        edge_kernel,
        slots,
        [
            pltpu.VMEM((400, 128), f32),
            pltpu.VMEM((160, 128), f32),
            pltpu.VMEM((20, 24, 128), f32),
            pltpu.SemaphoreType.DMA(()),
        ],
        2 * 64 * KIN * D,
        8,
    )(upper, lower, strip_table(), edge, base, weight, inner)
    slots = lax.all_to_all(
        slots.reshape(NXL, SLOTS // 4, 4, D), "gx", split_axis=0, concat_axis=0, tiled=True
    ).reshape(NXL * SLOTS // 4, 4, D)
    attention = [
        pltpu.VMEM((TOK, D), f32),
        pltpu.VMEM((TOK, 3 * D), bf16),
        pltpu.VMEM((TOK, D), bf16),
    ]
    tokens = whole(x_kernel, like((128, 2, D)), attention, 2 * TOK * D * 4 * D, 10)(
        slots, gather_sum(), qkv_weight, out_weight, interleave()
    )
    tokens = lax.all_to_all(
        tokens, ("gx", "gy"), split_axis=0, concat_axis=0, tiled=True
    )
    tokens = whole(
        y_kernel,
        like((TOK, D)),
        attention + [pltpu.VMEM((TOK, FF), bf16)],
        2 * TOK * D * (4 * D + 2 * FF),
        14,
    )(tokens, separate(), qkv_weight, out_weight, up_weight, down_weight)
    tokens = lax.all_to_all(
        tokens.reshape(8, 32, D), "gy", split_axis=0, concat_axis=0, tiled=True
    ).reshape(TOK, D)
    tokens = whole(home_kernel, like((TOK, D)), [], 2 * TOK * TOK * D, 8)(tokens, to_home())
    return tokens.reshape(2, 16, 8, D)


def solution(mesh):
    return jax.shard_map(
        shards,
        mesh=mesh,
        in_specs=(P(None, None, "gx", "gy"), P(), P(), P(), P(), P()),
        out_specs=P(None, "gy", "gx", None),
        check_vma=False,
    )
```

```python
import functools

import jax
import jax.numpy as jnp
import ml_dtypes
import numpy as np
from jax import lax
from jax.experimental import pallas as pl
from jax.experimental.pallas import tpu as pltpu
from jax.sharding import PartitionSpec as P

R = 4
NF = 5
ZS = 16
CX = 64
CY = 128
D = 768
FF = 3072
KIN = 2560
PAIRS = 6
NXL = 16
TOK = 256
EXT = 10
SLOTS = 28
BOUND = (0, 1, 8, 9)
HI_ROWS = EXT * 32
ALL_ROWS = HI_ROWS + 128
PADX = 16
SHRINK = 2.0**15
bf16 = jnp.bfloat16
f32 = jnp.float32


def np_taps():
    offsets = np.arange(-R, R + 1).astype(np.float32)
    values = np.exp(-offsets * offsets / np.float32(4.5)).astype(np.float32)
    return (values / values.sum(dtype=np.float32)).astype(np.float32)


TAPS = np_taps()


def as_bf16(values):
    return np.asarray(values, np.float32).astype(ml_dtypes.bfloat16)


def split_np(values):
    high = as_bf16(values)
    low = as_bf16(values - high.astype(np.float32))
    return high, low


def band_table():
    row = lax.broadcasted_iota(jnp.int32, (CY, CY), 0)
    column = lax.broadcasted_iota(jnp.int32, (CY, CY), 1)
    apart = jnp.abs(row - ((column & 15) * 8 + (column >> 4)))
    high = jnp.zeros((CY, CY), f32)
    low = jnp.zeros((CY, CY), f32)
    for k in range(R + 1):
        tap_hi, tap_lo = split_np(TAPS[R + k])
        high = jnp.where(apart == k, float(tap_hi), high)
        low = jnp.where(apart == k, float(tap_lo), low)
    left = jnp.concatenate([high, high], 0)
    right = jnp.concatenate([low, jnp.zeros_like(low)], 0)
    return jnp.concatenate([left, right], 1).astype(bf16)


def strip_table():
    table = np.zeros((384, 128), np.float32)
    for group in range(16):
        for x in range(8):
            for k in range(-R, R + 1):
                source = x + k + 8
                table[source // 8 * 128 + group * 8 + source % 8, group * 8 + x] = TAPS[R + k]
    high, low = split_np(table)
    return np.concatenate([high, high, low], 0)


def weight_order():
    row = lax.broadcasted_iota(jnp.int32, (256, 256), 0)
    column = lax.broadcasted_iota(jnp.int32, (256, 256), 1)
    return jnp.where(column == (row & 31) * 8 + (row >> 5), 1.0, 0.0).astype(bf16)


def permutation(rows, columns, source):
    table = np.zeros((rows, columns), np.float32)
    for row in range(rows):
        for column in source(row):
            table[row, column] = 1.0
    return as_bf16(table)


def message_order():
    row = lax.broadcasted_iota(jnp.int32, (ALL_ROWS, ALL_ROWS), 0)
    column = lax.broadcasted_iota(jnp.int32, (ALL_ROWS, ALL_ROWS), 1)
    slot, line = column >> 4, column & 15
    return jnp.where(row == line * SLOTS + slot, 1.0, 0.0).astype(bf16)


def gather_sum():
    low = {ext: 2 * EXT + 2 * n for n, ext in enumerate(BOUND)}

    def source(row):
        a, i, c = row // 128, row // 8 % 16, row % 8
        found = [i * SLOTS + (c + 1) * 2 + a]
        if c == 0:
            left = (i - 1) % NXL * SLOTS
            found += [i * SLOTS + low[1] + a, left + 18 + a, left + low[9] + a]
        if c == 7:
            right = (i + 1) % NXL * SLOTS
            found += [i * SLOTS + low[8] + a, right + a, right + low[0] + a]
        return found

    return permutation(TOK, NXL * SLOTS, source)


def interleave():
    return permutation(TOK, TOK, lambda r: [(r % 2) * 128 + r // 2])


def separate():
    return permutation(TOK, TOK, lambda r: [((r % 16) * 8 + r // 16 % 8) * 2 + r // 128])


def to_home():
    return permutation(TOK, TOK, lambda r: [(r % 8) * 32 + r // 8])


def dot(left, right):
    return lax.dot_general(left, right, (((1,), (0,)), ((), ())), preferred_element_type=f32)


def dot_split(left, table):
    high, low = halves(left)
    return dot(jnp.concatenate([high, low, high], 1), table)


def dot_t(left, right):
    return lax.dot_general(left, right, (((1,), (1,)), ((), ())), preferred_element_type=f32)


def halves(values):
    high = values.astype(bf16)
    return high, (values - high.astype(f32)).astype(bf16)


def prep_kernel(fields_ref, smooth_ref, upper_ref, lower_ref, cells, arrived):
    copies = [
        pltpu.make_async_copy(fields_ref.at[f], cells.at[f], arrived.at[f]) for f in range(NF)
    ]
    for copy in copies:
        copy.start()
    zero = jnp.zeros((NF, ZS, PADX, CY), f32)
    smooth_ref[:, :, 0:PADX] = zero
    smooth_ref[:, :, PADX + CX :] = zero

    def strip(index, block):
        turned = block.reshape(128, 128).T
        lower_ref[index] = turned[:R]
        upper_ref[index] = turned[CY - R :]

    for f in range(NF):
        copies[f].wait()
        for tile in range(CX // 8):
            rows = slice(tile * 8, tile * 8 + 8)
            plane = [cells[f, z, rows, :] for z in range(ZS + 2 * R)]
            for z in range(ZS):
                total = float(TAPS[R]) * plane[z + R]
                for k in range(1, R + 1):
                    total = total + float(TAPS[R + k]) * (plane[z + R - k] + plane[z + R + k])
                smooth_ref[f, z, PADX + tile * 8 : PADX + tile * 8 + 8, :] = total
        if f % 2 == 1:
            for a in range(2):
                for c in range(8):
                    rows = slice(PADX + c * 8, PADX + c * 8 + 8)
                    block = smooth_ref[f - 1 : f + 1, a * 8 : a * 8 + 8, rows, :]
                    strip((f // 2 * 2 + a) * 8 + c, block)
    for c in range(8):
        strip(32 + c, smooth_ref[NF - 1, :, PADX + c * 8 : PADX + c * 8 + 8, :])


def main_kernel(
    smooth_ref,
    weight_ref,
    out_ref,
    base_ref,
    edge_ref,
    order_ref,
    across,
    along,
    lhs,
    both,
    sums,
    mid,
):
    band = band_table()
    order = weight_order()
    first = lax.broadcasted_iota(jnp.int32, (16, 128), 1) < 64
    edge_ref[...] = jnp.zeros_like(edge_ref)

    def filtered(f):
        for z in range(ZS):
            total = float(TAPS[R]) * smooth_ref[f, z, PADX - 8 : PADX + 72, :]
            for k in range(1, R + 1):
                total = total + float(TAPS[R + k]) * (
                    smooth_ref[f, z, PADX - 8 - k : PADX + 72 - k, :]
                    + smooth_ref[f, z, PADX - 8 + k : PADX + 72 + k, :]
                )
            across[f, z] = total
        for part in range(4):
            planes = slice(part * 4, part * 4 + 4)
            high, low = halves(across[f, planes].reshape(320, CY))
            pair = dot(jnp.concatenate([high, low], 1), band)
            along[f, planes] = (pair[:, :CY] + pair[:, CY:]).reshape(4, 80, CY)

    def reordered(f):
        for tile in (2 * f, 2 * f + 1):
            turned = dot(order, weight_ref[tile * 256 : tile * 256 + 256, :]).astype(bf16)
            for y in range(8):
                if tile < 8:
                    start = tile // 4 * 1024 + y * 128 + tile % 4 * 32
                else:
                    start = 2048 + y * 64 + (tile - 8) * 32
                order_ref[start : start + 32, :] = turned[y * 32 : y * 32 + 32]

    def put(ext, a, start, side, place, values):
        high = values.astype(bf16)
        rest = values - high.astype(f32)
        row = (ext * 2 + a) * 16
        lhs[row : row + 16, start : start + 128] = high
        if ext in BOUND:
            row = HI_ROWS + (BOUND.index(ext) * 2 + a) * 16
            lhs[row : row + 16, start : start + 128] = rest.astype(bf16)
        else:
            row = ext * 2 + a
            edge_ref[side * 10 + place, row : row + 1, :] = rest[side * 15 : side * 15 + 1]

    for chunk, members in enumerate(((0, 1), (2, 3), (4,))):
        for f in members:
            filtered(f)
            reordered(f)
        for ext in range(EXT):
            rows = slice(ext * 8, ext * 8 + 8)
            if len(members) == 2:
                for a in range(2):
                    block = along[members[0] : members[0] + 2, a * 8 : a * 8 + 8, rows, :]
                    turned = block.reshape(128, 128).T
                    for y in range(8):
                        values = turned[y * 16 : y * 16 + 16]
                        start = chunk * 1024 + y * 128
                        put(ext, a, start, y // 4, chunk * 4 + y % 4, values)
            else:
                turned = along[4, :, rows, :].reshape(128, 128).T
                for m in range(4):
                    even = turned[m * 32 : m * 32 + 16]
                    odd = turned[m * 32 + 16 : m * 32 + 32]
                    start, place = 2048 + m * 128, 8 + m % 2
                    put(ext, 0, start, m // 2, place, jnp.where(first, even, pltpu.roll(odd, 64, 1)))
                    put(ext, 1, start, m // 2, place, jnp.where(first, pltpu.roll(even, 64, 1), odd))
        deep = slice(chunk * 1024, min(chunk * 1024 + 1024, KIN))
        for tile in range(3):
            columns = slice(tile * 256, tile * 256 + 256)
            part = dot(lhs[:, deep], order_ref[deep, columns])
            both[:, columns] = part if chunk == 0 else both[:, columns] + part
    for tile in range(6):
        columns = slice(tile * 128, tile * 128 + 128)
        for start, low in ((0, HI_ROWS), (256, HI_ROWS + 64)):
            rows, rest = slice(start, start + 64), slice(low, low + 64)
            total = both[rows, columns] + both[rest, columns]
            sums[tile, rows] = total
            mid[rows, columns], mid[rest, columns] = halves(total)
        total = both[64:256, columns]
        sums[tile, 64:256] = total
        mid[64:256, columns] = total.astype(bf16)
        for side in range(2):
            base_ref[side, 0 : 2 * EXT, columns] = sums[tile, pl.ds(side * 15, 2 * EXT, stride=16), :]
            base_ref[side, 2 * EXT :, columns] = jnp.zeros((4, 128), f32)
    slots = dot(message_order(), mid[...]).astype(bf16)
    out_ref[...] = slots.reshape(16 * SLOTS // 4, 4, D)


def edge_kernel(
    upper_ref,
    lower_ref,
    table_ref,
    edge_ref,
    base_ref,
    weight_ref,
    slots_ref,
    out_ref,
    parts,
    mixed,
    lhs,
    copied,
):
    inner = pl.ds(SLOTS // 4, 14 * SLOTS // 4)
    copy = pltpu.make_async_copy(slots_ref.at[inner], out_ref.at[inner], copied)
    copy.start()
    cells = jnp.concatenate([upper_ref[...], lower_ref[...]], 1).reshape(320, 128)
    place = lax.broadcasted_iota(jnp.int32, (320, 128), 0) & 7
    sums = jnp.zeros((320, 128), f32)
    for m in range(R):
        ahead = cells if m == 0 else pltpu.roll(cells, 320 - m, 0)
        behind = cells if m == 0 else pltpu.roll(cells, m, 0)
        used = jnp.where(place < R - m, ahead, jnp.where(place >= R + m, behind, 0.0))
        sums = sums + float(TAPS[2 * R - m]) * used
    none = jnp.zeros((16, 128), f32)
    blocks = []
    for group in range(5):
        tiles = sums[group * 64 : group * 64 + 64]
        blocks.append(
            jnp.concatenate(
                [
                    jnp.concatenate([none, tiles], 0),
                    jnp.concatenate([none[:8], tiles, none[:8]], 0),
                    jnp.concatenate([tiles, none], 0),
                ],
                1,
            )
        )
    high, low = halves(jnp.concatenate(blocks, 0))
    parts[...] = dot(jnp.concatenate([high, low, high], 1), table_ref[...])
    last = parts[320:]
    first = lax.broadcasted_iota(jnp.int32, (80, 128), 1) < 64
    rolled = pltpu.roll(last, 64, 1)
    mixed[0:80] = jnp.where(first, last, pltpu.roll(rolled, 79, 0))
    mixed[80:160] = jnp.where(first, rolled, pltpu.roll(last, 79, 0))
    lhs[...] = edge_ref[...]
    for side in range(2):
        for a in range(2):
            rows = pl.ds(a, EXT, stride=2)
            for pair in range(2):
                for q in range(4):
                    columns = slice(pair * 512 + q * 128, pair * 512 + q * 128 + 128)
                    found = parts[pl.ds((pair * 2 + a) * 80 + side * 4 + q, EXT, stride=8), :]
                    lhs[side * 10 + pair * 4 + q, rows] += found
            for q in range(2):
                found = mixed[pl.ds(a * 80 + side * 4 + q * 2, EXT, stride=8), :]
                lhs[side * 10 + 8 + q, rows] += found
    for side in range(2):
        result = base_ref[side]
        values = jnp.concatenate([lhs[side * 10 + n] for n in range(10)], 1)
        high, low = halves(values)
        values = jnp.concatenate([high.astype(f32), low.astype(f32)], 0).astype(bf16)
        for first_lane, start, count in (
            (0, side * 512, 512),
            (512, 1024 + side * 512, 512),
            (1024, 2048 + side * 256, 256),
        ):
            part = dot(values[:, first_lane : first_lane + count], weight_ref[start : start + count, :])
            result = result + (part[:24] + part[24:])
        high = result.astype(bf16).astype(f32)
        low = result - high
        slots = jnp.concatenate([high[: 2 * EXT], low[:4], low[16 : 2 * EXT]], 0).astype(bf16)
        row = side * 15 * SLOTS // 4
        out_ref[row : row + SLOTS // 4] = slots.reshape(SLOTS // 4, 4, D)
    copy.wait()


def layer_norm(hidden):
    center = hidden - jnp.mean(hidden, axis=-1, keepdims=True)
    spread = jnp.mean(center * center, axis=-1, keepdims=True)
    return (center * lax.rsqrt(spread + 1e-05)).astype(bf16)


def attention(a, hidden, qkv_ref, out_ref, three, mixed):
    rows = slice(a * 128, a * 128 + 128)
    normed = layer_norm(hidden[rows])
    yield
    for tile in range(9):
        columns = slice(tile * 256, tile * 256 + 256)
        three[rows, columns] = dot(normed, qkv_ref[:, columns]).astype(bf16)
        yield
    first = lax.broadcasted_iota(jnp.int32, (128, 128), 1) < 64
    none = jnp.zeros((128, 128), bf16)
    ones = jnp.concatenate([jnp.where(first, 1.0, 0.0), jnp.where(first, 0.0, 1.0)], 0).astype(bf16)
    for pair in range(PAIRS):
        columns = slice(pair * 128, pair * 128 + 128)
        query, keys, values = [
            three[rows, D * n + pair * 128 : D * n + pair * 128 + 128] for n in range(3)
        ]
        keys = jnp.concatenate([jnp.where(first, keys, none), jnp.where(first, none, keys)], 0)
        values = values * (1.0 / SHRINK)
        values = jnp.concatenate([jnp.where(first, values, none), jnp.where(first, none, values)], 0)
        weights = jnp.exp(dot_t(query, keys) * 0.125).astype(bf16)
        result = dot(weights, jnp.concatenate([values, ones], 1))
        mixed[rows, columns] = (result[:, :128] * (1.0 / result[:, 128:]) * SHRINK).astype(bf16)
        yield
    for tile in range(3):
        columns = slice(tile * 256, tile * 256 + 256)
        branch = dot(mixed[rows], out_ref[:, columns]).astype(bf16)
        hidden[rows, columns] = hidden[rows, columns] + branch.astype(f32)
        yield


def feed_forward(a, hidden, up_ref, down_ref, out_ref, upper):
    rows = slice(a * 128, a * 128 + 128)
    normed = layer_norm(hidden[rows])
    yield
    for tile in range(FF // 256):
        columns = slice(tile * 256, tile * 256 + 256)
        values = jax.nn.gelu(dot(normed, up_ref[:, columns]), approximate=True)
        upper[rows, columns] = values.astype(bf16)
        yield
    for tile in range(3):
        columns = slice(tile * 256, tile * 256 + 256)
        total = (hidden[rows, columns] + dot(upper[rows], down_ref[:, columns])).astype(bf16)
        for j in range(8):
            start = j * 32 + a * 16
            out_ref[start : start + 16, columns] = total[j * 16 : j * 16 + 16]
        yield


def staggered(chains, lag):
    lead, trail = chains
    for _ in range(lag):
        next(lead, None)
    while True:
        done = [next(lead, "end"), next(trail, "end")]
        if done == ["end", "end"]:
            break


X_LAG = 0
Y_LAG = 0


def x_kernel(slots_ref, sum_ref, qkv_ref, outw_ref, order_ref, out_ref, hidden, three, mixed):
    slots = slots_ref[...].reshape(NXL * SLOTS, D)

    def chain(a):
        rows = slice(a * 128, a * 128 + 128)
        hidden[rows] = dot(sum_ref[rows], slots)
        yield from attention(a, hidden, qkv_ref, outw_ref, three, mixed)

    staggered([chain(0), chain(1)], X_LAG)
    tokens = dot(order_ref[...], hidden[...].astype(bf16)).astype(bf16)
    out_ref[...] = tokens.reshape(128, 2, D)


def y_kernel(
    tokens_ref,
    split_ref,
    qkv_ref,
    outw_ref,
    up_ref,
    down_ref,
    out_ref,
    hidden,
    three,
    mixed,
    upper,
):
    tokens = tokens_ref[...].reshape(TOK, D)

    def chain(a):
        rows = slice(a * 128, a * 128 + 128)
        hidden[rows] = dot(split_ref[rows], tokens)
        yield from attention(a, hidden, qkv_ref, outw_ref, three, mixed)
        yield from feed_forward(a, hidden, up_ref, down_ref, out_ref, upper)

    staggered([chain(0), chain(1)], Y_LAG)


def home_kernel(tokens_ref, order_ref, out_ref):
    out_ref[...] = dot(order_ref[...], tokens_ref[...]).astype(bf16)


def whole(kernel, out_shape, scratch, flops, limit):
    space = pl.BlockSpec(memory_space=pltpu.VMEM)

    def call(*operands):
        size = sum(x.size * x.dtype.itemsize for x in operands)
        return pl.pallas_call(
            kernel,
            out_shape=out_shape,
            in_specs=[space] * len(operands),
            out_specs=[space] * len(out_shape) if isinstance(out_shape, list) else space,
            scratch_shapes=scratch,
            compiler_params=pltpu.CompilerParams(vmem_limit_bytes=limit << 20),
            cost_estimate=pl.CostEstimate(flops=flops, bytes_accessed=size, transcendentals=0),
        )(*operands)

    return call


def like(shape, kind=bf16):
    return jax.ShapeDtypeStruct(shape, kind)


def prepare(fields):
    space = pl.BlockSpec(memory_space=pltpu.VMEM)
    return pl.pallas_call(
        prep_kernel,
        in_specs=[pl.BlockSpec(memory_space=pltpu.HBM)],
        out_specs=[space] * 3,
        out_shape=[
            like((NF, ZS, CX + 2 * PADX, CY), f32),
            like((40, R, 128), f32),
            like((40, R, 128), f32),
        ],
        scratch_shapes=[
            pltpu.VMEM((NF, ZS + 2 * R, CX, CY), f32),
            pltpu.SemaphoreType.DMA((NF,)),
        ],
        compiler_params=pltpu.CompilerParams(vmem_limit_bytes=49 << 20),
    )(fields)


def shards(fields, embed_weight, qkv_weight, out_weight, up_weight, down_weight):
    count = lax.axis_size("gy")
    smooth, upper, lower = prepare(fields)
    upper = lax.ppermute(upper, "gy", [(i, (i + 1) % count) for i in range(count)])
    lower = lax.ppermute(lower, "gy", [((i + 1) % count, i) for i in range(count)])
    slots = like((16 * SLOTS // 4, 4, D))
    inner, base, edge, weight = whole(
        main_kernel,
        [slots, like((2, 24, D), f32), like((20, 24, 128), f32), like((KIN, D))],
        [
            pltpu.VMEM((NF, ZS, 80, CY), f32),
            pltpu.VMEM((NF, ZS, 80, CY), f32),
            pltpu.VMEM((ALL_ROWS, KIN), bf16),
            pltpu.VMEM((ALL_ROWS, D), f32),
            pltpu.VMEM((6, HI_ROWS, 128), f32),
            pltpu.VMEM((ALL_ROWS, D), bf16),
        ],
        2 * 6400 * 256 * 256 + 2 * KIN * 256 * D + 2 * ALL_ROWS * KIN * D,
        18,
    )(smooth, embed_weight)
    slots = whole(
        edge_kernel,
        slots,
        [
            pltpu.VMEM((400, 128), f32),
            pltpu.VMEM((160, 128), f32),
            pltpu.VMEM((20, 24, 128), f32),
            pltpu.SemaphoreType.DMA(()),
        ],
        2 * 64 * KIN * D,
        8,
    )(upper, lower, strip_table(), edge, base, weight, inner)
    slots = lax.all_to_all(
        slots.reshape(NXL, SLOTS // 4, 4, D), "gx", split_axis=0, concat_axis=0, tiled=True
    ).reshape(NXL * SLOTS // 4, 4, D)
    attention = [
        pltpu.VMEM((TOK, D), f32),
        pltpu.VMEM((TOK, 3 * D), bf16),
        pltpu.VMEM((TOK, D), bf16),
    ]
    tokens = whole(x_kernel, like((128, 2, D)), attention, 2 * TOK * D * 4 * D, 10)(
        slots, gather_sum(), qkv_weight, out_weight, interleave()
    )
    tokens = lax.all_to_all(
        tokens, ("gx", "gy"), split_axis=0, concat_axis=0, tiled=True
    )
    tokens = whole(
        y_kernel,
        like((TOK, D)),
        attention + [pltpu.VMEM((TOK, FF), bf16)],
        2 * TOK * D * (4 * D + 2 * FF),
        14,
    )(tokens, separate(), qkv_weight, out_weight, up_weight, down_weight)
    tokens = lax.all_to_all(
        tokens.reshape(8, 32, D), "gy", split_axis=0, concat_axis=0, tiled=True
    ).reshape(TOK, D)
    tokens = whole(home_kernel, like((TOK, D)), [], 2 * TOK * TOK * D, 8)(tokens, to_home())
    return tokens.reshape(2, 16, 8, D)


def solution(mesh):
    return jax.shard_map(
        shards,
        mesh=mesh,
        in_specs=(P(None, None, "gx", "gy"), P(), P(), P(), P(), P()),
        out_specs=P(None, "gy", "gx", None),
        check_vma=False,
    )
```

```python
import functools

import jax
import jax.numpy as jnp
import ml_dtypes
import numpy as np
from jax import lax
from jax.experimental import pallas as pl
from jax.experimental.pallas import tpu as pltpu
from jax.sharding import PartitionSpec as P

R = 4
NF = 5
ZS = 16
CX = 64
CY = 128
D = 768
FF = 3072
KIN = 2560
PAIRS = 6
NXL = 16
TOK = 256
EXT = 10
SLOTS = 28
BOUND = (0, 1, 8, 9)
HI_ROWS = EXT * 32
ALL_ROWS = HI_ROWS + 128
PADX = 16
SHRINK = 2.0**15
bf16 = jnp.bfloat16
f32 = jnp.float32


def np_taps():
    offsets = np.arange(-R, R + 1).astype(np.float32)
    values = np.exp(-offsets * offsets / np.float32(4.5)).astype(np.float32)
    return (values / values.sum(dtype=np.float32)).astype(np.float32)


TAPS = np_taps()


def as_bf16(values):
    return np.asarray(values, np.float32).astype(ml_dtypes.bfloat16)


def split_np(values):
    high = as_bf16(values)
    low = as_bf16(values - high.astype(np.float32))
    return high, low


def band_table():
    row = lax.broadcasted_iota(jnp.int32, (CY, CY), 0)
    column = lax.broadcasted_iota(jnp.int32, (CY, CY), 1)
    apart = jnp.abs(row - ((column & 15) * 8 + (column >> 4)))
    high = jnp.zeros((CY, CY), f32)
    low = jnp.zeros((CY, CY), f32)
    for k in range(R + 1):
        tap_hi, tap_lo = split_np(TAPS[R + k])
        high = jnp.where(apart == k, float(tap_hi), high)
        low = jnp.where(apart == k, float(tap_lo), low)
    left = jnp.concatenate([high, high], 0)
    right = jnp.concatenate([low, jnp.zeros_like(low)], 0)
    return jnp.concatenate([left, right], 1).astype(bf16)


def strip_table():
    table = np.zeros((384, 128), np.float32)
    for group in range(16):
        for x in range(8):
            for k in range(-R, R + 1):
                source = x + k + 8
                table[source // 8 * 128 + group * 8 + source % 8, group * 8 + x] = TAPS[R + k]
    high, low = split_np(table)
    return np.concatenate([high, high, low], 0)


def weight_order():
    row = lax.broadcasted_iota(jnp.int32, (256, 256), 0)
    column = lax.broadcasted_iota(jnp.int32, (256, 256), 1)
    return jnp.where(column == (row & 31) * 8 + (row >> 5), 1.0, 0.0).astype(bf16)


def permutation(rows, columns, source):
    table = np.zeros((rows, columns), np.float32)
    for row in range(rows):
        for column in source(row):
            table[row, column] = 1.0
    return as_bf16(table)


def message_order():
    row = lax.broadcasted_iota(jnp.int32, (ALL_ROWS, ALL_ROWS), 0)
    column = lax.broadcasted_iota(jnp.int32, (ALL_ROWS, ALL_ROWS), 1)
    slot, line = column >> 4, column & 15
    return jnp.where(row == line * SLOTS + slot, 1.0, 0.0).astype(bf16)


def gather_sum():
    low = {ext: 2 * EXT + 2 * n for n, ext in enumerate(BOUND)}

    def source(row):
        a, i, c = row // 128, row // 8 % 16, row % 8
        found = [i * SLOTS + (c + 1) * 2 + a]
        if c == 0:
            left = (i - 1) % NXL * SLOTS
            found += [i * SLOTS + low[1] + a, left + 18 + a, left + low[9] + a]
        if c == 7:
            right = (i + 1) % NXL * SLOTS
            found += [i * SLOTS + low[8] + a, right + a, right + low[0] + a]
        return found

    return permutation(TOK, NXL * SLOTS, source)


def interleave():
    return permutation(TOK, TOK, lambda r: [(r % 2) * 128 + r // 2])


def separate():
    return permutation(TOK, TOK, lambda r: [((r % 16) * 8 + r // 16 % 8) * 2 + r // 128])


def to_home():
    return permutation(TOK, TOK, lambda r: [(r % 8) * 32 + r // 8])


def dot(left, right):
    return lax.dot_general(left, right, (((1,), (0,)), ((), ())), preferred_element_type=f32)


def dot_split(left, table):
    high, low = halves(left)
    return dot(jnp.concatenate([high, low, high], 1), table)


def dot_t(left, right):
    return lax.dot_general(left, right, (((1,), (1,)), ((), ())), preferred_element_type=f32)


def halves(values):
    high = values.astype(bf16)
    return high, (values - high.astype(f32)).astype(bf16)


def prep_kernel(fields_ref, smooth_ref, upper_ref, lower_ref, cells, arrived):
    copies = [
        pltpu.make_async_copy(fields_ref.at[f], cells.at[f], arrived.at[f]) for f in range(NF)
    ]
    for copy in copies:
        copy.start()
    zero = jnp.zeros((NF, ZS, PADX, CY), f32)
    smooth_ref[:, :, 0:PADX] = zero
    smooth_ref[:, :, PADX + CX :] = zero

    def strip(index, block):
        turned = block.reshape(128, 128).T
        lower_ref[index] = turned[:R]
        upper_ref[index] = turned[CY - R :]

    for f in range(NF):
        copies[f].wait()
        for tile in range(CX // 8):
            rows = slice(tile * 8, tile * 8 + 8)
            plane = [cells[f, z, rows, :] for z in range(ZS + 2 * R)]
            for z in range(ZS):
                total = float(TAPS[R]) * plane[z + R]
                for k in range(1, R + 1):
                    total = total + float(TAPS[R + k]) * (plane[z + R - k] + plane[z + R + k])
                smooth_ref[f, z, PADX + tile * 8 : PADX + tile * 8 + 8, :] = total
        if f % 2 == 1:
            for a in range(2):
                for c in range(8):
                    rows = slice(PADX + c * 8, PADX + c * 8 + 8)
                    block = smooth_ref[f - 1 : f + 1, a * 8 : a * 8 + 8, rows, :]
                    strip((f // 2 * 2 + a) * 8 + c, block)
    for c in range(8):
        strip(32 + c, smooth_ref[NF - 1, :, PADX + c * 8 : PADX + c * 8 + 8, :])


CHUNKS = (0, 2, 1)
STRIDE = 2


def main_kernel(
    smooth_ref,
    weight_ref,
    out_ref,
    base_ref,
    edge_ref,
    order_ref,
    across,
    along,
    lhs,
    both,
    sums,
    mid,
):
    band = band_table()
    order = weight_order()
    first = lax.broadcasted_iota(jnp.int32, (16, 128), 1) < 64
    edge_ref[...] = jnp.zeros_like(edge_ref)

    def filtered(f):
        for part in range(4):
            planes = slice(part * 4, part * 4 + 4)
            for z in range(part * 4, part * 4 + 4):
                total = float(TAPS[R]) * smooth_ref[f, z, PADX - 8 : PADX + 72, :]
                for k in range(1, R + 1):
                    total = total + float(TAPS[R + k]) * (
                        smooth_ref[f, z, PADX - 8 - k : PADX + 72 - k, :]
                        + smooth_ref[f, z, PADX - 8 + k : PADX + 72 + k, :]
                    )
                across[f, z] = total
            high, low = halves(across[f, planes].reshape(320, CY))
            pair = dot(jnp.concatenate([high, low], 1), band)
            along[f, planes] = (pair[:, :CY] + pair[:, CY:]).reshape(4, 80, CY)
            yield

    def reordered(f):
        for tile in (2 * f, 2 * f + 1):
            turned = dot(order, weight_ref[tile * 256 : tile * 256 + 256, :]).astype(bf16)
            for y in range(8):
                if tile < 8:
                    start = tile // 4 * 1024 + y * 128 + tile % 4 * 32
                else:
                    start = 2048 + y * 64 + (tile - 8) * 32
                order_ref[start : start + 32, :] = turned[y * 32 : y * 32 + 32]
            yield

    def put(ext, a, start, side, place, values):
        high = values.astype(bf16)
        rest = values - high.astype(f32)
        row = (ext * 2 + a) * 16
        lhs[row : row + 16, start : start + 128] = high
        if ext in BOUND:
            row = HI_ROWS + (BOUND.index(ext) * 2 + a) * 16
            lhs[row : row + 16, start : start + 128] = rest.astype(bf16)
        else:
            row = ext * 2 + a
            edge_ref[side * 10 + place, row : row + 1, :] = rest[side * 15 : side * 15 + 1]

    def produce(chunk):
        members = range(chunk * 2, min(chunk * 2 + 2, NF))
        for f in members:
            yield from filtered(f)
            yield from reordered(f)
        for ext in range(EXT):
            rows = slice(ext * 8, ext * 8 + 8)
            if len(members) == 2:
                for a in range(2):
                    block = along[members[0] : members[0] + 2, a * 8 : a * 8 + 8, rows, :]
                    turned = block.reshape(128, 128).T
                    for y in range(8):
                        values = turned[y * 16 : y * 16 + 16]
                        start = chunk * 1024 + y * 128
                        put(ext, a, start, y // 4, chunk * 4 + y % 4, values)
            else:
                turned = along[4, :, rows, :].reshape(128, 128).T
                for m in range(4):
                    even = turned[m * 32 : m * 32 + 16]
                    odd = turned[m * 32 + 16 : m * 32 + 32]
                    start, place = 2048 + m * 128, 8 + m % 2
                    put(ext, 0, start, m // 2, place, jnp.where(first, even, pltpu.roll(odd, 64, 1)))
                    put(ext, 1, start, m // 2, place, jnp.where(first, pltpu.roll(even, 64, 1), odd))
            yield

    def consume(chunk, fresh):
        deep = slice(chunk * 1024, min(chunk * 1024 + 1024, KIN))
        for tile in range(3):
            columns = slice(tile * 256, tile * 256 + 256)
            for rows in (slice(0, ALL_ROWS // 2), slice(ALL_ROWS // 2, ALL_ROWS)):
                part = dot(lhs[rows, deep], order_ref[deep, columns])
                both[rows, columns] = part if fresh else both[rows, columns] + part
                yield

    for _ in produce(CHUNKS[0]):
        pass
    for n, chunk in enumerate(CHUNKS):
        ahead = produce(CHUNKS[n + 1]) if n + 1 < len(CHUNKS) else iter(())
        for _ in consume(chunk, n == 0):
            for _ in range(STRIDE):
                next(ahead, None)
        for _ in ahead:
            pass
    for tile in range(6):
        columns = slice(tile * 128, tile * 128 + 128)
        for start, low in ((0, HI_ROWS), (256, HI_ROWS + 64)):
            rows, rest = slice(start, start + 64), slice(low, low + 64)
            total = both[rows, columns] + both[rest, columns]
            sums[tile, rows] = total
            mid[rows, columns], mid[rest, columns] = halves(total)
        total = both[64:256, columns]
        sums[tile, 64:256] = total
        mid[64:256, columns] = total.astype(bf16)
        for side in range(2):
            base_ref[side, 0 : 2 * EXT, columns] = sums[tile, pl.ds(side * 15, 2 * EXT, stride=16), :]
            base_ref[side, 2 * EXT :, columns] = jnp.zeros((4, 128), f32)
    slots = dot(message_order(), mid[...]).astype(bf16)
    out_ref[...] = slots.reshape(16 * SLOTS // 4, 4, D)


def edge_kernel(
    upper_ref,
    lower_ref,
    table_ref,
    edge_ref,
    base_ref,
    weight_ref,
    slots_ref,
    out_ref,
    parts,
    mixed,
    lhs,
    copied,
):
    inner = pl.ds(SLOTS // 4, 14 * SLOTS // 4)
    copy = pltpu.make_async_copy(slots_ref.at[inner], out_ref.at[inner], copied)
    copy.start()
    cells = jnp.concatenate([upper_ref[...], lower_ref[...]], 1).reshape(320, 128)
    place = lax.broadcasted_iota(jnp.int32, (320, 128), 0) & 7
    sums = jnp.zeros((320, 128), f32)
    for m in range(R):
        ahead = cells if m == 0 else pltpu.roll(cells, 320 - m, 0)
        behind = cells if m == 0 else pltpu.roll(cells, m, 0)
        used = jnp.where(place < R - m, ahead, jnp.where(place >= R + m, behind, 0.0))
        sums = sums + float(TAPS[2 * R - m]) * used
    none = jnp.zeros((16, 128), f32)
    blocks = []
    for group in range(5):
        tiles = sums[group * 64 : group * 64 + 64]
        blocks.append(
            jnp.concatenate(
                [
                    jnp.concatenate([none, tiles], 0),
                    jnp.concatenate([none[:8], tiles, none[:8]], 0),
                    jnp.concatenate([tiles, none], 0),
                ],
                1,
            )
        )
    high, low = halves(jnp.concatenate(blocks, 0))
    parts[...] = dot(jnp.concatenate([high, low, high], 1), table_ref[...])
    last = parts[320:]
    first = lax.broadcasted_iota(jnp.int32, (80, 128), 1) < 64
    rolled = pltpu.roll(last, 64, 1)
    mixed[0:80] = jnp.where(first, last, pltpu.roll(rolled, 79, 0))
    mixed[80:160] = jnp.where(first, rolled, pltpu.roll(last, 79, 0))
    lhs[...] = edge_ref[...]
    for side in range(2):
        for a in range(2):
            rows = pl.ds(a, EXT, stride=2)
            for pair in range(2):
                for q in range(4):
                    columns = slice(pair * 512 + q * 128, pair * 512 + q * 128 + 128)
                    found = parts[pl.ds((pair * 2 + a) * 80 + side * 4 + q, EXT, stride=8), :]
                    lhs[side * 10 + pair * 4 + q, rows] += found
            for q in range(2):
                found = mixed[pl.ds(a * 80 + side * 4 + q * 2, EXT, stride=8), :]
                lhs[side * 10 + 8 + q, rows] += found
    for side in range(2):
        result = base_ref[side]
        values = jnp.concatenate([lhs[side * 10 + n] for n in range(10)], 1)
        high, low = halves(values)
        values = jnp.concatenate([high.astype(f32), low.astype(f32)], 0).astype(bf16)
        for first_lane, start, count in (
            (0, side * 512, 512),
            (512, 1024 + side * 512, 512),
            (1024, 2048 + side * 256, 256),
        ):
            part = dot(values[:, first_lane : first_lane + count], weight_ref[start : start + count, :])
            result = result + (part[:24] + part[24:])
        high = result.astype(bf16).astype(f32)
        low = result - high
        slots = jnp.concatenate([high[: 2 * EXT], low[:4], low[16 : 2 * EXT]], 0).astype(bf16)
        row = side * 15 * SLOTS // 4
        out_ref[row : row + SLOTS // 4] = slots.reshape(SLOTS // 4, 4, D)
    copy.wait()


def layer_norm(hidden):
    center = hidden - jnp.mean(hidden, axis=-1, keepdims=True)
    spread = jnp.mean(center * center, axis=-1, keepdims=True)
    return (center * lax.rsqrt(spread + 1e-05)).astype(bf16)


def attention(a, hidden, qkv_ref, out_ref, three, mixed):
    rows = slice(a * 128, a * 128 + 128)
    normed = layer_norm(hidden[rows])
    yield
    for tile in range(9):
        columns = slice(tile * 256, tile * 256 + 256)
        three[rows, columns] = dot(normed, qkv_ref[:, columns]).astype(bf16)
        yield
    first = lax.broadcasted_iota(jnp.int32, (128, 128), 1) < 64
    none = jnp.zeros((128, 128), bf16)
    ones = jnp.concatenate([jnp.where(first, 1.0, 0.0), jnp.where(first, 0.0, 1.0)], 0).astype(bf16)
    for pair in range(PAIRS):
        columns = slice(pair * 128, pair * 128 + 128)
        query, keys, values = [
            three[rows, D * n + pair * 128 : D * n + pair * 128 + 128] for n in range(3)
        ]
        keys = jnp.concatenate([jnp.where(first, keys, none), jnp.where(first, none, keys)], 0)
        values = values * (1.0 / SHRINK)
        values = jnp.concatenate([jnp.where(first, values, none), jnp.where(first, none, values)], 0)
        weights = jnp.exp(dot_t(query, keys) * 0.125).astype(bf16)
        result = dot(weights, jnp.concatenate([values, ones], 1))
        mixed[rows, columns] = (result[:, :128] * (1.0 / result[:, 128:]) * SHRINK).astype(bf16)
        yield
    for tile in range(3):
        columns = slice(tile * 256, tile * 256 + 256)
        branch = dot(mixed[rows], out_ref[:, columns]).astype(bf16)
        hidden[rows, columns] = hidden[rows, columns] + branch.astype(f32)
        yield


def feed_forward(a, hidden, up_ref, down_ref, out_ref, upper):
    rows = slice(a * 128, a * 128 + 128)
    normed = layer_norm(hidden[rows])
    yield
    for tile in range(FF // 256):
        columns = slice(tile * 256, tile * 256 + 256)
        values = jax.nn.gelu(dot(normed, up_ref[:, columns]), approximate=True)
        upper[rows, columns] = values.astype(bf16)
        yield
    for tile in range(3):
        columns = slice(tile * 256, tile * 256 + 256)
        total = (hidden[rows, columns] + dot(upper[rows], down_ref[:, columns])).astype(bf16)
        for j in range(8):
            start = j * 32 + a * 16
            out_ref[start : start + 16, columns] = total[j * 16 : j * 16 + 16]
        yield


def staggered(chains, lag):
    lead, trail = chains
    for _ in range(lag):
        next(lead, None)
    while True:
        done = [next(lead, "end"), next(trail, "end")]
        if done == ["end", "end"]:
            break


X_LAG = 0
Y_LAG = 0


def x_kernel(slots_ref, sum_ref, qkv_ref, outw_ref, order_ref, out_ref, hidden, three, mixed):
    slots = slots_ref[...].reshape(NXL * SLOTS, D)

    def chain(a):
        rows = slice(a * 128, a * 128 + 128)
        hidden[rows] = dot(sum_ref[rows], slots)
        yield from attention(a, hidden, qkv_ref, outw_ref, three, mixed)

    staggered([chain(0), chain(1)], X_LAG)
    tokens = dot(order_ref[...], hidden[...].astype(bf16)).astype(bf16)
    out_ref[...] = tokens.reshape(128, 2, D)


def y_kernel(
    tokens_ref,
    split_ref,
    qkv_ref,
    outw_ref,
    up_ref,
    down_ref,
    out_ref,
    hidden,
    three,
    mixed,
    upper,
):
    tokens = tokens_ref[...].reshape(TOK, D)

    def chain(a):
        rows = slice(a * 128, a * 128 + 128)
        hidden[rows] = dot(split_ref[rows], tokens)
        yield from attention(a, hidden, qkv_ref, outw_ref, three, mixed)
        yield from feed_forward(a, hidden, up_ref, down_ref, out_ref, upper)

    staggered([chain(0), chain(1)], Y_LAG)


def home_kernel(tokens_ref, order_ref, out_ref):
    out_ref[...] = dot(order_ref[...], tokens_ref[...]).astype(bf16)


def whole(kernel, out_shape, scratch, flops, limit):
    space = pl.BlockSpec(memory_space=pltpu.VMEM)

    def call(*operands):
        size = sum(x.size * x.dtype.itemsize for x in operands)
        return pl.pallas_call(
            kernel,
            out_shape=out_shape,
            in_specs=[space] * len(operands),
            out_specs=[space] * len(out_shape) if isinstance(out_shape, list) else space,
            scratch_shapes=scratch,
            compiler_params=pltpu.CompilerParams(vmem_limit_bytes=limit << 20),
            cost_estimate=pl.CostEstimate(flops=flops, bytes_accessed=size, transcendentals=0),
        )(*operands)

    return call


def like(shape, kind=bf16):
    return jax.ShapeDtypeStruct(shape, kind)


def prepare(fields):
    space = pl.BlockSpec(memory_space=pltpu.VMEM)
    return pl.pallas_call(
        prep_kernel,
        in_specs=[pl.BlockSpec(memory_space=pltpu.HBM)],
        out_specs=[space] * 3,
        out_shape=[
            like((NF, ZS, CX + 2 * PADX, CY), f32),
            like((40, R, 128), f32),
            like((40, R, 128), f32),
        ],
        scratch_shapes=[
            pltpu.VMEM((NF, ZS + 2 * R, CX, CY), f32),
            pltpu.SemaphoreType.DMA((NF,)),
        ],
        compiler_params=pltpu.CompilerParams(vmem_limit_bytes=49 << 20),
    )(fields)


def shards(fields, embed_weight, qkv_weight, out_weight, up_weight, down_weight):
    count = lax.axis_size("gy")
    smooth, upper, lower = prepare(fields)
    upper = lax.ppermute(upper, "gy", [(i, (i + 1) % count) for i in range(count)])
    lower = lax.ppermute(lower, "gy", [((i + 1) % count, i) for i in range(count)])
    slots = like((16 * SLOTS // 4, 4, D))
    inner, base, edge, weight = whole(
        main_kernel,
        [slots, like((2, 24, D), f32), like((20, 24, 128), f32), like((KIN, D))],
        [
            pltpu.VMEM((NF, ZS, 80, CY), f32),
            pltpu.VMEM((NF, ZS, 80, CY), f32),
            pltpu.VMEM((ALL_ROWS, KIN), bf16),
            pltpu.VMEM((ALL_ROWS, D), f32),
            pltpu.VMEM((6, HI_ROWS, 128), f32),
            pltpu.VMEM((ALL_ROWS, D), bf16),
        ],
        2 * 6400 * 256 * 256 + 2 * KIN * 256 * D + 2 * ALL_ROWS * KIN * D,
        18,
    )(smooth, embed_weight)
    slots = whole(
        edge_kernel,
        slots,
        [
            pltpu.VMEM((400, 128), f32),
            pltpu.VMEM((160, 128), f32),
            pltpu.VMEM((20, 24, 128), f32),
            pltpu.SemaphoreType.DMA(()),
        ],
        2 * 64 * KIN * D,
        8,
    )(upper, lower, strip_table(), edge, base, weight, inner)
    slots = lax.all_to_all(
        slots.reshape(NXL, SLOTS // 4, 4, D), "gx", split_axis=0, concat_axis=0, tiled=True
    ).reshape(NXL * SLOTS // 4, 4, D)
    attention = [
        pltpu.VMEM((TOK, D), f32),
        pltpu.VMEM((TOK, 3 * D), bf16),
        pltpu.VMEM((TOK, D), bf16),
    ]
    tokens = whole(x_kernel, like((128, 2, D)), attention, 2 * TOK * D * 4 * D, 10)(
        slots, gather_sum(), qkv_weight, out_weight, interleave()
    )
    tokens = lax.all_to_all(
        tokens, ("gx", "gy"), split_axis=0, concat_axis=0, tiled=True
    )
    tokens = whole(
        y_kernel,
        like((TOK, D)),
        attention + [pltpu.VMEM((TOK, FF), bf16)],
        2 * TOK * D * (4 * D + 2 * FF),
        14,
    )(tokens, separate(), qkv_weight, out_weight, up_weight, down_weight)
    tokens = lax.all_to_all(
        tokens.reshape(8, 32, D), "gy", split_axis=0, concat_axis=0, tiled=True
    ).reshape(TOK, D)
    tokens = whole(home_kernel, like((TOK, D)), [], 2 * TOK * TOK * D, 8)(tokens, to_home())
    return tokens.reshape(2, 16, 8, D)


def solution(mesh):
    return jax.shard_map(
        shards,
        mesh=mesh,
        in_specs=(P(None, None, "gx", "gy"), P(), P(), P(), P(), P()),
        out_specs=P(None, "gy", "gx", None),
        check_vma=False,
    )
```

```python
import functools

import jax
import jax.numpy as jnp
import ml_dtypes
import numpy as np
from jax import lax
from jax.experimental import pallas as pl
from jax.experimental.pallas import tpu as pltpu
from jax.sharding import PartitionSpec as P

R = 4
NF = 5
ZS = 16
CX = 64
CY = 128
D = 768
FF = 3072
KIN = 2560
PAIRS = 6
NXL = 16
TOK = 256
EXT = 10
SLOTS = 28
BOUND = (0, 1, 8, 9)
HI_ROWS = EXT * 32
ALL_ROWS = HI_ROWS + 128
PADX = 16
SHRINK = 2.0**15
bf16 = jnp.bfloat16
f32 = jnp.float32


def np_taps():
    offsets = np.arange(-R, R + 1).astype(np.float32)
    values = np.exp(-offsets * offsets / np.float32(4.5)).astype(np.float32)
    return (values / values.sum(dtype=np.float32)).astype(np.float32)


TAPS = np_taps()


def as_bf16(values):
    return np.asarray(values, np.float32).astype(ml_dtypes.bfloat16)


def split_np(values):
    high = as_bf16(values)
    low = as_bf16(values - high.astype(np.float32))
    return high, low


def band_table():
    row = lax.broadcasted_iota(jnp.int32, (CY, CY), 0)
    column = lax.broadcasted_iota(jnp.int32, (CY, CY), 1)
    apart = jnp.abs(row - ((column & 15) * 8 + (column >> 4)))
    high = jnp.zeros((CY, CY), f32)
    low = jnp.zeros((CY, CY), f32)
    for k in range(R + 1):
        tap_hi, tap_lo = split_np(TAPS[R + k])
        high = jnp.where(apart == k, float(tap_hi), high)
        low = jnp.where(apart == k, float(tap_lo), low)
    left = jnp.concatenate([high, high], 0)
    right = jnp.concatenate([low, jnp.zeros_like(low)], 0)
    return jnp.concatenate([left, right], 1).astype(bf16)


def strip_table():
    table = np.zeros((384, 128), np.float32)
    for group in range(16):
        for x in range(8):
            for k in range(-R, R + 1):
                source = x + k + 8
                table[source // 8 * 128 + group * 8 + source % 8, group * 8 + x] = TAPS[R + k]
    high, low = split_np(table)
    return np.concatenate([high, high, low], 0)


def weight_order():
    row = lax.broadcasted_iota(jnp.int32, (256, 256), 0)
    column = lax.broadcasted_iota(jnp.int32, (256, 256), 1)
    return jnp.where(column == (row & 31) * 8 + (row >> 5), 1.0, 0.0).astype(bf16)


def permutation(rows, columns, source):
    table = np.zeros((rows, columns), np.float32)
    for row in range(rows):
        for column in source(row):
            table[row, column] = 1.0
    return as_bf16(table)


def message_order():
    row = lax.broadcasted_iota(jnp.int32, (ALL_ROWS, ALL_ROWS), 0)
    column = lax.broadcasted_iota(jnp.int32, (ALL_ROWS, ALL_ROWS), 1)
    slot, line = column >> 4, column & 15
    return jnp.where(row == line * SLOTS + slot, 1.0, 0.0).astype(bf16)


def gather_sum():
    low = {ext: 2 * EXT + 2 * n for n, ext in enumerate(BOUND)}

    def source(row):
        a, i, c = row // 128, row // 8 % 16, row % 8
        found = [i * SLOTS + (c + 1) * 2 + a]
        if c == 0:
            left = (i - 1) % NXL * SLOTS
            found += [i * SLOTS + low[1] + a, left + 18 + a, left + low[9] + a]
        if c == 7:
            right = (i + 1) % NXL * SLOTS
            found += [i * SLOTS + low[8] + a, right + a, right + low[0] + a]
        return found

    return permutation(TOK, NXL * SLOTS, source)


def interleave():
    return permutation(TOK, TOK, lambda r: [(r % 2) * 128 + r // 2])


def separate():
    return permutation(TOK, TOK, lambda r: [((r % 16) * 8 + r // 16 % 8) * 2 + r // 128])


def to_home():
    return permutation(TOK, TOK, lambda r: [(r % 8) * 32 + r // 8])


def dot(left, right):
    return lax.dot_general(left, right, (((1,), (0,)), ((), ())), preferred_element_type=f32)


def dot_split(left, table):
    high, low = halves(left)
    return dot(jnp.concatenate([high, low, high], 1), table)


def dot_t(left, right):
    return lax.dot_general(left, right, (((1,), (1,)), ((), ())), preferred_element_type=f32)


def halves(values):
    high = values.astype(bf16)
    return high, (values - high.astype(f32)).astype(bf16)


def prep_kernel(fields_ref, smooth_ref, upper_ref, lower_ref, cells, arrived):
    copies = [
        pltpu.make_async_copy(fields_ref.at[f], cells.at[f], arrived.at[f]) for f in range(NF)
    ]
    for copy in copies:
        copy.start()
    zero = jnp.zeros((NF, ZS, PADX, CY), f32)
    smooth_ref[:, :, 0:PADX] = zero
    smooth_ref[:, :, PADX + CX :] = zero

    def strip(index, block):
        turned = block.reshape(128, 128).T
        lower_ref[index] = turned[:R]
        upper_ref[index] = turned[CY - R :]

    for f in range(NF):
        copies[f].wait()
        for tile in range(CX // 8):
            rows = slice(tile * 8, tile * 8 + 8)
            plane = [cells[f, z, rows, :] for z in range(ZS + 2 * R)]
            for z in range(ZS):
                total = float(TAPS[R]) * plane[z + R]
                for k in range(1, R + 1):
                    total = total + float(TAPS[R + k]) * (plane[z + R - k] + plane[z + R + k])
                smooth_ref[f, z, PADX + tile * 8 : PADX + tile * 8 + 8, :] = total
        if f % 2 == 1:
            for a in range(2):
                for c in range(8):
                    rows = slice(PADX + c * 8, PADX + c * 8 + 8)
                    block = smooth_ref[f - 1 : f + 1, a * 8 : a * 8 + 8, rows, :]
                    strip((f // 2 * 2 + a) * 8 + c, block)
    for c in range(8):
        strip(32 + c, smooth_ref[NF - 1, :, PADX + c * 8 : PADX + c * 8 + 8, :])


CHUNKS = (0, 2, 1)
STRIDE = 2


def main_kernel(
    smooth_ref,
    weight_ref,
    out_ref,
    base_ref,
    edge_ref,
    order_ref,
    along,
    lhs,
    both,
    sums,
    mid,
):
    band = band_table()
    order = weight_order()
    first = lax.broadcasted_iota(jnp.int32, (16, 128), 1) < 64
    edge_ref[...] = jnp.zeros_like(edge_ref)

    def filtered(f):
        for part in range(8):
            planes = slice(part * 2, part * 2 + 2)
            found = []
            for z in range(part * 2, part * 2 + 2):
                total = float(TAPS[R]) * smooth_ref[f, z, PADX - 8 : PADX + 72, :]
                for k in range(1, R + 1):
                    total = total + float(TAPS[R + k]) * (
                        smooth_ref[f, z, PADX - 8 - k : PADX + 72 - k, :]
                        + smooth_ref[f, z, PADX - 8 + k : PADX + 72 + k, :]
                    )
                found.append(total)
            high, low = halves(jnp.concatenate(found, 0))
            pair = dot(jnp.concatenate([high, low], 1), band)
            along[f, planes] = (pair[:, :CY] + pair[:, CY:]).reshape(2, 80, CY)
            yield

    def reordered(f):
        for tile in (2 * f, 2 * f + 1):
            turned = dot(order, weight_ref[tile * 256 : tile * 256 + 256, :]).astype(bf16)
            for y in range(8):
                if tile < 8:
                    start = tile // 4 * 1024 + y * 128 + tile % 4 * 32
                else:
                    start = 2048 + y * 64 + (tile - 8) * 32
                order_ref[start : start + 32, :] = turned[y * 32 : y * 32 + 32]
            yield

    def put(ext, a, start, side, place, values):
        high = values.astype(bf16)
        rest = values - high.astype(f32)
        row = (ext * 2 + a) * 16
        lhs[row : row + 16, start : start + 128] = high
        if ext in BOUND:
            row = HI_ROWS + (BOUND.index(ext) * 2 + a) * 16
            lhs[row : row + 16, start : start + 128] = rest.astype(bf16)
        else:
            row = ext * 2 + a
            edge_ref[side * 10 + place, row : row + 1, :] = rest[side * 15 : side * 15 + 1]

    def produce(chunk):
        members = range(chunk * 2, min(chunk * 2 + 2, NF))
        for f in members:
            yield from filtered(f)
            yield from reordered(f)
        for ext in range(EXT):
            rows = slice(ext * 8, ext * 8 + 8)
            if len(members) == 2:
                for a in range(2):
                    block = along[members[0] : members[0] + 2, a * 8 : a * 8 + 8, rows, :]
                    turned = block.reshape(128, 128).T
                    for y in range(8):
                        values = turned[y * 16 : y * 16 + 16]
                        start = chunk * 1024 + y * 128
                        put(ext, a, start, y // 4, chunk * 4 + y % 4, values)
            else:
                turned = along[4, :, rows, :].reshape(128, 128).T
                for m in range(4):
                    even = turned[m * 32 : m * 32 + 16]
                    odd = turned[m * 32 + 16 : m * 32 + 32]
                    start, place = 2048 + m * 128, 8 + m % 2
                    put(ext, 0, start, m // 2, place, jnp.where(first, even, pltpu.roll(odd, 64, 1)))
                    put(ext, 1, start, m // 2, place, jnp.where(first, pltpu.roll(even, 64, 1), odd))
            yield

    def consume(chunk, fresh):
        deep = slice(chunk * 1024, min(chunk * 1024 + 1024, KIN))
        for tile in range(3):
            columns = slice(tile * 256, tile * 256 + 256)
            for rows in (slice(0, ALL_ROWS // 2), slice(ALL_ROWS // 2, ALL_ROWS)):
                part = dot(lhs[rows, deep], order_ref[deep, columns])
                both[rows, columns] = part if fresh else both[rows, columns] + part
                yield

    for _ in produce(CHUNKS[0]):
        pass
    for n, chunk in enumerate(CHUNKS):
        ahead = produce(CHUNKS[n + 1]) if n + 1 < len(CHUNKS) else iter(())
        for _ in consume(chunk, n == 0):
            for _ in range(STRIDE):
                next(ahead, None)
        for _ in ahead:
            pass
    for tile in range(6):
        columns = slice(tile * 128, tile * 128 + 128)
        for start, low in ((0, HI_ROWS), (256, HI_ROWS + 64)):
            rows, rest = slice(start, start + 64), slice(low, low + 64)
            total = both[rows, columns] + both[rest, columns]
            sums[tile, rows] = total
            mid[rows, columns], mid[rest, columns] = halves(total)
        total = both[64:256, columns]
        sums[tile, 64:256] = total
        mid[64:256, columns] = total.astype(bf16)
        for side in range(2):
            base_ref[side, 0 : 2 * EXT, columns] = sums[tile, pl.ds(side * 15, 2 * EXT, stride=16), :]
            base_ref[side, 2 * EXT :, columns] = jnp.zeros((4, 128), f32)
    slots = dot(message_order(), mid[...]).astype(bf16)
    out_ref[...] = slots.reshape(16 * SLOTS // 4, 4, D)


def edge_kernel(
    upper_ref,
    lower_ref,
    table_ref,
    edge_ref,
    base_ref,
    weight_ref,
    slots_ref,
    out_ref,
    parts,
    mixed,
    lhs,
    copied,
):
    inner = pl.ds(SLOTS // 4, 14 * SLOTS // 4)
    copy = pltpu.make_async_copy(slots_ref.at[inner], out_ref.at[inner], copied)
    copy.start()
    cells = jnp.concatenate([upper_ref[...], lower_ref[...]], 1).reshape(320, 128)
    place = lax.broadcasted_iota(jnp.int32, (320, 128), 0) & 7
    sums = jnp.zeros((320, 128), f32)
    for m in range(R):
        ahead = cells if m == 0 else pltpu.roll(cells, 320 - m, 0)
        behind = cells if m == 0 else pltpu.roll(cells, m, 0)
        used = jnp.where(place < R - m, ahead, jnp.where(place >= R + m, behind, 0.0))
        sums = sums + float(TAPS[2 * R - m]) * used
    none = jnp.zeros((16, 128), f32)
    blocks = []
    for group in range(5):
        tiles = sums[group * 64 : group * 64 + 64]
        blocks.append(
            jnp.concatenate(
                [
                    jnp.concatenate([none, tiles], 0),
                    jnp.concatenate([none[:8], tiles, none[:8]], 0),
                    jnp.concatenate([tiles, none], 0),
                ],
                1,
            )
        )
    high, low = halves(jnp.concatenate(blocks, 0))
    parts[...] = dot(jnp.concatenate([high, low, high], 1), table_ref[...])
    last = parts[320:]
    first = lax.broadcasted_iota(jnp.int32, (80, 128), 1) < 64
    rolled = pltpu.roll(last, 64, 1)
    mixed[0:80] = jnp.where(first, last, pltpu.roll(rolled, 79, 0))
    mixed[80:160] = jnp.where(first, rolled, pltpu.roll(last, 79, 0))
    lhs[...] = edge_ref[...]
    for side in range(2):
        for a in range(2):
            rows = pl.ds(a, EXT, stride=2)
            for pair in range(2):
                for q in range(4):
                    columns = slice(pair * 512 + q * 128, pair * 512 + q * 128 + 128)
                    found = parts[pl.ds((pair * 2 + a) * 80 + side * 4 + q, EXT, stride=8), :]
                    lhs[side * 10 + pair * 4 + q, rows] += found
            for q in range(2):
                found = mixed[pl.ds(a * 80 + side * 4 + q * 2, EXT, stride=8), :]
                lhs[side * 10 + 8 + q, rows] += found
    for side in range(2):
        result = base_ref[side]
        values = jnp.concatenate([lhs[side * 10 + n] for n in range(10)], 1)
        high, low = halves(values)
        values = jnp.concatenate([high.astype(f32), low.astype(f32)], 0).astype(bf16)
        for first_lane, start, count in (
            (0, side * 512, 512),
            (512, 1024 + side * 512, 512),
            (1024, 2048 + side * 256, 256),
        ):
            part = dot(values[:, first_lane : first_lane + count], weight_ref[start : start + count, :])
            result = result + (part[:24] + part[24:])
        high = result.astype(bf16).astype(f32)
        low = result - high
        slots = jnp.concatenate([high[: 2 * EXT], low[:4], low[16 : 2 * EXT]], 0).astype(bf16)
        row = side * 15 * SLOTS // 4
        out_ref[row : row + SLOTS // 4] = slots.reshape(SLOTS // 4, 4, D)
    copy.wait()


def layer_norm(hidden):
    center = hidden - jnp.mean(hidden, axis=-1, keepdims=True)
    spread = jnp.mean(center * center, axis=-1, keepdims=True)
    return (center * lax.rsqrt(spread + 1e-05)).astype(bf16)


def attention(a, hidden, qkv_ref, out_ref, three, mixed):
    rows = slice(a * 128, a * 128 + 128)
    normed = layer_norm(hidden[rows])
    yield
    for tile in range(9):
        columns = slice(tile * 256, tile * 256 + 256)
        three[rows, columns] = dot(normed, qkv_ref[:, columns]).astype(bf16)
        yield
    first = lax.broadcasted_iota(jnp.int32, (128, 128), 1) < 64
    none = jnp.zeros((128, 128), bf16)
    ones = jnp.concatenate([jnp.where(first, 1.0, 0.0), jnp.where(first, 0.0, 1.0)], 0).astype(bf16)
    for pair in range(PAIRS):
        columns = slice(pair * 128, pair * 128 + 128)
        query, keys, values = [
            three[rows, D * n + pair * 128 : D * n + pair * 128 + 128] for n in range(3)
        ]
        keys = jnp.concatenate([jnp.where(first, keys, none), jnp.where(first, none, keys)], 0)
        values = values * (1.0 / SHRINK)
        values = jnp.concatenate([jnp.where(first, values, none), jnp.where(first, none, values)], 0)
        weights = jnp.exp(dot_t(query, keys) * 0.125).astype(bf16)
        result = dot(weights, jnp.concatenate([values, ones], 1))
        mixed[rows, columns] = (result[:, :128] * (1.0 / result[:, 128:]) * SHRINK).astype(bf16)
        yield
    for tile in range(3):
        columns = slice(tile * 256, tile * 256 + 256)
        branch = dot(mixed[rows], out_ref[:, columns]).astype(bf16)
        hidden[rows, columns] = hidden[rows, columns] + branch.astype(f32)
        yield


def feed_forward(a, hidden, up_ref, down_ref, out_ref, upper):
    rows = slice(a * 128, a * 128 + 128)
    normed = layer_norm(hidden[rows])
    yield
    for tile in range(FF // 256):
        columns = slice(tile * 256, tile * 256 + 256)
        values = jax.nn.gelu(dot(normed, up_ref[:, columns]), approximate=True)
        upper[rows, columns] = values.astype(bf16)
        yield
    for tile in range(3):
        columns = slice(tile * 256, tile * 256 + 256)
        total = (hidden[rows, columns] + dot(upper[rows], down_ref[:, columns])).astype(bf16)
        for j in range(8):
            start = j * 32 + a * 16
            out_ref[start : start + 16, columns] = total[j * 16 : j * 16 + 16]
        yield


def staggered(chains, lag):
    lead, trail = chains
    for _ in range(lag):
        next(lead, None)
    while True:
        done = [next(lead, "end"), next(trail, "end")]
        if done == ["end", "end"]:
            break


X_LAG = 0
Y_LAG = 0


def x_kernel(slots_ref, sum_ref, qkv_ref, outw_ref, order_ref, out_ref, hidden, three, mixed):
    slots = slots_ref[...].reshape(NXL * SLOTS, D)

    def chain(a):
        rows = slice(a * 128, a * 128 + 128)
        hidden[rows] = dot(sum_ref[rows], slots)
        yield from attention(a, hidden, qkv_ref, outw_ref, three, mixed)

    staggered([chain(0), chain(1)], X_LAG)
    tokens = dot(order_ref[...], hidden[...].astype(bf16)).astype(bf16)
    out_ref[...] = tokens.reshape(128, 2, D)


def y_kernel(
    tokens_ref,
    split_ref,
    qkv_ref,
    outw_ref,
    up_ref,
    down_ref,
    out_ref,
    hidden,
    three,
    mixed,
    upper,
):
    tokens = tokens_ref[...].reshape(TOK, D)

    def chain(a):
        rows = slice(a * 128, a * 128 + 128)
        hidden[rows] = dot(split_ref[rows], tokens)
        yield from attention(a, hidden, qkv_ref, outw_ref, three, mixed)
        yield from feed_forward(a, hidden, up_ref, down_ref, out_ref, upper)

    staggered([chain(0), chain(1)], Y_LAG)


def home_kernel(tokens_ref, order_ref, out_ref):
    out_ref[...] = dot(order_ref[...], tokens_ref[...]).astype(bf16)


def whole(kernel, out_shape, scratch, flops, limit):
    space = pl.BlockSpec(memory_space=pltpu.VMEM)

    def call(*operands):
        size = sum(x.size * x.dtype.itemsize for x in operands)
        return pl.pallas_call(
            kernel,
            out_shape=out_shape,
            in_specs=[space] * len(operands),
            out_specs=[space] * len(out_shape) if isinstance(out_shape, list) else space,
            scratch_shapes=scratch,
            compiler_params=pltpu.CompilerParams(vmem_limit_bytes=limit << 20),
            cost_estimate=pl.CostEstimate(flops=flops, bytes_accessed=size, transcendentals=0),
        )(*operands)

    return call


def like(shape, kind=bf16):
    return jax.ShapeDtypeStruct(shape, kind)


def prepare(fields):
    space = pl.BlockSpec(memory_space=pltpu.VMEM)
    return pl.pallas_call(
        prep_kernel,
        in_specs=[pl.BlockSpec(memory_space=pltpu.HBM)],
        out_specs=[space] * 3,
        out_shape=[
            like((NF, ZS, CX + 2 * PADX, CY), f32),
            like((40, R, 128), f32),
            like((40, R, 128), f32),
        ],
        scratch_shapes=[
            pltpu.VMEM((NF, ZS + 2 * R, CX, CY), f32),
            pltpu.SemaphoreType.DMA((NF,)),
        ],
        compiler_params=pltpu.CompilerParams(vmem_limit_bytes=49 << 20),
    )(fields)


def shards(fields, embed_weight, qkv_weight, out_weight, up_weight, down_weight):
    count = lax.axis_size("gy")
    smooth, upper, lower = prepare(fields)
    upper = lax.ppermute(upper, "gy", [(i, (i + 1) % count) for i in range(count)])
    lower = lax.ppermute(lower, "gy", [((i + 1) % count, i) for i in range(count)])
    slots = like((16 * SLOTS // 4, 4, D))
    inner, base, edge, weight = whole(
        main_kernel,
        [slots, like((2, 24, D), f32), like((20, 24, 128), f32), like((KIN, D))],
        [
            pltpu.VMEM((NF, ZS, 80, CY), f32),
            pltpu.VMEM((ALL_ROWS, KIN), bf16),
            pltpu.VMEM((ALL_ROWS, D), f32),
            pltpu.VMEM((6, HI_ROWS, 128), f32),
            pltpu.VMEM((ALL_ROWS, D), bf16),
        ],
        2 * 6400 * 256 * 256 + 2 * KIN * 256 * D + 2 * ALL_ROWS * KIN * D,
        18,
    )(smooth, embed_weight)
    slots = whole(
        edge_kernel,
        slots,
        [
            pltpu.VMEM((400, 128), f32),
            pltpu.VMEM((160, 128), f32),
            pltpu.VMEM((20, 24, 128), f32),
            pltpu.SemaphoreType.DMA(()),
        ],
        2 * 64 * KIN * D,
        8,
    )(upper, lower, strip_table(), edge, base, weight, inner)
    slots = lax.all_to_all(
        slots.reshape(NXL, SLOTS // 4, 4, D), "gx", split_axis=0, concat_axis=0, tiled=True
    ).reshape(NXL * SLOTS // 4, 4, D)
    attention = [
        pltpu.VMEM((TOK, D), f32),
        pltpu.VMEM((TOK, 3 * D), bf16),
        pltpu.VMEM((TOK, D), bf16),
    ]
    tokens = whole(x_kernel, like((128, 2, D)), attention, 2 * TOK * D * 4 * D, 10)(
        slots, gather_sum(), qkv_weight, out_weight, interleave()
    )
    tokens = lax.all_to_all(
        tokens, ("gx", "gy"), split_axis=0, concat_axis=0, tiled=True
    )
    tokens = whole(
        y_kernel,
        like((TOK, D)),
        attention + [pltpu.VMEM((TOK, FF), bf16)],
        2 * TOK * D * (4 * D + 2 * FF),
        14,
    )(tokens, separate(), qkv_weight, out_weight, up_weight, down_weight)
    tokens = lax.all_to_all(
        tokens.reshape(8, 32, D), "gy", split_axis=0, concat_axis=0, tiled=True
    ).reshape(TOK, D)
    tokens = whole(home_kernel, like((TOK, D)), [], 2 * TOK * TOK * D, 8)(tokens, to_home())
    return tokens.reshape(2, 16, 8, D)


def solution(mesh):
    return jax.shard_map(
        shards,
        mesh=mesh,
        in_specs=(P(None, None, "gx", "gy"), P(), P(), P(), P(), P()),
        out_specs=P(None, "gy", "gx", None),
        check_vma=False,
    )
```

```python
import functools

import jax
import jax.numpy as jnp
import ml_dtypes
import numpy as np
from jax import lax
from jax.experimental import pallas as pl
from jax.experimental.pallas import tpu as pltpu
from jax.sharding import PartitionSpec as P

R = 4
NF = 5
ZS = 16
CX = 64
CY = 128
D = 768
FF = 3072
KIN = 2560
PAIRS = 6
NXL = 16
TOK = 256
EXT = 10
SLOTS = 28
BOUND = (0, 1, 8, 9)
HI_ROWS = EXT * 32
ALL_ROWS = HI_ROWS + 128
PADX = 16
SHRINK = 2.0**15
bf16 = jnp.bfloat16
f32 = jnp.float32


def np_taps():
    offsets = np.arange(-R, R + 1).astype(np.float32)
    values = np.exp(-offsets * offsets / np.float32(4.5)).astype(np.float32)
    return (values / values.sum(dtype=np.float32)).astype(np.float32)


TAPS = np_taps()


def as_bf16(values):
    return np.asarray(values, np.float32).astype(ml_dtypes.bfloat16)


def split_np(values):
    high = as_bf16(values)
    low = as_bf16(values - high.astype(np.float32))
    return high, low


def band_table():
    row = lax.broadcasted_iota(jnp.int32, (CY, CY), 0)
    column = lax.broadcasted_iota(jnp.int32, (CY, CY), 1)
    apart = jnp.abs(row - ((column & 15) * 8 + (column >> 4)))
    high = jnp.zeros((CY, CY), f32)
    low = jnp.zeros((CY, CY), f32)
    for k in range(R + 1):
        tap_hi, tap_lo = split_np(TAPS[R + k])
        high = jnp.where(apart == k, float(tap_hi), high)
        low = jnp.where(apart == k, float(tap_lo), low)
    left = jnp.concatenate([high, high], 0)
    right = jnp.concatenate([low, jnp.zeros_like(low)], 0)
    return jnp.concatenate([left, right], 1).astype(bf16)


def strip_table():
    table = np.zeros((384, 128), np.float32)
    for group in range(16):
        for x in range(8):
            for k in range(-R, R + 1):
                source = x + k + 8
                table[source // 8 * 128 + group * 8 + source % 8, group * 8 + x] = TAPS[R + k]
    high, low = split_np(table)
    right = np.concatenate([low, np.zeros_like(low)], 0)
    return np.concatenate([np.concatenate([high, high], 0), right], 1)


def weight_order():
    row = lax.broadcasted_iota(jnp.int32, (256, 256), 0)
    column = lax.broadcasted_iota(jnp.int32, (256, 256), 1)
    return jnp.where(column == (row & 31) * 8 + (row >> 5), 1.0, 0.0).astype(bf16)


def permutation(rows, columns, source):
    table = np.zeros((rows, columns), np.float32)
    for row in range(rows):
        for column in source(row):
            table[row, column] = 1.0
    return as_bf16(table)


def message_order():
    row = lax.broadcasted_iota(jnp.int32, (ALL_ROWS, ALL_ROWS), 0)
    column = lax.broadcasted_iota(jnp.int32, (ALL_ROWS, ALL_ROWS), 1)
    slot, line = column >> 4, column & 15
    return jnp.where(row == line * SLOTS + slot, 1.0, 0.0).astype(bf16)


def gather_sum():
    low = {ext: 2 * EXT + 2 * n for n, ext in enumerate(BOUND)}

    def source(row):
        a, i, c = row // 128, row // 8 % 16, row % 8
        found = [i * SLOTS + (c + 1) * 2 + a]
        if c == 0:
            left = (i - 1) % NXL * SLOTS
            found += [i * SLOTS + low[1] + a, left + 18 + a, left + low[9] + a]
        if c == 7:
            right = (i + 1) % NXL * SLOTS
            found += [i * SLOTS + low[8] + a, right + a, right + low[0] + a]
        return found

    return permutation(TOK, NXL * SLOTS, source)


def interleave():
    return permutation(TOK, TOK, lambda r: [(r % 2) * 128 + r // 2])


def separate():
    return permutation(TOK, TOK, lambda r: [((r % 16) * 8 + r // 16 % 8) * 2 + r // 128])


def to_home():
    return permutation(TOK, TOK, lambda r: [(r % 8) * 32 + r // 8])


def dot(left, right):
    return lax.dot_general(left, right, (((1,), (0,)), ((), ())), preferred_element_type=f32)


def dot_split(left, table):
    high, low = halves(left)
    return dot(jnp.concatenate([high, low, high], 1), table)


def dot_t(left, right):
    return lax.dot_general(left, right, (((1,), (1,)), ((), ())), preferred_element_type=f32)


def halves(values):
    high = values.astype(bf16)
    return high, (values - high.astype(f32)).astype(bf16)


def prep_kernel(fields_ref, smooth_ref, upper_ref, lower_ref, cells, arrived):
    copies = [
        pltpu.make_async_copy(fields_ref.at[f], cells.at[f], arrived.at[f]) for f in range(NF)
    ]
    for copy in copies:
        copy.start()
    zero = jnp.zeros((NF, ZS, PADX, CY), f32)
    smooth_ref[:, :, 0:PADX] = zero
    smooth_ref[:, :, PADX + CX :] = zero

    def strip(index, block):
        turned = block.reshape(128, 128).T
        lower_ref[index] = turned[:R]
        upper_ref[index] = turned[CY - R :]

    for f in range(NF):
        copies[f].wait()
        for tile in range(CX // 8):
            rows = slice(tile * 8, tile * 8 + 8)
            plane = [cells[f, z, rows, :] for z in range(ZS + 2 * R)]
            for z in range(ZS):
                total = float(TAPS[R]) * plane[z + R]
                for k in range(1, R + 1):
                    total = total + float(TAPS[R + k]) * (plane[z + R - k] + plane[z + R + k])
                smooth_ref[f, z, PADX + tile * 8 : PADX + tile * 8 + 8, :] = total
        if f % 2 == 1:
            for a in range(2):
                for c in range(8):
                    rows = slice(PADX + c * 8, PADX + c * 8 + 8)
                    block = smooth_ref[f - 1 : f + 1, a * 8 : a * 8 + 8, rows, :]
                    strip((f // 2 * 2 + a) * 8 + c, block)
    for c in range(8):
        strip(32 + c, smooth_ref[NF - 1, :, PADX + c * 8 : PADX + c * 8 + 8, :])


CHUNKS = (0, 2, 1)
STRIDE = 2


def main_kernel(
    smooth_ref,
    weight_ref,
    out_ref,
    base_ref,
    edge_ref,
    order_ref,
    along,
    lhs,
    both,
    sums,
    mid,
):
    band = band_table()
    order = weight_order()
    first = lax.broadcasted_iota(jnp.int32, (16, 128), 1) < 64
    edge_ref[...] = jnp.zeros_like(edge_ref)

    def filtered(f):
        for part in range(8):
            planes = slice(part * 2, part * 2 + 2)
            found = []
            for z in range(part * 2, part * 2 + 2):
                total = float(TAPS[R]) * smooth_ref[f, z, PADX - 8 : PADX + 72, :]
                for k in range(1, R + 1):
                    total = total + float(TAPS[R + k]) * (
                        smooth_ref[f, z, PADX - 8 - k : PADX + 72 - k, :]
                        + smooth_ref[f, z, PADX - 8 + k : PADX + 72 + k, :]
                    )
                found.append(total)
            high, low = halves(jnp.concatenate(found, 0))
            pair = dot(jnp.concatenate([high, low], 1), band)
            along[f, planes] = (pair[:, :CY] + pair[:, CY:]).reshape(2, 80, CY)
            yield

    def reordered(f):
        for tile in (2 * f, 2 * f + 1):
            turned = dot(order, weight_ref[tile * 256 : tile * 256 + 256, :]).astype(bf16)
            for y in range(8):
                if tile < 8:
                    start = tile // 4 * 1024 + y * 128 + tile % 4 * 32
                else:
                    start = 2048 + y * 64 + (tile - 8) * 32
                order_ref[start : start + 32, :] = turned[y * 32 : y * 32 + 32]
            yield

    def put(ext, a, start, side, place, values):
        high = values.astype(bf16)
        rest = values - high.astype(f32)
        row = (ext * 2 + a) * 16
        lhs[row : row + 16, start : start + 128] = high
        if ext in BOUND:
            row = HI_ROWS + (BOUND.index(ext) * 2 + a) * 16
            lhs[row : row + 16, start : start + 128] = rest.astype(bf16)
        else:
            row = ext * 2 + a
            edge_ref[side * 10 + place, row : row + 1, :] = rest[side * 15 : side * 15 + 1]

    def produce(chunk):
        members = range(chunk * 2, min(chunk * 2 + 2, NF))
        for f in members:
            yield from filtered(f)
            yield from reordered(f)
        for ext in range(EXT):
            rows = slice(ext * 8, ext * 8 + 8)
            if len(members) == 2:
                for a in range(2):
                    block = along[members[0] : members[0] + 2, a * 8 : a * 8 + 8, rows, :]
                    turned = block.reshape(128, 128).T
                    for y in range(8):
                        values = turned[y * 16 : y * 16 + 16]
                        start = chunk * 1024 + y * 128
                        put(ext, a, start, y // 4, chunk * 4 + y % 4, values)
            else:
                turned = along[4, :, rows, :].reshape(128, 128).T
                for m in range(4):
                    even = turned[m * 32 : m * 32 + 16]
                    odd = turned[m * 32 + 16 : m * 32 + 32]
                    start, place = 2048 + m * 128, 8 + m % 2
                    put(ext, 0, start, m // 2, place, jnp.where(first, even, pltpu.roll(odd, 64, 1)))
                    put(ext, 1, start, m // 2, place, jnp.where(first, pltpu.roll(even, 64, 1), odd))
            yield

    def consume(chunk, fresh):
        deep = slice(chunk * 1024, min(chunk * 1024 + 1024, KIN))
        for tile in range(3):
            columns = slice(tile * 256, tile * 256 + 256)
            for rows in (slice(0, ALL_ROWS // 2), slice(ALL_ROWS // 2, ALL_ROWS)):
                part = dot(lhs[rows, deep], order_ref[deep, columns])
                both[rows, columns] = part if fresh else both[rows, columns] + part
                yield

    for _ in produce(CHUNKS[0]):
        pass
    for n, chunk in enumerate(CHUNKS):
        ahead = produce(CHUNKS[n + 1]) if n + 1 < len(CHUNKS) else iter(())
        for _ in consume(chunk, n == 0):
            for _ in range(STRIDE):
                next(ahead, None)
        for _ in ahead:
            pass
    for tile in range(6):
        columns = slice(tile * 128, tile * 128 + 128)
        for start, low in ((0, HI_ROWS), (256, HI_ROWS + 64)):
            rows, rest = slice(start, start + 64), slice(low, low + 64)
            total = both[rows, columns] + both[rest, columns]
            sums[tile, rows] = total
            mid[rows, columns], mid[rest, columns] = halves(total)
        total = both[64:256, columns]
        sums[tile, 64:256] = total
        mid[64:256, columns] = total.astype(bf16)
        for side in range(2):
            base_ref[side, 0 : 2 * EXT, columns] = sums[tile, pl.ds(side * 15, 2 * EXT, stride=16), :]
            base_ref[side, 2 * EXT :, columns] = jnp.zeros((4, 128), f32)
    slots = dot(message_order(), mid[...]).astype(bf16)
    out_ref[...] = slots.reshape(16 * SLOTS // 4, 4, D)


def edge_kernel(
    upper_ref,
    lower_ref,
    table_ref,
    edge_ref,
    base_ref,
    weight_ref,
    slots_ref,
    out_ref,
    parts,
    mixed,
    lhs,
    copied,
):
    inner = pl.ds(SLOTS // 4, 14 * SLOTS // 4)
    copy = pltpu.make_async_copy(slots_ref.at[inner], out_ref.at[inner], copied)
    copy.start()
    cells = jnp.concatenate([upper_ref[...], lower_ref[...]], 1).reshape(320, 128)
    place = lax.broadcasted_iota(jnp.int32, (320, 128), 0) & 7
    sums = jnp.zeros((320, 128), f32)
    for m in range(R):
        ahead = cells if m == 0 else pltpu.roll(cells, 320 - m, 0)
        behind = cells if m == 0 else pltpu.roll(cells, m, 0)
        used = jnp.where(place < R - m, ahead, jnp.where(place >= R + m, behind, 0.0))
        sums = sums + float(TAPS[2 * R - m]) * used
    none = jnp.zeros((16, 128), f32)
    blocks = []
    for group in range(5):
        tiles = sums[group * 64 : group * 64 + 64]
        blocks.append(
            jnp.concatenate(
                [
                    jnp.concatenate([none, tiles], 0),
                    jnp.concatenate([none[:8], tiles, none[:8]], 0),
                    jnp.concatenate([tiles, none], 0),
                ],
                1,
            )
        )
    high, low = halves(jnp.concatenate(blocks, 0))
    pair = dot(jnp.concatenate([high, low], 1), table_ref[...])
    parts[...] = pair[:, :128] + pair[:, 128:]
    last = parts[320:]
    first = lax.broadcasted_iota(jnp.int32, (80, 128), 1) < 64
    rolled = pltpu.roll(last, 64, 1)
    mixed[0:80] = jnp.where(first, last, pltpu.roll(rolled, 79, 0))
    mixed[80:160] = jnp.where(first, rolled, pltpu.roll(last, 79, 0))
    lhs[...] = edge_ref[...]
    for side in range(2):
        for a in range(2):
            rows = pl.ds(a, EXT, stride=2)
            for pair in range(2):
                for q in range(4):
                    columns = slice(pair * 512 + q * 128, pair * 512 + q * 128 + 128)
                    found = parts[pl.ds((pair * 2 + a) * 80 + side * 4 + q, EXT, stride=8), :]
                    lhs[side * 10 + pair * 4 + q, rows] += found
            for q in range(2):
                found = mixed[pl.ds(a * 80 + side * 4 + q * 2, EXT, stride=8), :]
                lhs[side * 10 + 8 + q, rows] += found
    for side in range(2):
        result = base_ref[side]
        values = jnp.concatenate([lhs[side * 10 + n] for n in range(10)], 1)
        high, low = halves(values)
        values = jnp.concatenate([high.astype(f32), low.astype(f32)], 0).astype(bf16)
        for first_lane, start, count in (
            (0, side * 512, 512),
            (512, 1024 + side * 512, 512),
            (1024, 2048 + side * 256, 256),
        ):
            part = dot(values[:, first_lane : first_lane + count], weight_ref[start : start + count, :])
            result = result + (part[:24] + part[24:])
        high = result.astype(bf16).astype(f32)
        low = result - high
        slots = jnp.concatenate([high[: 2 * EXT], low[:4], low[16 : 2 * EXT]], 0).astype(bf16)
        row = side * 15 * SLOTS // 4
        out_ref[row : row + SLOTS // 4] = slots.reshape(SLOTS // 4, 4, D)
    copy.wait()


def layer_norm(hidden):
    center = hidden - jnp.mean(hidden, axis=-1, keepdims=True)
    spread = jnp.mean(center * center, axis=-1, keepdims=True)
    return (center * lax.rsqrt(spread + 1e-05)).astype(bf16)


def attention(a, hidden, qkv_ref, out_ref, three, mixed):
    rows = slice(a * 128, a * 128 + 128)
    normed = layer_norm(hidden[rows])
    yield
    for tile in range(9):
        columns = slice(tile * 256, tile * 256 + 256)
        three[rows, columns] = dot(normed, qkv_ref[:, columns]).astype(bf16)
        yield
    first = lax.broadcasted_iota(jnp.int32, (128, 128), 1) < 64
    none = jnp.zeros((128, 128), bf16)
    ones = jnp.concatenate([jnp.where(first, 1.0, 0.0), jnp.where(first, 0.0, 1.0)], 0).astype(bf16)
    for pair in range(PAIRS):
        columns = slice(pair * 128, pair * 128 + 128)
        query, keys, values = [
            three[rows, D * n + pair * 128 : D * n + pair * 128 + 128] for n in range(3)
        ]
        keys = jnp.concatenate([jnp.where(first, keys, none), jnp.where(first, none, keys)], 0)
        values = values * (1.0 / SHRINK)
        values = jnp.concatenate([jnp.where(first, values, none), jnp.where(first, none, values)], 0)
        weights = jnp.exp(dot_t(query, keys) * 0.125).astype(bf16)
        result = dot(weights, jnp.concatenate([values, ones], 1))
        mixed[rows, columns] = (result[:, :128] * (1.0 / result[:, 128:]) * SHRINK).astype(bf16)
        yield
    for tile in range(3):
        columns = slice(tile * 256, tile * 256 + 256)
        branch = dot(mixed[rows], out_ref[:, columns]).astype(bf16)
        hidden[rows, columns] = hidden[rows, columns] + branch.astype(f32)
        yield


def feed_forward(a, hidden, up_ref, down_ref, out_ref, upper):
    rows = slice(a * 128, a * 128 + 128)
    normed = layer_norm(hidden[rows])
    yield
    for tile in range(FF // 256):
        columns = slice(tile * 256, tile * 256 + 256)
        values = jax.nn.gelu(dot(normed, up_ref[:, columns]), approximate=True)
        upper[rows, columns] = values.astype(bf16)
        yield
    for tile in range(3):
        columns = slice(tile * 256, tile * 256 + 256)
        total = (hidden[rows, columns] + dot(upper[rows], down_ref[:, columns])).astype(bf16)
        for j in range(8):
            start = j * 32 + a * 16
            out_ref[start : start + 16, columns] = total[j * 16 : j * 16 + 16]
        yield


def staggered(chains, lag):
    lead, trail = chains
    for _ in range(lag):
        next(lead, None)
    while True:
        done = [next(lead, "end"), next(trail, "end")]
        if done == ["end", "end"]:
            break


X_LAG = 0
Y_LAG = 0


def x_kernel(slots_ref, sum_ref, qkv_ref, outw_ref, order_ref, out_ref, hidden, three, mixed):
    slots = slots_ref[...].reshape(NXL * SLOTS, D)

    def chain(a):
        rows = slice(a * 128, a * 128 + 128)
        hidden[rows] = dot(sum_ref[rows], slots)
        yield from attention(a, hidden, qkv_ref, outw_ref, three, mixed)

    staggered([chain(0), chain(1)], X_LAG)
    tokens = dot(order_ref[...], hidden[...].astype(bf16)).astype(bf16)
    out_ref[...] = tokens.reshape(128, 2, D)


def y_kernel(
    tokens_ref,
    split_ref,
    qkv_ref,
    outw_ref,
    up_ref,
    down_ref,
    out_ref,
    hidden,
    three,
    mixed,
    upper,
):
    tokens = tokens_ref[...].reshape(TOK, D)

    def chain(a):
        rows = slice(a * 128, a * 128 + 128)
        hidden[rows] = dot(split_ref[rows], tokens)
        yield from attention(a, hidden, qkv_ref, outw_ref, three, mixed)
        yield from feed_forward(a, hidden, up_ref, down_ref, out_ref, upper)

    staggered([chain(0), chain(1)], Y_LAG)


def home_kernel(tokens_ref, order_ref, out_ref):
    out_ref[...] = dot(order_ref[...], tokens_ref[...]).astype(bf16)


def whole(kernel, out_shape, scratch, flops, limit):
    space = pl.BlockSpec(memory_space=pltpu.VMEM)

    def call(*operands):
        size = sum(x.size * x.dtype.itemsize for x in operands)
        return pl.pallas_call(
            kernel,
            out_shape=out_shape,
            in_specs=[space] * len(operands),
            out_specs=[space] * len(out_shape) if isinstance(out_shape, list) else space,
            scratch_shapes=scratch,
            compiler_params=pltpu.CompilerParams(vmem_limit_bytes=limit << 20),
            cost_estimate=pl.CostEstimate(flops=flops, bytes_accessed=size, transcendentals=0),
        )(*operands)

    return call


def like(shape, kind=bf16):
    return jax.ShapeDtypeStruct(shape, kind)


def prepare(fields):
    space = pl.BlockSpec(memory_space=pltpu.VMEM)
    return pl.pallas_call(
        prep_kernel,
        in_specs=[pl.BlockSpec(memory_space=pltpu.HBM)],
        out_specs=[space] * 3,
        out_shape=[
            like((NF, ZS, CX + 2 * PADX, CY), f32),
            like((40, R, 128), f32),
            like((40, R, 128), f32),
        ],
        scratch_shapes=[
            pltpu.VMEM((NF, ZS + 2 * R, CX, CY), f32),
            pltpu.SemaphoreType.DMA((NF,)),
        ],
        compiler_params=pltpu.CompilerParams(vmem_limit_bytes=49 << 20),
    )(fields)


def shards(fields, embed_weight, qkv_weight, out_weight, up_weight, down_weight):
    count = lax.axis_size("gy")
    smooth, upper, lower = prepare(fields)
    upper = lax.ppermute(upper, "gy", [(i, (i + 1) % count) for i in range(count)])
    lower = lax.ppermute(lower, "gy", [((i + 1) % count, i) for i in range(count)])
    slots = like((16 * SLOTS // 4, 4, D))
    inner, base, edge, weight = whole(
        main_kernel,
        [slots, like((2, 24, D), f32), like((20, 24, 128), f32), like((KIN, D))],
        [
            pltpu.VMEM((NF, ZS, 80, CY), f32),
            pltpu.VMEM((ALL_ROWS, KIN), bf16),
            pltpu.VMEM((ALL_ROWS, D), f32),
            pltpu.VMEM((6, HI_ROWS, 128), f32),
            pltpu.VMEM((ALL_ROWS, D), bf16),
        ],
        2 * 6400 * 256 * 256 + 2 * KIN * 256 * D + 2 * ALL_ROWS * KIN * D,
        18,
    )(smooth, embed_weight)
    slots = whole(
        edge_kernel,
        slots,
        [
            pltpu.VMEM((400, 128), f32),
            pltpu.VMEM((160, 128), f32),
            pltpu.VMEM((20, 24, 128), f32),
            pltpu.SemaphoreType.DMA(()),
        ],
        2 * 64 * KIN * D,
        8,
    )(upper, lower, strip_table(), edge, base, weight, inner)
    slots = lax.all_to_all(
        slots.reshape(NXL, SLOTS // 4, 4, D), "gx", split_axis=0, concat_axis=0, tiled=True
    ).reshape(NXL * SLOTS // 4, 4, D)
    attention = [
        pltpu.VMEM((TOK, D), f32),
        pltpu.VMEM((TOK, 3 * D), bf16),
        pltpu.VMEM((TOK, D), bf16),
    ]
    tokens = whole(x_kernel, like((128, 2, D)), attention, 2 * TOK * D * 4 * D, 10)(
        slots, gather_sum(), qkv_weight, out_weight, interleave()
    )
    tokens = lax.all_to_all(
        tokens, ("gx", "gy"), split_axis=0, concat_axis=0, tiled=True
    )
    tokens = whole(
        y_kernel,
        like((TOK, D)),
        attention + [pltpu.VMEM((TOK, FF), bf16)],
        2 * TOK * D * (4 * D + 2 * FF),
        14,
    )(tokens, separate(), qkv_weight, out_weight, up_weight, down_weight)
    tokens = lax.all_to_all(
        tokens.reshape(8, 32, D), "gy", split_axis=0, concat_axis=0, tiled=True
    ).reshape(TOK, D)
    tokens = whole(home_kernel, like((TOK, D)), [], 2 * TOK * TOK * D, 8)(tokens, to_home())
    return tokens.reshape(2, 16, 8, D)


def solution(mesh):
    return jax.shard_map(
        shards,
        mesh=mesh,
        in_specs=(P(None, None, "gx", "gy"), P(), P(), P(), P(), P()),
        out_specs=P(None, "gy", "gx", None),
        check_vma=False,
    )
```

```python
import functools

import jax
import jax.numpy as jnp
import ml_dtypes
import numpy as np
from jax import lax
from jax.experimental import pallas as pl
from jax.experimental.pallas import tpu as pltpu
from jax.sharding import PartitionSpec as P

R = 4
NF = 5
ZS = 16
CX = 64
CY = 128
D = 768
FF = 3072
KIN = 2560
PAIRS = 6
NXL = 16
TOK = 256
EXT = 10
SLOTS = 28
BOUND = (0, 1, 8, 9)
HI_ROWS = EXT * 32
ALL_ROWS = HI_ROWS + 128
PADX = 16
SHRINK = 2.0**15
bf16 = jnp.bfloat16
f32 = jnp.float32


def np_taps():
    offsets = np.arange(-R, R + 1).astype(np.float32)
    values = np.exp(-offsets * offsets / np.float32(4.5)).astype(np.float32)
    return (values / values.sum(dtype=np.float32)).astype(np.float32)


TAPS = np_taps()


def as_bf16(values):
    return np.asarray(values, np.float32).astype(ml_dtypes.bfloat16)


def split_np(values):
    high = as_bf16(values)
    low = as_bf16(values - high.astype(np.float32))
    return high, low


def band_table():
    row = lax.broadcasted_iota(jnp.int32, (CY, CY), 0)
    column = lax.broadcasted_iota(jnp.int32, (CY, CY), 1)
    apart = jnp.abs(row - ((column & 15) * 8 + (column >> 4)))
    high = jnp.zeros((CY, CY), f32)
    low = jnp.zeros((CY, CY), f32)
    for k in range(R + 1):
        tap_hi, tap_lo = split_np(TAPS[R + k])
        high = jnp.where(apart == k, float(tap_hi), high)
        low = jnp.where(apart == k, float(tap_lo), low)
    left = jnp.concatenate([high, high], 0)
    right = jnp.concatenate([low, jnp.zeros_like(low)], 0)
    return jnp.concatenate([left, right], 1).astype(bf16)


def strip_table():
    table = np.zeros((384, 128), np.float32)
    for group in range(16):
        for x in range(8):
            for k in range(-R, R + 1):
                source = x + k + 8
                table[source // 8 * 128 + group * 8 + source % 8, group * 8 + x] = TAPS[R + k]
    high, low = split_np(table)
    right = np.concatenate([low, np.zeros_like(low)], 0)
    return np.concatenate([np.concatenate([high, high], 0), right], 1)


def weight_order():
    row = lax.broadcasted_iota(jnp.int32, (256, 256), 0)
    column = lax.broadcasted_iota(jnp.int32, (256, 256), 1)
    return jnp.where(column == (row & 31) * 8 + (row >> 5), 1.0, 0.0).astype(bf16)


def permutation(rows, columns, source):
    table = np.zeros((rows, columns), np.float32)
    for row in range(rows):
        for column in source(row):
            table[row, column] = 1.0
    return as_bf16(table)


def message_order():
    row = lax.broadcasted_iota(jnp.int32, (ALL_ROWS, ALL_ROWS), 0)
    column = lax.broadcasted_iota(jnp.int32, (ALL_ROWS, ALL_ROWS), 1)
    slot, line = column >> 4, column & 15
    return jnp.where(row == line * SLOTS + slot, 1.0, 0.0).astype(bf16)


def gather_sum():
    low = {ext: 2 * EXT + 2 * n for n, ext in enumerate(BOUND)}

    def source(row):
        a, i, c = row // 128, row // 8 % 16, row % 8
        found = [i * SLOTS + (c + 1) * 2 + a]
        if c == 0:
            left = (i - 1) % NXL * SLOTS
            found += [i * SLOTS + low[1] + a, left + 18 + a, left + low[9] + a]
        if c == 7:
            right = (i + 1) % NXL * SLOTS
            found += [i * SLOTS + low[8] + a, right + a, right + low[0] + a]
        return found

    return permutation(TOK, NXL * SLOTS, source)


def interleave():
    return permutation(TOK, TOK, lambda r: [(r % 2) * 128 + r // 2])


def separate():
    return permutation(TOK, TOK, lambda r: [((r % 16) * 8 + r // 16 % 8) * 2 + r // 128])


def to_home():
    return permutation(TOK, TOK, lambda r: [(r % 8) * 32 + r // 8])


def dot(left, right):
    return lax.dot_general(left, right, (((1,), (0,)), ((), ())), preferred_element_type=f32)


def dot_split(left, table):
    high, low = halves(left)
    return dot(jnp.concatenate([high, low, high], 1), table)


def dot_t(left, right):
    return lax.dot_general(left, right, (((1,), (1,)), ((), ())), preferred_element_type=f32)


def halves(values):
    high = values.astype(bf16)
    return high, (values - high.astype(f32)).astype(bf16)


def prep_kernel(fields_ref, smooth_ref, upper_ref, lower_ref, cells, arrived):
    copies = [
        pltpu.make_async_copy(fields_ref.at[f], cells.at[f], arrived.at[f]) for f in range(NF)
    ]
    for copy in copies:
        copy.start()
    zero = jnp.zeros((NF, ZS, PADX, CY), f32)
    smooth_ref[:, :, 0:PADX] = zero
    smooth_ref[:, :, PADX + CX :] = zero

    def strip(index, block):
        turned = block.reshape(128, 128).T
        lower_ref[index] = turned[:R]
        upper_ref[index] = turned[CY - R :]

    for f in range(NF):
        copies[f].wait()
        for tile in range(CX // 8):
            rows = slice(tile * 8, tile * 8 + 8)
            plane = [cells[f, z, rows, :] for z in range(ZS + 2 * R)]
            for z in range(ZS):
                total = float(TAPS[R]) * plane[z + R]
                for k in range(1, R + 1):
                    total = total + float(TAPS[R + k]) * (plane[z + R - k] + plane[z + R + k])
                smooth_ref[f, z, PADX + tile * 8 : PADX + tile * 8 + 8, :] = total
        if f % 2 == 1:
            for a in range(2):
                for c in range(8):
                    rows = slice(PADX + c * 8, PADX + c * 8 + 8)
                    block = smooth_ref[f - 1 : f + 1, a * 8 : a * 8 + 8, rows, :]
                    strip((f // 2 * 2 + a) * 8 + c, block)
    for c in range(8):
        strip(32 + c, smooth_ref[NF - 1, :, PADX + c * 8 : PADX + c * 8 + 8, :])


CHUNKS = (0, 2, 1)
STRIDE = 2


def main_kernel(
    smooth_ref,
    weight_ref,
    out_ref,
    base_ref,
    edge_ref,
    order_ref,
    along,
    lhs,
    both,
    sums,
    mid,
):
    band = band_table()
    order = weight_order()
    first = lax.broadcasted_iota(jnp.int32, (16, 128), 1) < 64
    edge_ref[...] = jnp.zeros_like(edge_ref)

    def filtered(f):
        for part in range(8):
            planes = slice(part * 2, part * 2 + 2)
            found = []
            for z in range(part * 2, part * 2 + 2):
                total = float(TAPS[R]) * smooth_ref[f, z, PADX - 8 : PADX + 72, :]
                for k in range(1, R + 1):
                    total = total + float(TAPS[R + k]) * (
                        smooth_ref[f, z, PADX - 8 - k : PADX + 72 - k, :]
                        + smooth_ref[f, z, PADX - 8 + k : PADX + 72 + k, :]
                    )
                found.append(total)
            high, low = halves(jnp.concatenate(found, 0))
            pair = dot(jnp.concatenate([high, low], 1), band)
            along[f, planes] = (pair[:, :CY] + pair[:, CY:]).reshape(2, 80, CY)
            yield

    def reordered(f):
        for tile in (2 * f, 2 * f + 1):
            turned = dot(order, weight_ref[tile * 256 : tile * 256 + 256, :]).astype(bf16)
            for y in range(8):
                if tile < 8:
                    start = tile // 4 * 1024 + y * 128 + tile % 4 * 32
                else:
                    start = 2048 + y * 64 + (tile - 8) * 32
                order_ref[start : start + 32, :] = turned[y * 32 : y * 32 + 32]
            yield

    def put(ext, a, start, side, place, values):
        high = values.astype(bf16)
        rest = values - high.astype(f32)
        row = (ext * 2 + a) * 16
        lhs[row : row + 16, start : start + 128] = high
        if ext in BOUND:
            row = HI_ROWS + (BOUND.index(ext) * 2 + a) * 16
            lhs[row : row + 16, start : start + 128] = rest.astype(bf16)
        else:
            row = ext * 2 + a
            edge_ref[side * 10 + place, row : row + 1, :] = rest[side * 15 : side * 15 + 1]

    def produce(chunk):
        members = range(chunk * 2, min(chunk * 2 + 2, NF))
        for f in members:
            yield from filtered(f)
            yield from reordered(f)
        for ext in range(EXT):
            rows = slice(ext * 8, ext * 8 + 8)
            if len(members) == 2:
                for a in range(2):
                    block = along[members[0] : members[0] + 2, a * 8 : a * 8 + 8, rows, :]
                    turned = block.reshape(128, 128).T
                    for y in range(8):
                        values = turned[y * 16 : y * 16 + 16]
                        start = chunk * 1024 + y * 128
                        put(ext, a, start, y // 4, chunk * 4 + y % 4, values)
            else:
                turned = along[4, :, rows, :].reshape(128, 128).T
                for m in range(4):
                    even = turned[m * 32 : m * 32 + 16]
                    odd = turned[m * 32 + 16 : m * 32 + 32]
                    start, place = 2048 + m * 128, 8 + m % 2
                    put(ext, 0, start, m // 2, place, jnp.where(first, even, pltpu.roll(odd, 64, 1)))
                    put(ext, 1, start, m // 2, place, jnp.where(first, pltpu.roll(even, 64, 1), odd))
            yield

    def consume(chunk, fresh):
        deep = slice(chunk * 1024, min(chunk * 1024 + 1024, KIN))
        for tile in range(3):
            columns = slice(tile * 256, tile * 256 + 256)
            for rows in (slice(0, ALL_ROWS // 2), slice(ALL_ROWS // 2, ALL_ROWS)):
                part = dot(lhs[rows, deep], order_ref[deep, columns])
                both[rows, columns] = part if fresh else both[rows, columns] + part
                yield

    for _ in produce(CHUNKS[0]):
        pass
    for n, chunk in enumerate(CHUNKS):
        ahead = produce(CHUNKS[n + 1]) if n + 1 < len(CHUNKS) else iter(())
        for _ in consume(chunk, n == 0):
            for _ in range(STRIDE):
                next(ahead, None)
        for _ in ahead:
            pass
    for tile in range(6):
        columns = slice(tile * 128, tile * 128 + 128)
        for start, low in ((0, HI_ROWS), (256, HI_ROWS + 64)):
            rows, rest = slice(start, start + 64), slice(low, low + 64)
            total = both[rows, columns] + both[rest, columns]
            sums[tile, rows] = total
            mid[rows, columns], mid[rest, columns] = halves(total)
        total = both[64:256, columns]
        sums[tile, 64:256] = total
        mid[64:256, columns] = total.astype(bf16)
        for side in range(2):
            base_ref[side, 0 : 2 * EXT, columns] = sums[tile, pl.ds(side * 15, 2 * EXT, stride=16), :]
            base_ref[side, 2 * EXT :, columns] = jnp.zeros((4, 128), f32)
    slots = dot(message_order(), mid[...]).astype(bf16)
    out_ref[...] = slots.reshape(16 * SLOTS // 4, 4, D)


def edge_kernel(
    upper_ref,
    lower_ref,
    table_ref,
    edge_ref,
    base_ref,
    weight_ref,
    slots_ref,
    out_ref,
    parts,
    mixed,
    lhs,
    copied,
):
    inner = pl.ds(SLOTS // 4, 14 * SLOTS // 4)
    copy = pltpu.make_async_copy(slots_ref.at[inner], out_ref.at[inner], copied)
    copy.start()
    cells = jnp.concatenate([upper_ref[...], lower_ref[...]], 1).reshape(320, 128)
    place = lax.broadcasted_iota(jnp.int32, (320, 128), 0) & 7
    sums = jnp.zeros((320, 128), f32)
    for m in range(R):
        ahead = cells if m == 0 else pltpu.roll(cells, 320 - m, 0)
        behind = cells if m == 0 else pltpu.roll(cells, m, 0)
        used = jnp.where(place < R - m, ahead, jnp.where(place >= R + m, behind, 0.0))
        sums = sums + float(TAPS[2 * R - m]) * used
    none = jnp.zeros((16, 128), f32)
    blocks = []
    for group in range(5):
        tiles = sums[group * 64 : group * 64 + 64]
        blocks.append(
            jnp.concatenate(
                [
                    jnp.concatenate([none, tiles], 0),
                    jnp.concatenate([none[:8], tiles, none[:8]], 0),
                    jnp.concatenate([tiles, none], 0),
                ],
                1,
            )
        )
    high, low = halves(jnp.concatenate(blocks, 0))
    pair = dot(jnp.concatenate([high, low], 1), table_ref[...])
    parts[...] = pair[:, :128] + pair[:, 128:]
    last = parts[320:]
    first = lax.broadcasted_iota(jnp.int32, (80, 128), 1) < 64
    rolled = pltpu.roll(last, 64, 1)
    mixed[0:80] = jnp.where(first, last, pltpu.roll(rolled, 79, 0))
    mixed[80:160] = jnp.where(first, rolled, pltpu.roll(last, 79, 0))
    lhs[:, 0:24] = edge_ref[...]
    for side in range(2):
        for a in range(2):
            rows = pl.ds(a, EXT, stride=2)
            for pair in range(2):
                for q in range(4):
                    columns = slice(pair * 512 + q * 128, pair * 512 + q * 128 + 128)
                    found = parts[pl.ds((pair * 2 + a) * 80 + side * 4 + q, EXT, stride=8), :]
                    lhs[side * 10 + pair * 4 + q, rows] += found
            for q in range(2):
                found = mixed[pl.ds(a * 80 + side * 4 + q * 2, EXT, stride=8), :]
                lhs[side * 10 + 8 + q, rows] += found
    for side in range(2):
        result = base_ref[side]
        values = jnp.concatenate([lhs[side * 10 + n, 0:24] for n in range(10)], 1)
        high, low = halves(values)
        values = jnp.concatenate([high.astype(f32), low.astype(f32)], 0).astype(bf16)
        for first_lane, start, count in (
            (0, side * 512, 512),
            (512, 1024 + side * 512, 512),
            (1024, 2048 + side * 256, 256),
        ):
            part = dot(values[:, first_lane : first_lane + count], weight_ref[start : start + count, :])
            result = result + (part[:24] + part[24:])
        high = result.astype(bf16).astype(f32)
        low = result - high
        slots = jnp.concatenate([high[: 2 * EXT], low[:4], low[16 : 2 * EXT]], 0).astype(bf16)
        row = side * 15 * SLOTS // 4
        out_ref[row : row + SLOTS // 4] = slots.reshape(SLOTS // 4, 4, D)
    copy.wait()


def layer_norm(hidden):
    center = hidden - jnp.mean(hidden, axis=-1, keepdims=True)
    spread = jnp.mean(center * center, axis=-1, keepdims=True)
    return (center * lax.rsqrt(spread + 1e-05)).astype(bf16)


def attention(a, hidden, qkv_ref, out_ref, three, mixed):
    rows = slice(a * 128, a * 128 + 128)
    normed = layer_norm(hidden[rows])
    yield
    for tile in range(9):
        columns = slice(tile * 256, tile * 256 + 256)
        three[rows, columns] = dot(normed, qkv_ref[:, columns]).astype(bf16)
        yield
    first = lax.broadcasted_iota(jnp.int32, (128, 128), 1) < 64
    none = jnp.zeros((128, 128), bf16)
    ones = jnp.concatenate([jnp.where(first, 1.0, 0.0), jnp.where(first, 0.0, 1.0)], 0).astype(bf16)
    for pair in range(PAIRS):
        columns = slice(pair * 128, pair * 128 + 128)
        query, keys, values = [
            three[rows, D * n + pair * 128 : D * n + pair * 128 + 128] for n in range(3)
        ]
        keys = jnp.concatenate([jnp.where(first, keys, none), jnp.where(first, none, keys)], 0)
        values = values * (1.0 / SHRINK)
        values = jnp.concatenate([jnp.where(first, values, none), jnp.where(first, none, values)], 0)
        weights = jnp.exp(dot_t(query, keys) * 0.125).astype(bf16)
        result = dot(weights, jnp.concatenate([values, ones], 1))
        mixed[rows, columns] = (result[:, :128] * (1.0 / result[:, 128:]) * SHRINK).astype(bf16)
        yield
    for tile in range(3):
        columns = slice(tile * 256, tile * 256 + 256)
        branch = dot(mixed[rows], out_ref[:, columns]).astype(bf16)
        hidden[rows, columns] = hidden[rows, columns] + branch.astype(f32)
        yield


def feed_forward(a, hidden, up_ref, down_ref, out_ref, upper):
    rows = slice(a * 128, a * 128 + 128)
    normed = layer_norm(hidden[rows])
    yield
    for tile in range(FF // 256):
        columns = slice(tile * 256, tile * 256 + 256)
        values = jax.nn.gelu(dot(normed, up_ref[:, columns]), approximate=True)
        upper[rows, columns] = values.astype(bf16)
        yield
    for tile in range(3):
        columns = slice(tile * 256, tile * 256 + 256)
        total = (hidden[rows, columns] + dot(upper[rows], down_ref[:, columns])).astype(bf16)
        for j in range(8):
            start = j * 32 + a * 16
            out_ref[start : start + 16, columns] = total[j * 16 : j * 16 + 16]
        yield


def staggered(chains, lag):
    lead, trail = chains
    for _ in range(lag):
        next(lead, None)
    while True:
        done = [next(lead, "end"), next(trail, "end")]
        if done == ["end", "end"]:
            break


X_LAG = 0
Y_LAG = 0


def x_kernel(slots_ref, sum_ref, qkv_ref, outw_ref, order_ref, out_ref, hidden, three, mixed):
    slots = slots_ref[...].reshape(NXL * SLOTS, D)

    def chain(a):
        rows = slice(a * 128, a * 128 + 128)
        hidden[rows] = dot(sum_ref[rows], slots)
        yield from attention(a, hidden, qkv_ref, outw_ref, three, mixed)

    staggered([chain(0), chain(1)], X_LAG)
    tokens = dot(order_ref[...], hidden[...].astype(bf16)).astype(bf16)
    out_ref[...] = tokens.reshape(128, 2, D)


def y_kernel(
    tokens_ref,
    split_ref,
    qkv_ref,
    outw_ref,
    up_ref,
    down_ref,
    out_ref,
    hidden,
    three,
    mixed,
    upper,
):
    tokens = tokens_ref[...].reshape(TOK, D)

    def chain(a):
        rows = slice(a * 128, a * 128 + 128)
        hidden[rows] = dot(split_ref[rows], tokens)
        yield from attention(a, hidden, qkv_ref, outw_ref, three, mixed)
        yield from feed_forward(a, hidden, up_ref, down_ref, out_ref, upper)

    staggered([chain(0), chain(1)], Y_LAG)


def home_kernel(tokens_ref, order_ref, out_ref):
    out_ref[...] = dot(order_ref[...], tokens_ref[...]).astype(bf16)


def whole(kernel, out_shape, scratch, flops, limit):
    space = pl.BlockSpec(memory_space=pltpu.VMEM)

    def call(*operands):
        size = sum(x.size * x.dtype.itemsize for x in operands)
        return pl.pallas_call(
            kernel,
            out_shape=out_shape,
            in_specs=[space] * len(operands),
            out_specs=[space] * len(out_shape) if isinstance(out_shape, list) else space,
            scratch_shapes=scratch,
            compiler_params=pltpu.CompilerParams(vmem_limit_bytes=limit << 20),
            cost_estimate=pl.CostEstimate(flops=flops, bytes_accessed=size, transcendentals=0),
        )(*operands)

    return call


def like(shape, kind=bf16):
    return jax.ShapeDtypeStruct(shape, kind)


def prepare(fields):
    space = pl.BlockSpec(memory_space=pltpu.VMEM)
    return pl.pallas_call(
        prep_kernel,
        in_specs=[pl.BlockSpec(memory_space=pltpu.HBM)],
        out_specs=[space] * 3,
        out_shape=[
            like((NF, ZS, CX + 2 * PADX, CY), f32),
            like((40, R, 128), f32),
            like((40, R, 128), f32),
        ],
        scratch_shapes=[
            pltpu.VMEM((NF, ZS + 2 * R, CX, CY), f32),
            pltpu.SemaphoreType.DMA((NF,)),
        ],
        compiler_params=pltpu.CompilerParams(vmem_limit_bytes=49 << 20),
    )(fields)


def shards(fields, embed_weight, qkv_weight, out_weight, up_weight, down_weight):
    count = lax.axis_size("gy")
    smooth, upper, lower = prepare(fields)
    upper = lax.ppermute(upper, "gy", [(i, (i + 1) % count) for i in range(count)])
    lower = lax.ppermute(lower, "gy", [((i + 1) % count, i) for i in range(count)])
    slots = like((16 * SLOTS // 4, 4, D))
    inner, base, edge, weight = whole(
        main_kernel,
        [slots, like((2, 24, D), f32), like((20, 24, 128), f32), like((KIN, D))],
        [
            pltpu.VMEM((NF, ZS, 80, CY), f32),
            pltpu.VMEM((ALL_ROWS, KIN), bf16),
            pltpu.VMEM((ALL_ROWS, D), f32),
            pltpu.VMEM((6, HI_ROWS + 80, 128), f32),
            pltpu.VMEM((ALL_ROWS, D), bf16),
        ],
        2 * 6400 * 256 * 256 + 2 * KIN * 256 * D + 2 * ALL_ROWS * KIN * D,
        18,
    )(smooth, embed_weight)
    slots = whole(
        edge_kernel,
        slots,
        [
            pltpu.VMEM((400, 128), f32),
            pltpu.VMEM((224, 128), f32),
            pltpu.VMEM((20, 40, 128), f32),
            pltpu.SemaphoreType.DMA(()),
        ],
        2 * 64 * KIN * D,
        8,
    )(upper, lower, strip_table(), edge, base, weight, inner)
    slots = lax.all_to_all(
        slots.reshape(NXL, SLOTS // 4, 4, D), "gx", split_axis=0, concat_axis=0, tiled=True
    ).reshape(NXL * SLOTS // 4, 4, D)
    attention = [
        pltpu.VMEM((TOK, D), f32),
        pltpu.VMEM((TOK, 3 * D), bf16),
        pltpu.VMEM((TOK, D), bf16),
    ]
    tokens = whole(x_kernel, like((128, 2, D)), attention, 2 * TOK * D * 4 * D, 10)(
        slots, gather_sum(), qkv_weight, out_weight, interleave()
    )
    tokens = lax.all_to_all(
        tokens, ("gx", "gy"), split_axis=0, concat_axis=0, tiled=True
    )
    tokens = whole(
        y_kernel,
        like((TOK, D)),
        attention + [pltpu.VMEM((TOK, FF), bf16)],
        2 * TOK * D * (4 * D + 2 * FF),
        14,
    )(tokens, separate(), qkv_weight, out_weight, up_weight, down_weight)
    tokens = lax.all_to_all(
        tokens.reshape(8, 32, D), "gy", split_axis=0, concat_axis=0, tiled=True
    ).reshape(TOK, D)
    tokens = whole(home_kernel, like((TOK, D)), [], 2 * TOK * TOK * D, 8)(tokens, to_home())
    return tokens.reshape(2, 16, 8, D)


def solution(mesh):
    return jax.shard_map(
        shards,
        mesh=mesh,
        in_specs=(P(None, None, "gx", "gy"), P(), P(), P(), P(), P()),
        out_specs=P(None, "gy", "gx", None),
        check_vma=False,
    )
```
